128 devices in a mesh: dp: 4 (over y), seq: 32 (over z, x, core).
Axes of the slice: x: 4, y: 4, z: 4, core: 2. Of those that a mesh axis runs over, the one named last changes fastest.
Arguments:
- byte_keys: bfloat16 [4, 65536, 1024], P('dp', 'seq')
- byte_values: bfloat16 [4, 65536, 1024], P('dp', 'seq'), may hold values from -6 to 6
- doc_ids: int32 [4, 65536], P('dp', 'seq'), may hold values from 0 to 255, as said below
- queries: bfloat16 [4, 16384, 1024], P('dp', 'seq')
- patch_end: int32 [4, 16384], P('dp', 'seq'), may hold values from 1 to 65536, as said below
- cotangent: bfloat16 [4, 16384, 4096], P('dp', 'seq'), may hold values from -6 to 6
- proj_weight: bfloat16 [4096, 1024], P('seq'), may hold values from -0.1875 to 0.1875
- norm_gain: float32 [4096], replicated, may hold values from 0.25 to 1.75
Outputs:
- d_queries: bfloat16 [4, 16384, 1024], P('dp', 'seq')
- d_keys: bfloat16 [4, 65536, 1024], P('dp', 'seq')
- d_values: bfloat16 [4, 65536, 1024], P('dp', 'seq')
- d_proj: float32 [4096, 1024], P('seq')
- d_gain: float32 [4096], replicated
The draws below stay inside these ranges and needn't reach their ends.
Inputs may be any that keep to these rules, and one draw needn't show every extreme that they name: `patch_end`: within a stream the ends rise strictly, each patch has 1 to 7 bytes, the last end is 65536; for every rank d from 1 to the seq size less 1, patch d * 512 - 1 ends at d * 2048 + e with -256 <= e <= 256, and in every stream e = -256 occurs at some rank and e = 256 at another; some patch has 7 bytes in every stream. `doc_ids`: within a stream the numbers never fall, start at 0, change only at bytes where a patch begins, and rise by one at each change; every stream holds exactly 256 documents.
All inputs are finite; a program needn't handle non-finite values.
Results may differ from the reference program's by a relative error of at most 0.024.
Values may be sent and summed in bfloat16 or wider, within the bound.
No kernel may reach another device: no remote copies, remote signals or barrier semaphores. Data moves between devices by JAX's collectives and lax.ppermute only.
A program may use at most 192 MiB of HBM per device.

```python
import math
import jax
import jax.numpy as jnp
from jax import lax

DG = 4096
HEADS = 8
HD = 128
DA = 1024
BYTE_DEV = 2048
PATCH_DEV = 512
DRIFT = 256
WIN = 128
PG = 64
DOCP = 64
SLAB = 576
STREAMS = 4
BYTES = 65536
PATCHES = 16384


def patch_layout(key):
    seq_count = PATCHES // PATCH_DEV
    half_count = PATCH_DEV // 2
    base_key = jax.random.fold_in(key, 55)
    inner = jax.random.randint(jax.random.fold_in(base_key, 1), (STREAMS, seq_count + 1), -DRIFT, DRIFT)
    interior = jnp.broadcast_to(jnp.arange(seq_count - 1) + 1, (STREAMS, seq_count - 1))
    picked = jax.random.permutation(jax.random.fold_in(base_key, 2), interior, axis=1, independent=True)
    position = jnp.arange(seq_count + 1)[None, :]
    drift_all = jnp.where(position == picked[:, 0:1], -DRIFT, inner)
    drift_all = jnp.where(position == picked[:, 1:2], DRIFT, drift_all)
    drift_all = jnp.where((position == 0) | (position == seq_count), 0, drift_all)
    bounds = position * BYTE_DEV + drift_all
    excess = bounds[:, 1:] - bounds[:, :-1] - 4 * PATCH_DEV
    steps_half = jax.random.randint(jax.random.fold_in(base_key, 3), (STREAMS, seq_count, half_count), -2, 3)
    steps_half = steps_half.at[:, :, 0].set(2)
    step_all = jnp.concatenate([steps_half, -steps_half], axis=2)
    order = jnp.broadcast_to(jnp.arange(PATCH_DEV), (STREAMS, seq_count, PATCH_DEV))
    order = jax.random.permutation(jax.random.fold_in(base_key, 4), order, axis=2, independent=True)
    placed = jnp.take_along_axis(step_all, order, axis=2)
    adjust = jnp.where(order < jnp.abs(excess)[..., None], jnp.sign(excess)[..., None], 0)
    lengths = 4 + placed + adjust
    patch_ends = (bounds[:, :-1, None] + jnp.cumsum(lengths, axis=2)).reshape(STREAMS, PATCHES)
    doc_count = PATCHES // DOCP
    ranks = jnp.broadcast_to(jnp.arange(PATCHES - 1), (STREAMS, PATCHES - 1))
    ranks = jax.random.permutation(jax.random.fold_in(base_key, 5), ranks, axis=1, independent=True)
    closing = jnp.concatenate([ranks < doc_count - 1, jnp.zeros((STREAMS, 1), bool)], axis=1)
    starts = jnp.zeros((STREAMS, BYTES + 1), jnp.int32)
    rows_index = jnp.broadcast_to(jnp.arange(STREAMS)[:, None], (STREAMS, PATCHES))
    starts = starts.at[rows_index, patch_ends].add(closing.astype(jnp.int32))
    documents = jnp.cumsum(starts[:, :BYTES], axis=1)
    return (patch_ends.astype(jnp.int32), documents.astype(jnp.int32))


def draw_patch_end(key, part):
    patch_ends, documents = patch_layout(key)
    return patch_ends


def draw_doc_ids(key, part):
    patch_ends, documents = patch_layout(key)
    return documents


def draw_byte_keys(key, part):
    key = jax.random.fold_in(key, 1)
    result = jax.random.normal(key, (STREAMS, BYTES, DA), jnp.float32)
    return result.astype(jnp.bfloat16)


def draw_queries(key, part):
    key = jax.random.fold_in(key, 2)
    result = jax.random.normal(key, (STREAMS, PATCHES, DA), jnp.float32)
    return result.astype(jnp.bfloat16)


def strengthened(values, own_key, source, target, shards_of, factor):
    owner, partner = [(jnp.arange(values.shape[axis_at]) // (values.shape[axis_at] // shards_of)).reshape([-1 if axis == axis_at else 1 for axis in range(values.ndim)]) for axis_at in (source, target)]
    chosen = jax.random.permutation(own_key, shards_of)[partner]
    strong = (owner == chosen) | (owner == (partner + shards_of // 2) % shards_of)
    return jnp.where(strong, factor * values, values)


def steps_of(stream_key, extent, shards, low, high):
    def one(dim, shards_of):
        heights = jax.random.uniform(jax.random.fold_in(jax.random.fold_in(stream_key, 6), dim), (shards_of,), jnp.float32, low / len(shards), high / len(shards))
        return jnp.repeat(jnp.exp(heights), extent[dim] // shards_of).reshape((-1,) + (1,) * (len(extent) - dim - 1))

    factor_of = one(*shards[0])
    for cut in shards[1:]:
        factor_of = factor_of * one(*cut)
    return factor_of


def bell_draw(rng, extent, deviation, bound, split=(), held_as=jnp.bfloat16):
    values = deviation * jax.random.normal(rng, extent, jnp.float32)
    if split:
        values = values * steps_of(rng, extent, split, -0.22, 0.18)
    return jnp.clip(values, -bound, bound).astype(held_as)


def noise_with(rng, extent, deviation, reach, pieces, heavy, kind=jnp.bfloat16):
    values = deviation * jax.random.normal(rng, extent, jnp.float32)
    if pieces:
        values = values * steps_of(rng, extent, pieces, -0.22, 0.18)
    return jnp.clip(strengthened(values, jax.random.fold_in(rng, 3), *heavy), -reach, reach).astype(kind)


def setup_inputs(seed: int = 0) -> dict:
    streams_of = jax.random.split(jax.random.key(seed), 9)
    return {
        "byte_keys": draw_byte_keys(jax.random.fold_in(streams_of[8], 71), 0),
        "byte_values": bell_draw(streams_of[1], (STREAMS, BYTES, DA), 1.0, 6.0, ((0, 4), (1, 32))),
        "doc_ids": draw_doc_ids(jax.random.fold_in(streams_of[8], 71), 0),
        "queries": draw_queries(jax.random.fold_in(streams_of[8], 71), 0),
        "patch_end": draw_patch_end(jax.random.fold_in(streams_of[8], 71), 0),
        "cotangent": noise_with(streams_of[5], (STREAMS, PATCHES, DG), 1.0, 6.0, ((0, 4), (1, 32)), (1, 2, 32, 2.75)),
        "proj_weight": bell_draw(streams_of[6], (DG, DA), DA ** -0.5, 0.1875, ((0, 32),)),
        "norm_gain": jnp.clip(1.0 + 0.15 * jax.random.normal(streams_of[7], (DG,), jnp.float32), 0.25, 1.75),
    }


masked_score = -1e+30
epsilon = 1e-05

def block_probs(query_group, key_slab, visible):
    score_scale = 1.0 / math.sqrt(HD)
    scores = jnp.einsum('phd,jhd->hpj', query_group.astype(jnp.float32), key_slab.astype(jnp.float32)) * score_scale
    scores = jnp.where(visible[None], scores, masked_score)
    top_score = lax.optimization_barrier(jnp.max(scores, axis=2, keepdims=True))
    expo = jnp.exp(scores - top_score)
    return expo / lax.optimization_barrier(jnp.sum(expo, axis=2, keepdims=True))

def reference(byte_keys, byte_values, doc_ids, queries, patch_end, cotangent, proj_weight, norm_gain):
    score_scale = 1.0 / math.sqrt(HD)
    d_proj = jnp.zeros((DG, DA), jnp.float32)
    d_gain = jnp.zeros((DG,), jnp.float32)
    out_queries = []
    out_keys = []
    out_values = []
    groups = PATCHES // PG
    for stream in range(STREAMS):
        byte_pair = jnp.concatenate([byte_keys[stream], byte_values[stream]], axis=1)
        pair_pad = jnp.pad(byte_pair, ((WIN, SLAB), (0, 0)))
        doc_pad = jnp.pad(doc_ids[stream], (WIN, SLAB), constant_values=-1)
        patch_ends = patch_end[stream].astype(jnp.int32)
        last_doc = doc_ids[stream][patch_ends - 1]
        group_ends = patch_ends.reshape(groups, PG)
        group_docs = last_doc.reshape(groups, PG)
        group_queries = queries[stream].reshape(groups, PG, HEADS, HD)

        def setup(index):
            ends_here = group_ends[index]
            offset = ends_here[0].astype(jnp.int32)
            slab = lax.dynamic_slice_in_dim(pair_pad, offset, SLAB, 0)
            slab_doc = lax.dynamic_slice_in_dim(doc_pad, offset, SLAB, 0)
            position = offset - WIN + jnp.arange(SLAB).astype(jnp.int32)
            visible = (position[None, :] >= ends_here[:, None] - WIN) & (position[None, :] < ends_here[:, None])
            visible = visible & (position[None, :] >= 0) & (position[None, :] < BYTES)
            visible = visible & (slab_doc[None, :] == group_docs[index][:, None])
            key_slab = slab[:, :DA].reshape(SLAB, HEADS, HD)
            value_slab = slab[:, DA:].reshape(SLAB, HEADS, HD)
            return (offset, visible, key_slab, value_slab, group_queries[index])

        def forward_group(index):
            offset, visible, key_slab, value_slab, query_group = setup(index)
            probs = block_probs(query_group, key_slab, visible).astype(jnp.bfloat16)
            attended = jnp.einsum('hpj,jhd->phd', probs.astype(jnp.float32), value_slab.astype(jnp.float32))
            return attended.reshape(PG, DA).astype(jnp.bfloat16)
        attended_all = lax.map(forward_group, jnp.arange(groups).astype(jnp.int32)).reshape(PATCHES, DA)
        latent = lax.dot_general(attended_all, proj_weight, (((1,), (1,)), ((), ())), preferred_element_type=jnp.float32)
        upstream = cotangent[stream].astype(jnp.float32) * norm_gain
        inverse = lax.rsqrt(lax.optimization_barrier(jnp.mean(latent * latent, axis=1, keepdims=True)) + epsilon)
        d_gain = d_gain + lax.optimization_barrier(jnp.sum(cotangent[stream].astype(jnp.float32) * latent * inverse, axis=0))
        mixed_dot = lax.optimization_barrier(jnp.mean(upstream * latent, axis=1, keepdims=True))
        d_latent = (inverse * upstream - latent * inverse * inverse * inverse * mixed_dot).astype(jnp.bfloat16)
        d_proj = d_proj + lax.dot_general(d_latent, attended_all, (((0,), (0,)), ((), ())), preferred_element_type=jnp.float32)
        d_attended = jnp.dot(d_latent, proj_weight, preferred_element_type=jnp.float32).astype(jnp.bfloat16)

        def backward_group(grad_bytes, index):
            offset, visible, key_slab, value_slab, query_group = setup(index)
            probs = block_probs(query_group, key_slab, visible)
            d_out = lax.dynamic_slice_in_dim(d_attended, index * PG, PG, 0).reshape(PG, HEADS, HD).astype(jnp.float32)
            out_group = lax.dynamic_slice_in_dim(attended_all, index * PG, PG, 0).reshape(PG, HEADS, HD).astype(jnp.float32)
            row_dot = jnp.transpose(lax.optimization_barrier(jnp.sum(d_out * out_group, axis=2)))[:, :, None]
            d_probs = jnp.einsum('phd,jhd->hpj', d_out, value_slab.astype(jnp.float32))
            d_scores = (probs * (d_probs - row_dot) * score_scale).astype(jnp.bfloat16).astype(jnp.float32)
            d_query = jnp.einsum('hpj,jhd->phd', d_scores, key_slab.astype(jnp.float32)).reshape(PG, DA).astype(jnp.bfloat16)
            d_key = jnp.einsum('hpj,phd->jhd', d_scores, query_group.astype(jnp.float32)).reshape(SLAB, DA)
            rounded = probs.astype(jnp.bfloat16).astype(jnp.float32)
            d_value = jnp.einsum('hpj,phd->jhd', rounded, d_out).reshape(SLAB, DA)
            current = lax.dynamic_slice_in_dim(grad_bytes, offset, SLAB, 0)
            grad_bytes = lax.dynamic_update_slice_in_dim(grad_bytes, current + jnp.concatenate([d_key, d_value], axis=1), offset, 0)
            return (grad_bytes, d_query)
        start_grad = jnp.zeros((BYTES + WIN + SLAB, 2 * DA), jnp.float32)
        grad_bytes, d_query_groups = lax.scan(backward_group, start_grad, jnp.arange(groups).astype(jnp.int32))
        out_queries.append(d_query_groups.reshape(PATCHES, DA))
        out_keys.append(grad_bytes[WIN:WIN + BYTES, :DA].astype(jnp.bfloat16))
        out_values.append(grad_bytes[WIN:WIN + BYTES, DA:].astype(jnp.bfloat16))
    return (jnp.stack(out_queries), jnp.stack(out_keys), jnp.stack(out_values), d_proj, d_gain)
```

```python
import math

import jax
import jax.numpy as jnp
from jax import lax
from jax.experimental import pallas as pl
from jax.experimental.pallas import tpu as pltpu
from jax.sharding import PartitionSpec as P

HEADS = 8
HD = 128
WIN = 128
LOW = 384
HIGH = 256
PG = 32
SLAB = 384
RING = 4
LANES = 128

masked_score = -1e30
epsilon = 1e-05
score_scale = 1.0 / math.sqrt(HD)
bf16, f32 = jnp.bfloat16, jnp.float32
MIB = 1024 * 1024
VMEM_GRANT = 60 * MIB


def dot(a, b):
    return jnp.dot(a, b, preferred_element_type=f32)


def dot_rows(a, b):
    return lax.dot_general(a, b, (((1,), (1,)), ((), ())), preferred_element_type=f32)


def dot_columns(a, b):
    return lax.dot_general(a, b, (((0,), (0,)), ((), ())), preferred_element_type=f32)


def of_head(head):
    return slice(head * HD, (head + 1) * HD)


def fetch_bytes(low_ref, high_ref, keys_ref, values_ref, key_ext, value_ext, sems):
    own = keys_ref.shape[0]
    copies = []
    for which, (own_ref, ext) in enumerate(((keys_ref, key_ext), (values_ref, value_ext))):
        parts = (
            (low_ref.at[pl.ds(which * LOW, LOW)], pl.ds(0, LOW)),
            (own_ref, pl.ds(LOW, own)),
            (high_ref.at[pl.ds(which * HIGH, HIGH)], pl.ds(LOW + own, HIGH)),
        )
        for part, (source, rows) in enumerate(parts):
            copies.append(
                pltpu.make_async_copy(source, ext.at[rows], sems.at[which * 3 + part])
            )
    return copies


def visible_bias(offset, span_ref, rows):
    position = offset + lax.broadcasted_iota(jnp.int32, (PG, SLAB), 1)
    visible = (position >= span_ref[rows, 0:1]) & (position < span_ref[rows, 1:2])
    return jnp.where(visible, 0.0, masked_score)


def forward_kernel(
    offset_ref, span_ref, low_ref, high_ref, keys_ref, values_ref, query_ref,
    attended_ref, level_ref, key_ext, value_ext, sems,
):
    step = pl.program_id(0)

    @pl.when(step == 0)
    def _():
        copies = fetch_bytes(low_ref, high_ref, keys_ref, values_ref, key_ext, value_ext, sems)
        for copy in copies:
            copy.start()
        for copy in copies:
            copy.wait()

    groups = query_ref.shape[0] // PG

    def one_group(group, carry):
        rows = pl.ds(pl.multiple_of(group * PG, PG), PG)
        offset = pl.multiple_of(offset_ref[step * groups + group], 16)
        slab = pl.ds(offset, SLAB)
        bias = visible_bias(offset, span_ref, rows)
        heads = [of_head(head) for head in range(HEADS)]
        scores = [dot_rows(query_ref[rows, h], key_ext[slab, h]) for h in heads]
        scores = [x * score_scale + bias for x in scores]
        top = [jnp.max(x, axis=1, keepdims=True) for x in scores]
        expo = [jnp.exp(x - y) for x, y in zip(scores, top)]
        total = [jnp.sum(x, axis=1, keepdims=True) for x in expo]
        probs = [(x * (1.0 / y)).astype(bf16) for x, y in zip(expo, total)]
        attended = [dot(x, value_ext[slab, h]) for x, h in zip(probs, heads)]
        for h, x, y, z in zip(heads, attended, top, total):
            attended_ref[rows, h] = x.astype(bf16)
            level_ref[rows, h] = jnp.broadcast_to(y + jnp.log(z), (PG, HD))
        return carry

    lax.fori_loop(0, groups, one_group, 0)


def backward_kernel(
    offset_ref, span_ref, low_ref, high_ref, keys_ref, values_ref, query_ref,
    attended_ref, level_ref, d_attended_ref, after_ref,
    d_query_ref, d_key_ref, d_value_ref, d_low_ref, d_high_ref,
    key_ext, value_ext, sems, d_key, d_value,
):
    step = pl.program_id(0)
    own = keys_ref.shape[0]

    @pl.when(step == 0)
    def _():
        copies = fetch_bytes(low_ref, high_ref, keys_ref, values_ref, key_ext, value_ext, sems)
        for copy in copies:
            copy.start()
        d_key[...] = jnp.zeros_like(d_key)
        d_value[...] = jnp.zeros_like(d_value)
        for copy in copies:
            copy.wait()

    groups = query_ref.shape[0] // PG

    def one_group(group, carry):
        rows = pl.ds(pl.multiple_of(group * PG, PG), PG)
        offset = pl.multiple_of(offset_ref[step * groups + group], 16)
        slab = pl.ds(offset, SLAB)
        bias = visible_bias(offset, span_ref, rows)
        heads = [of_head(head) for head in range(HEADS)]
        scores = [dot_rows(query_ref[rows, h], key_ext[slab, h]) for h in heads]
        d_probs = [dot_rows(d_attended_ref[rows, h], value_ext[slab, h]) for h in heads]
        row_dot = [
            jnp.sum(
                d_attended_ref[rows, h].astype(f32) * attended_ref[rows, h].astype(f32),
                axis=1, keepdims=True,
            )
            for h in heads
        ]
        level = [jnp.concatenate([level_ref[rows, h]] * (SLAB // HD), axis=1) for h in heads]
        probs = [jnp.exp(x * score_scale + bias - y) for x, y in zip(scores, level)]
        d_scores = [
            (x * (y - z) * score_scale).astype(bf16) for x, y, z in zip(probs, d_probs, row_dot)
        ]
        probs = [x.astype(bf16) for x in probs]
        d_query = [dot(x, key_ext[slab, h]) for x, h in zip(d_scores, heads)]
        key_part = [dot_columns(x, query_ref[rows, h]) for x, h in zip(d_scores, heads)]
        value_part = [dot_columns(x, d_attended_ref[rows, h]) for x, h in zip(probs, heads)]
        for h, x, y, z in zip(heads, d_query, key_part, value_part):
            d_query_ref[rows, h] = x.astype(bf16)
            d_key[slab, h] += y
            d_value[slab, h] += z
        return carry

    lax.fori_loop(0, groups, one_group, 0)

    @pl.when(step == pl.num_programs(0) - 1)
    def _():
        for which, (total, own_ref) in enumerate(((d_key, d_key_ref), (d_value, d_value_ref))):
            d_low_ref[which * LOW : (which + 1) * LOW, :] = total[:LOW, :].astype(bf16)
            own_ref[...] = total[LOW : LOW + own, :].astype(bf16)
            d_high_ref[which * HIGH : (which + 1) * HIGH, :] = total[LOW + own :, :].astype(bf16)


def forward_call(inputs):
    own, width = inputs[4].shape
    patches = inputs[6].shape[0]
    steps = 4
    ext_rows = LOW + own + HIGH

    def per_step(columns):
        return pl.BlockSpec((patches // steps, columns), lambda step, offset: (step, 0))

    return pl.pallas_call(
        forward_kernel,
        out_shape=[
            jax.ShapeDtypeStruct((patches, width), bf16),
            jax.ShapeDtypeStruct((patches, width), f32),
        ],
        grid_spec=pltpu.PrefetchScalarGridSpec(
            num_scalar_prefetch=1,
            grid=(steps,),
            in_specs=[per_step(2)] + [pl.BlockSpec(memory_space=pl.ANY)] * 4 + [per_step(width)],
            out_specs=[per_step(width)] * 2,
            scratch_shapes=[pltpu.VMEM((ext_rows, width), bf16)] * 2
            + [pltpu.SemaphoreType.DMA((6,))],
        ),
        compiler_params=pltpu.CompilerParams(vmem_limit_bytes=VMEM_GRANT),
        cost_estimate=pl.CostEstimate(
            flops=4 * HEADS * patches * SLAB * HD,
            bytes_accessed=20 * MIB,
            transcendentals=HEADS * patches * SLAB,
        ),
        name="attention_forward",
    )(*inputs)


def backward_call(inputs, after):
    own, width = inputs[4].shape
    patches = inputs[6].shape[0]
    steps = 4
    ext_rows = LOW + own + HIGH
    step_block = pl.BlockSpec((patches // steps, width), lambda step, offset: (step, 0))
    anywhere = pl.BlockSpec(memory_space=pl.ANY)

    def kept(rows):
        return pl.BlockSpec(
            (rows, width), lambda step, offset: (0, 0), pipeline_mode=pl.Buffered(1)
        )

    rows = (own, own, 2 * LOW, 2 * HIGH)
    return pl.pallas_call(
        backward_kernel,
        out_shape=[jax.ShapeDtypeStruct((count, width), bf16) for count in (patches,) + rows],
        grid_spec=pltpu.PrefetchScalarGridSpec(
            num_scalar_prefetch=1,
            grid=(steps,),
            in_specs=[pl.BlockSpec((patches // steps, 2), lambda step, offset: (step, 0))]
            + [anywhere] * 4
            + [step_block] * 4
            + [anywhere],
            out_specs=[step_block] + [kept(count) for count in rows],
            scratch_shapes=[pltpu.VMEM((ext_rows, width), bf16)] * 2
            + [pltpu.SemaphoreType.DMA((6,))]
            + [pltpu.VMEM((ext_rows, width), f32)] * 2,
        ),
        compiler_params=pltpu.CompilerParams(vmem_limit_bytes=VMEM_GRANT),
        cost_estimate=pl.CostEstimate(
            flops=14 * HEADS * patches * SLAB * HD,
            bytes_accessed=40 * MIB,
            transcendentals=HEADS * patches * SLAB,
        ),
        name="attention_backward",
    )(*inputs, after)


def chip_block(place_ref, chunk):
    side, first, second = chunk // 16, chunk // 4 % 4, chunk % 4
    core = (place_ref[2] + side) % 2
    z = (place_ref[0] - jnp.where(core == 0, first, second) + RING) % RING
    x = (place_ref[1] - jnp.where(core == 0, second, first) + RING) % RING
    return (z * RING + x) * 2 + core


def fetch_weights(place_ref, weights_ref, weight, sems):
    copies = []
    for chunk in range(32):
        start = pl.multiple_of(chip_block(place_ref, chunk) * LANES, LANES)
        copies.append(
            pltpu.make_async_copy(
                weights_ref.at[pl.ds(start, LANES)],
                weight.at[pl.ds(chunk * LANES, LANES)],
                sems.at[chunk],
            )
        )
    return [copies[start : start + 4] for start in range(0, 32, 4)]


def latent_kernel(
    place_ref, attended_ref, norm_ref, cotangent_ref, weights_ref,
    mine_ref, other_ref, gain_ref, weight, cotangent, latent, square, mixed, sems,
):
    pieces = fetch_weights(place_ref, weights_ref, weight, sems)
    cotangent_copy = pltpu.make_async_copy(cotangent_ref, cotangent, sems.at[32])
    for slab, copies in enumerate(pieces):
        for copy in copies:
            copy.start()
        if slab == 0:
            cotangent_copy.start()
    square[...] = jnp.zeros_like(square)
    mixed[...] = jnp.zeros_like(mixed)

    def columns_of(chunk):
        return pl.ds(pl.multiple_of(chip_block(place_ref, chunk) * LANES, LANES), LANES)

    for slab in range(8):
        for copy in pieces[slab]:
            copy.wait()
        for half in range(2):
            start = slab * 512 + half * 256
            block = dot_rows(attended_ref[...], weight[start : start + 256, :])
            if slab == 0 and half == 0:
                cotangent_copy.wait()
            for side in range(2):
                chunk = slab * 4 + half * 2 + side
                columns = columns_of(chunk)
                here = block[:, side * LANES : (side + 1) * LANES]
                latent[chunk] = here
                square[...] += here * here
                mixed[...] += here * (cotangent[:, columns].astype(f32) * norm_ref[:, columns])

    count = cotangent.shape[1]
    inverse = lax.rsqrt(jnp.sum(square[...], axis=1, keepdims=True) / count + epsilon)
    back = inverse * inverse * inverse * (jnp.sum(mixed[...], axis=1, keepdims=True) / count)
    square[...] = jnp.broadcast_to(inverse, square.shape)
    mixed[...] = jnp.broadcast_to(back, mixed.shape)

    def finish(chunk, out_ref):
        columns = columns_of(chunk)
        here = latent[chunk]
        arriving = cotangent[:, columns].astype(f32)
        scaled = arriving * square[...]
        gain = jnp.sum(scaled * here, axis=0, keepdims=True)
        spot = pl.ds(pl.multiple_of(chip_block(place_ref, chunk) * 8, 8), 8)
        gain_ref[spot, :] = jnp.broadcast_to(gain, (8, LANES))
        d_latent = scaled * norm_ref[:, columns] - here * mixed[...]
        place = pl.ds(pl.multiple_of(chunk % 16 * LANES, LANES), LANES)
        out_ref[:, place] = d_latent.astype(bf16)

    lax.fori_loop(0, 16, lambda chunk, carry: (finish(chunk, mine_ref), carry)[1], 0)
    lax.fori_loop(16, 32, lambda chunk, carry: (finish(chunk, other_ref), carry)[1], 0)


def latent_call(place, attended, norm_gain, cotangent, weights):
    patches, count = cotangent.shape
    return pl.pallas_call(
        latent_kernel,
        out_shape=[
            jax.ShapeDtypeStruct((patches, count // 2), bf16),
            jax.ShapeDtypeStruct((patches, count // 2), bf16),
            jax.ShapeDtypeStruct((count // LANES * 8, LANES), f32),
        ],
        in_specs=[pl.BlockSpec(memory_space=pltpu.SMEM)]
        + [pl.BlockSpec(memory_space=pltpu.VMEM)] * 2
        + [pl.BlockSpec(memory_space=pl.ANY)] * 2,
        out_specs=[pl.BlockSpec(memory_space=pltpu.VMEM)] * 3,
        scratch_shapes=[
            pltpu.VMEM(weights.shape, bf16),
            pltpu.VMEM((patches, count), bf16),
            pltpu.VMEM((32, patches, LANES), f32),
            pltpu.VMEM((patches, LANES), f32),
            pltpu.VMEM((patches, LANES), f32),
            pltpu.SemaphoreType.DMA((33,)),
        ],
        compiler_params=pltpu.CompilerParams(vmem_limit_bytes=VMEM_GRANT),
        cost_estimate=pl.CostEstimate(
            flops=2 * patches * count * 1024, bytes_accessed=18 * MIB, transcendentals=patches
        ),
        name="latent",
    )(place, attended, norm_gain, cotangent, weights)


def d_attended_kernel(place_ref, mine_ref, other_ref, weights_ref, out_ref, weight, total, sems):
    pieces = fetch_weights(place_ref, weights_ref, weight, sems)
    for copies in pieces:
        for copy in copies:
            copy.start()
    for slab in range(8):
        source = mine_ref if slab < 4 else other_ref
        d_latent = source[:, slab % 4 * 512 : slab % 4 * 512 + 512]
        for copy in pieces[slab]:
            copy.wait()
        part = dot(d_latent, weight[slab * 512 : slab * 512 + 512, :])
        if slab == 0:
            total[...] = part
        elif slab < 7:
            total[...] += part
        else:
            out_ref[...] = (total[...] + part).astype(bf16)


def d_attended_call(place, mine, other, weights):
    patches, width = mine.shape[0], weights.shape[1]
    return pl.pallas_call(
        d_attended_kernel,
        out_shape=jax.ShapeDtypeStruct((patches, width), bf16),
        in_specs=[pl.BlockSpec(memory_space=pltpu.SMEM)]
        + [pl.BlockSpec(memory_space=pltpu.VMEM)] * 2
        + [pl.BlockSpec(memory_space=pl.ANY)],
        out_specs=pl.BlockSpec(memory_space=pltpu.VMEM),
        scratch_shapes=[
            pltpu.VMEM(weights.shape, bf16),
            pltpu.VMEM((patches, width), f32),
            pltpu.SemaphoreType.DMA((32,)),
        ],
        compiler_params=pltpu.CompilerParams(vmem_limit_bytes=VMEM_GRANT),
        cost_estimate=pl.CostEstimate(
            flops=4 * patches * mine.shape[1] * width, bytes_accessed=14 * MIB, transcendentals=0
        ),
        name="d_attended",
    )(place, mine, other, weights)


def d_proj_kernel(
    mine_ref, peer_ref, attended_ref, peer_attended_ref, gain_ref, after_ref, *refs
):
    outs, (turned, peer_turned) = refs[:4], refs[4:]
    turned[...] = attended_ref[...].T
    peer_turned[...] = peer_attended_ref[...].T
    width = turned.shape[0]
    for k in range(RING):
        distance = (RING - k) % RING
        columns = slice(distance * 512, distance * 512 + 512)
        part = dot(turned[...], mine_ref[:, columns])
        part += dot(peer_turned[...], peer_ref[:, columns])
        outs[k][:width, :] = part.astype(bf16)
        outs[k][width:, :] = gain_ref[...]


def d_proj_call(mine, peer, attended, peer_attended, gain, after):
    patches, width = attended.shape
    return pl.pallas_call(
        d_proj_kernel,
        out_shape=[jax.ShapeDtypeStruct((width + 16, 512), bf16)] * 4,
        in_specs=[pl.BlockSpec(memory_space=pltpu.VMEM)] * 5
        + [pl.BlockSpec(memory_space=pl.ANY)],
        out_specs=[pl.BlockSpec(memory_space=pltpu.VMEM)] * 4,
        scratch_shapes=[pltpu.VMEM((width, patches), bf16)] * 2,
        compiler_params=pltpu.CompilerParams(vmem_limit_bytes=VMEM_GRANT),
        cost_estimate=pl.CostEstimate(
            flops=4 * patches * mine.shape[1] * width, bytes_accessed=12 * MIB, transcendentals=0
        ),
        name="d_proj",
    )(mine, peer, attended, peer_attended, gain, after)


def rim_kernel(
    key_in, value_in, below_ref, above_ref, key_out, value_out, key_rim, value_rim, sems
):
    own = key_in.shape[0]
    places = ((pl.ds(0, HIGH), pl.ds(0, HIGH)), (pl.ds(own - LOW, LOW), pl.ds(HIGH, LOW)))

    def copies(outward):
        found = []
        for which, (source, out, rim) in enumerate(
            ((key_in, key_out, key_rim), (value_in, value_out, value_rim))
        ):
            for side, (far, near) in enumerate(places):
                sem = sems.at[4 * outward + 2 * which + side]
                if outward:
                    found.append(pltpu.make_async_copy(rim.at[near], out.at[far], sem))
                else:
                    found.append(pltpu.make_async_copy(source.at[far], rim.at[near], sem))
        return found

    inward, outward = copies(0), copies(1)
    for copy in inward:
        copy.start()
    for which, rim in enumerate((key_rim, value_rim)):
        inward[2 * which].wait()
        below = below_ref[which * HIGH : (which + 1) * HIGH, :].astype(f32)
        rim[:HIGH, :] = (rim[:HIGH, :].astype(f32) + below).astype(bf16)
        outward[2 * which].start()
        inward[2 * which + 1].wait()
        above = above_ref[which * LOW : (which + 1) * LOW, :].astype(f32)
        rim[HIGH:, :] = (rim[HIGH:, :].astype(f32) + above).astype(bf16)
        outward[2 * which + 1].start()
    for copy in outward:
        copy.wait()


def rim_call(d_key, d_value, from_below, from_above):
    width = from_below.shape[1]
    anywhere = pl.BlockSpec(memory_space=pl.ANY)
    vmem = pl.BlockSpec(memory_space=pltpu.VMEM)
    return pl.pallas_call(
        rim_kernel,
        out_shape=[jax.ShapeDtypeStruct(d_key.shape, bf16)] * 2,
        in_specs=[anywhere, anywhere, vmem, vmem],
        out_specs=[anywhere, anywhere],
        scratch_shapes=[pltpu.VMEM((HIGH + LOW, width), bf16)] * 2
        + [pltpu.SemaphoreType.DMA((8,))],
        input_output_aliases={0: 0, 1: 1},
        compiler_params=pltpu.CompilerParams(vmem_limit_bytes=VMEM_GRANT),
        name="rims",
    )(d_key, d_value, from_below, from_above)


def along(which, distance):
    pairs = []
    for z in range(RING):
        for x in range(RING):
            for core in range(2):
                on_z = (which == "first") == (core == 0)
                to_z = (z + distance) % RING if on_z else z
                to_x = x if on_z else (x + distance) % RING
                pairs.append(((z * RING + x) * 2 + core, (to_z * RING + to_x) * 2 + core))
    return pairs


def to_peer(value):
    return lax.ppermute(value, "seq", [(i, i ^ 1) for i in range(lax.axis_size("seq"))])


def ring(values, which):
    return [values[0]] + [
        lax.ppermute(values[k], "seq", along(which, k)) for k in range(1, RING)
    ]


def total_of(parts):
    parts = [part.astype(f32) for part in parts]
    return (parts[0] + parts[2]) + (parts[1] + parts[3])


def halves(value):
    upper = value.astype(bf16)
    lower = (value - upper.astype(f32)).astype(bf16)
    return jnp.concatenate([upper, lower])


def joined(value):
    rows = value.shape[0] // 2
    return value[:rows] + value[rows:]


def first_sum_kernel(*refs):
    parts, outs = refs[:4], refs[4:]
    width = parts[0].shape[0] - 16
    gain = joined(total_of([ref[width:, :] for ref in parts]))
    gain = halves(
        jnp.concatenate([gain[:, k * LANES : (k + 1) * LANES] for k in range(RING)])
    )
    for k in range(RING):
        start = (RING - k) % RING * LANES
        columns = slice(start, start + LANES)
        outs[k][:width, :] = total_of([ref[:width, columns] for ref in parts]).astype(bf16)
        outs[k][width:, :] = gain


def first_sum(parts):
    width = parts[0].shape[0] - 16
    vmem = pl.BlockSpec(memory_space=pltpu.VMEM)
    return pl.pallas_call(
        first_sum_kernel,
        out_shape=[jax.ShapeDtypeStruct((width + 64, LANES), bf16)] * RING,
        in_specs=[vmem] * 4,
        out_specs=[vmem] * 4,
        compiler_params=pltpu.CompilerParams(vmem_limit_bytes=VMEM_GRANT),
        name="first_sum",
    )(*parts)


def second_sum_kernel(place_ref, *refs):
    parts, outs, total = refs[:4], refs[4:8], refs[8]
    width = total.shape[0]
    quarter = width // RING
    total[...] = total_of([ref[:width, :] for ref in parts])
    gain = halves(joined(total_of([ref[width:, :] for ref in parts])))
    for k in range(RING):
        start = pl.multiple_of((place_ref[3] + k) % RING * quarter, quarter)
        outs[k][:quarter, :] = total[pl.ds(start, quarter), :].astype(bf16)
        outs[k][quarter:, :] = gain


def second_sum(place, parts):
    width = parts[0].shape[0] - 64
    vmem = pl.BlockSpec(memory_space=pltpu.VMEM)
    return pl.pallas_call(
        second_sum_kernel,
        out_shape=[jax.ShapeDtypeStruct((width // RING + 64, LANES), bf16)] * RING,
        in_specs=[pl.BlockSpec(memory_space=pltpu.SMEM)]
        + [vmem] * 4,
        out_specs=[vmem] * RING,
        scratch_shapes=[pltpu.VMEM((width, LANES), f32)],
        name="second_sum",
    )(place, *parts)


def stream_sum_kernel(*refs):
    parts, part_ref, gain_ref = refs[:4], refs[4], refs[5]
    quarter = part_ref.shape[0]
    total = total_of([ref[...] for ref in parts])
    part_ref[...] = total[:quarter, :].astype(bf16)
    gain_ref[...] = joined(total[quarter:, :])


def stream_sum(parts):
    quarter = parts[0].shape[0] - 64
    vmem = pl.BlockSpec(memory_space=pltpu.VMEM)
    return pl.pallas_call(
        stream_sum_kernel,
        out_shape=[
            jax.ShapeDtypeStruct((quarter, LANES), bf16),
            jax.ShapeDtypeStruct((32, LANES), f32),
        ],
        in_specs=[vmem] * 4,
        out_specs=[vmem] * 2,
        name="stream_sum",
    )(*parts)


def finish_kernel(place_ref, *refs):
    parts, out_ref = refs[:4], refs[4]
    quarter = parts[0].shape[0]
    for k in range(RING):
        start = pl.multiple_of((place_ref[3] - k + RING) % RING * quarter, quarter)
        out_ref[:, pl.ds(start, quarter)] = parts[k][...].astype(f32).T


def finish_call(place, parts):
    quarter = parts[0].shape[0]
    vmem = pl.BlockSpec(memory_space=pltpu.VMEM)
    return pl.pallas_call(
        finish_kernel,
        out_shape=jax.ShapeDtypeStruct((LANES, RING * quarter), f32),
        in_specs=[pl.BlockSpec(memory_space=pltpu.SMEM)] + [vmem] * 4,
        out_specs=vmem,
        name="d_proj_rows",
    )(place, *parts)


def stream_ring(values):
    count = lax.axis_size("dp")
    return [values[0]] + [
        lax.ppermute(values[k], "dp", [(i, (i + k) % count) for i in range(count)])
        for k in range(1, RING)
    ]


def on_device(
    byte_keys, byte_values, doc_ids, queries, patch_end, cotangent, proj_weight, norm_gain
):
    own, width = byte_keys.shape[1:]
    patches = queries.shape[1]
    seq_count = lax.axis_size("seq")
    seq_rank = lax.axis_index("seq")
    upward = [(i, i + 1) for i in range(seq_count - 1)]
    downward = [(i + 1, i) for i in range(seq_count - 1)]
    keys, values, docs = byte_keys[0], byte_values[0], doc_ids[0]
    place = jnp.stack([seq_rank // (2 * RING), seq_rank // 2 % RING, seq_rank % 2, lax.axis_index("dp")])

    low_docs = lax.ppermute(docs[own - LOW :], "seq", upward)
    high_docs = lax.ppermute(docs[:HIGH], "seq", downward)
    low = jnp.concatenate([keys[own - LOW :], values[own - LOW :]])
    high = jnp.concatenate([keys[:HIGH], values[:HIGH]])
    low, high = lax.ppermute(low, "seq", upward), lax.ppermute(high, "seq", downward)
    weights = lax.all_gather(proj_weight, "seq", axis=0, tiled=True)

    ext_docs = jnp.concatenate([low_docs, docs, high_docs])
    ends = patch_end[0] - (seq_rank * own - LOW)
    position = jnp.arange(ext_docs.shape[0], dtype=jnp.int32)
    last_doc = jnp.sum(
        jnp.where(position[None, :] == ends[:, None] - 1, ext_docs[None, :], 0), axis=1
    )
    earlier = (ext_docs[None, :] < last_doc[:, None]) & (position[None, :] < ends[:, None])
    doc_start = jnp.sum(earlier.astype(jnp.int32), axis=1)
    first = jnp.maximum(jnp.maximum(ends - WIN, doc_start), jnp.where(seq_rank == 0, LOW, 0))
    span = jnp.stack([first, ends], axis=1)
    offsets = jnp.clip(ends[::PG] - WIN, 0, LOW + own + HIGH - SLAB) // 16 * 16

    common = (offsets, span, low, high, keys, values, queries[0])
    attended, level = forward_call(common)
    peer_attended = to_peer(attended)

    mine, other, gain = latent_call(place, attended, norm_gain[None], cotangent[0], weights)
    peer_mine = to_peer(other)
    gain = gain.reshape(RING, 8, 8, LANES)[:, :, 0].transpose(1, 0, 2).reshape(8, 512)
    gain = gain + to_peer(gain)
    d_attended = d_attended_call(place, mine, other, weights)
    to_send = d_proj_call(mine, peer_mine, attended, peer_attended, halves(gain), d_attended)
    from_ring = ring(to_send, "first")

    inputs = common + (attended, level, d_attended)
    d_query, d_keys, d_values, d_low, d_high = backward_call(inputs, to_send[0])
    from_ring, d_low, d_high = lax.optimization_barrier((from_ring, d_low, d_high))
    from_above = lax.ppermute(d_low, "seq", downward)
    from_below = lax.ppermute(d_high, "seq", upward)
    from_ring = ring(first_sum(from_ring), "second")
    to_send = second_sum(place, from_ring)
    part, gain = stream_sum(stream_ring(to_send))
    d_proj = finish_call(place, stream_ring([part] * RING))
    d_gain = gain.reshape(-1)

    d_keys, d_values = rim_call(d_keys, d_values, from_below, from_above)
    return (d_query[None], d_keys[None], d_values[None], d_proj, d_gain)


def solution(mesh):
    in_specs = (
        P("dp", "seq", None),
        P("dp", "seq", None),
        P("dp", "seq"),
        P("dp", "seq", None),
        P("dp", "seq"),
        P("dp", "seq", None),
        P("seq", None),
        P(),
    )
    out_specs = (
        P("dp", "seq", None),
        P("dp", "seq", None),
        P("dp", "seq", None),
        P("seq", None),
        P(),
    )
    return jax.shard_map(
        on_device, mesh=mesh, in_specs=in_specs, out_specs=out_specs, check_vma=False
    )
```

```python
import functools
import math

import jax
import jax.numpy as jnp
from jax import lax
from jax.experimental import pallas as pl
from jax.experimental.pallas import tpu as pltpu
from jax.sharding import PartitionSpec as P

HEADS = 8
HD = 128
WIN = 128
LOW = 384
HIGH = 256
PG = 64
SLAB = 592
SHORT = 448
PAD = 400
PAIR = 2
RING = 4
LANES = 128

masked_score = -1e30
epsilon = 1e-05
score_scale = 1.0 / math.sqrt(HD)
bf16, f32 = jnp.bfloat16, jnp.float32
MIB = 1024 * 1024
VMEM_GRANT = 60 * MIB


def dot(a, b):
    return jnp.dot(a, b, preferred_element_type=f32)


def dot_rows(a, b):
    return lax.dot_general(a, b, (((1,), (1,)), ((), ())), preferred_element_type=f32)


def dot_columns(a, b):
    return lax.dot_general(a, b, (((0,), (0,)), ((), ())), preferred_element_type=f32)


def of_pair(pair):
    return slice(pair * PAIR * HD, (pair + 1) * PAIR * HD)


def spread(block):
    column = lax.broadcasted_iota(jnp.int32, block.shape, 1)
    zero = jnp.zeros_like(block)
    return jnp.concatenate(
        [jnp.where(column // HD == head, block, zero) for head in range(PAIR)]
    )


def gathered_heads(block):
    rows = block.shape[0] // PAIR
    return jnp.concatenate(
        [block[h * rows : (h + 1) * rows, h * HD : (h + 1) * HD] for h in range(PAIR)], axis=1
    )


def fetch_bytes(low_ref, high_ref, keys_ref, values_ref, key_ext, value_ext, sems):
    own = keys_ref.shape[0]
    copies = []
    for which, (own_ref, ext) in enumerate(((keys_ref, key_ext), (values_ref, value_ext))):
        parts = [
            (low_ref.at[pl.ds(which * LOW, LOW)], pl.ds(0, LOW)),
            (high_ref.at[pl.ds(which * HIGH, HIGH)], pl.ds(LOW + own, HIGH)),
        ]
        parts += [
            (own_ref.at[pl.ds(start, 256)], pl.ds(LOW + start, 256))
            for start in range(0, own, 256)
        ]
        for source, rows in parts:
            copies.append(
                pltpu.make_async_copy(source, ext.at[rows], sems.at[len(copies)])
            )
    return copies


def load_bytes(low_ref, high_ref, keys_ref, values_ref, key_ext, value_ext, sems, totals):
    copies = fetch_bytes(low_ref, high_ref, keys_ref, values_ref, key_ext, value_ext, sems)
    for copy in copies:
        copy.start()
    rows = key_ext.shape[0] - PAD
    for ext in (key_ext, value_ext):
        ext[rows:, :] = jnp.zeros((PAD, ext.shape[1]), bf16)
    for total in totals:
        total[...] = jnp.zeros_like(total)
    for copy in copies:
        copy.wait()


def visible_bias(offset, length, span):
    position = offset + lax.broadcasted_iota(jnp.int32, (length, PAIR * PG), 0)
    visible = (position >= span[0:1, :]) & (position < span[1:2, :])
    return jnp.where(visible, 0.0, masked_score)


def each_group(offset_ref, short_ref, groups, one_group):
    step = pl.program_id(0)

    def body(group, carry):
        offset = pl.multiple_of(offset_ref[step * groups + group], 16)
        short = short_ref[step * groups + group]

        @pl.when(short == 1)
        def _():
            one_group(group, offset, SHORT)

        @pl.when(short == 0)
        def _():
            one_group(group, offset, SLAB)

        return carry

    lax.fori_loop(0, groups, body, 0)


def forward_kernel(
    offset_ref, short_ref, span_ref, low_ref, high_ref, keys_ref, values_ref, query_ref,
    attended_ref, level_ref, key_ext, value_ext, sems,
):
    @pl.when(pl.program_id(0) == 0)
    def _():
        load_bytes(low_ref, high_ref, keys_ref, values_ref, key_ext, value_ext, sems, ())

    def one_group(group, offset, length):
        rows = pl.ds(pl.multiple_of(group * PG, PG), PG)
        marks = pl.ds(pl.multiple_of(group * 8, 8), 8)
        slab = pl.ds(offset, length)
        bias = visible_bias(offset, length, span_ref[marks, :])
        pairs = [of_pair(pair) for pair in range(HEADS // PAIR)]
        scores = [dot_rows(key_ext[slab, c], spread(query_ref[rows, c])) for c in pairs]
        scores = [x * score_scale + bias for x in scores]
        top = [jnp.max(x, axis=0, keepdims=True) for x in scores]
        expo = [jnp.exp(x - y) for x, y in zip(scores, top)]
        total = [jnp.sum(x, axis=0, keepdims=True) for x in expo]
        probs = [(x * (1.0 / y)).astype(bf16) for x, y in zip(expo, total)]
        attended = [dot_columns(x, value_ext[slab, c]) for x, c in zip(probs, pairs)]
        for x, c in zip(attended, pairs):
            attended_ref[rows, c] = gathered_heads(x).astype(bf16)
        level = [x + jnp.log(y) for x, y in zip(top, total)]
        level.append(jnp.zeros((8 - len(pairs), PAIR * PG), f32))
        level_ref[marks, :] = jnp.concatenate(level)

    each_group(offset_ref, short_ref, query_ref.shape[0] // PG, one_group)


def backward_kernel(
    offset_ref, short_ref, span_ref, low_ref, high_ref, keys_ref, values_ref, query_ref,
    attended_ref, level_ref, d_attended_ref, after_ref,
    d_query_ref, d_key_ref, d_value_ref, d_low_ref, d_high_ref,
    key_ext, value_ext, sems, d_key, d_value, key_out, value_out, out_sems,
):
    own = keys_ref.shape[0]

    @pl.when(pl.program_id(0) == 0)
    def _():
        load_bytes(
            low_ref, high_ref, keys_ref, values_ref, key_ext, value_ext, sems, (d_key, d_value)
        )

    def one_group(group, offset, length):
        rows = pl.ds(pl.multiple_of(group * PG, PG), PG)
        marks = pl.ds(pl.multiple_of(group * 8, 8), 8)
        slab = pl.ds(offset, length)
        bias = visible_bias(offset, length, span_ref[marks, :])
        levels = level_ref[marks, :]
        for first in range(0, HEADS // PAIR, 2):
            pairs = [of_pair(pair) for pair in range(first, first + 2)]
            query = [spread(query_ref[rows, c]) for c in pairs]
            d_out = [spread(d_attended_ref[rows, c]) for c in pairs]
            scores = [dot_rows(key_ext[slab, c], x) for x, c in zip(query, pairs)]
            d_probs = [dot_rows(value_ext[slab, c], x) for x, c in zip(d_out, pairs)]
            row_dot = []
            for c in pairs:
                both = d_attended_ref[rows, c].astype(f32) * attended_ref[rows, c].astype(f32)
                both = jnp.concatenate([both[:, h * HD : (h + 1) * HD] for h in range(PAIR)])
                row_dot.append(jnp.sum(both.T, axis=0, keepdims=True))
            probs = [
                jnp.exp(x * score_scale + bias - levels[first + i : first + i + 1, :])
                for i, x in enumerate(scores)
            ]
            d_scores = [
                (x * (y - z) * score_scale).astype(bf16)
                for x, y, z in zip(probs, d_probs, row_dot)
            ]
            probs = [x.astype(bf16) for x in probs]
            for c, x in zip(pairs, d_scores):
                d_query = dot_columns(x, key_ext[slab, c])
                d_query_ref[rows, c] = gathered_heads(d_query).astype(bf16)
            for c, x, y in zip(pairs, d_scores, query):
                d_key[slab, c] += dot(x, y)
            for c, x, y in zip(pairs, probs, d_out):
                d_value[slab, c] += dot(x, y)

    each_group(offset_ref, short_ref, query_ref.shape[0] // PG, one_group)

    @pl.when(pl.program_id(0) == pl.num_programs(0) - 1)
    def _():
        copies = []
        sources = ((d_key, key_out, d_key_ref), (d_value, value_out, d_value_ref))
        for which, (total, staged, out_ref) in enumerate(sources):
            parts = [(0, LOW, d_low_ref, which * LOW), (LOW + own, HIGH, d_high_ref, which * HIGH)]
            parts += [(LOW + start, 256, out_ref, start) for start in range(0, own, 256)]
            for start, count, out, place in parts:
                rows = slice(start, start + count)
                staged[rows, :] = total[rows, :].astype(bf16)
                copy = pltpu.make_async_copy(
                    staged.at[pl.ds(start, count)],
                    out.at[pl.ds(place, count)],
                    out_sems.at[len(copies)],
                )
                copy.start()
                copies.append(copy)
        for copy in copies:
            copy.wait()


def forward_call(inputs):
    own, width = inputs[5].shape
    patches = inputs[7].shape[0]
    steps = 4
    ext_rows = LOW + own + HIGH + PAD
    marks = patches // PG * 8
    block = pl.BlockSpec((patches // steps, width), lambda step, *scalars: (step, 0))
    mark_block = pl.BlockSpec((marks // steps, PAIR * PG), lambda step, *scalars: (step, 0))
    return pl.pallas_call(
        forward_kernel,
        out_shape=[
            jax.ShapeDtypeStruct((patches, width), bf16),
            jax.ShapeDtypeStruct((marks, PAIR * PG), f32),
        ],
        grid_spec=pltpu.PrefetchScalarGridSpec(
            num_scalar_prefetch=2,
            grid=(steps,),
            in_specs=[mark_block] + [pl.BlockSpec(memory_space=pl.ANY)] * 4 + [block],
            out_specs=[block, mark_block],
            scratch_shapes=[pltpu.VMEM((ext_rows, width), bf16)] * 2
            + [pltpu.SemaphoreType.DMA((2 * (2 + own // 256),))],
        ),
        compiler_params=pltpu.CompilerParams(vmem_limit_bytes=VMEM_GRANT),
        cost_estimate=pl.CostEstimate(
            flops=4 * HEADS * patches * SLAB * HD,
            bytes_accessed=20 * MIB,
            transcendentals=HEADS * patches * SLAB,
        ),
        name="attention_forward",
    )(*inputs)


def backward_call(inputs, after):
    own, width = inputs[5].shape
    patches = inputs[7].shape[0]
    steps = 4
    ext_rows = LOW + own + HIGH + PAD
    marks = patches // PG * 8
    block = pl.BlockSpec((patches // steps, width), lambda step, *scalars: (step, 0))
    mark_block = pl.BlockSpec((marks // steps, PAIR * PG), lambda step, *scalars: (step, 0))
    anywhere = pl.BlockSpec(memory_space=pl.ANY)
    rows = (patches, own, own, 2 * LOW, 2 * HIGH)
    return pl.pallas_call(
        backward_kernel,
        out_shape=[jax.ShapeDtypeStruct((count, width), bf16) for count in rows],
        grid_spec=pltpu.PrefetchScalarGridSpec(
            num_scalar_prefetch=2,
            grid=(steps,),
            in_specs=[mark_block]
            + [anywhere] * 4
            + [block, block, mark_block, block]
            + [anywhere],
            out_specs=[block] + [anywhere] * 4,
            scratch_shapes=[pltpu.VMEM((ext_rows, width), bf16)] * 2
            + [pltpu.SemaphoreType.DMA((2 * (2 + own // 256),))]
            + [pltpu.VMEM((ext_rows, width), f32)] * 2
            + [pltpu.VMEM((ext_rows - PAD, width), bf16)] * 2
            + [pltpu.SemaphoreType.DMA((2 * (2 + own // 256),))],
        ),
        compiler_params=pltpu.CompilerParams(vmem_limit_bytes=VMEM_GRANT),
        cost_estimate=pl.CostEstimate(
            flops=14 * HEADS * patches * SLAB * HD,
            bytes_accessed=40 * MIB,
            transcendentals=HEADS * patches * SLAB,
        ),
        name="attention_backward",
    )(*inputs, after)


def chip_block(place_ref, chunk):
    side, first, second = chunk // 16, chunk // 4 % 4, chunk % 4
    core = (place_ref[2] + side) % 2
    z = (place_ref[0] - jnp.where(core == 0, first, second) + RING) % RING
    x = (place_ref[1] - jnp.where(core == 0, second, first) + RING) % RING
    return (z * RING + x) * 2 + core


def fetch_weights(place_ref, weights_ref, weight, sems):
    copies = []
    for chunk in range(32):
        start = pl.multiple_of(chip_block(place_ref, chunk) * LANES, LANES)
        copies.append(
            pltpu.make_async_copy(
                weights_ref.at[pl.ds(start, LANES)],
                weight.at[pl.ds(chunk * LANES, LANES)],
                sems.at[chunk],
            )
        )
    return [copies[start : start + 4] for start in range(0, 32, 4)]


def latent_kernel(
    place_ref, attended_ref, norm_ref, cotangent_ref, weights_ref,
    mine_ref, other_ref, gain_ref,
    weight, cotangent, latent, square, mixed, mine, other, sems,
):
    pieces = fetch_weights(place_ref, weights_ref, weight, sems)
    rows_each = cotangent.shape[0] // 8
    cotangent_copies = [
        pltpu.make_async_copy(
            cotangent_ref.at[pl.ds(part * rows_each, rows_each)],
            cotangent.at[pl.ds(part * rows_each, rows_each)],
            sems.at[32 + part],
        )
        for part in range(8)
    ]
    for slab, copies in enumerate(pieces):
        for copy in copies:
            copy.start()
        if slab == 0:
            for copy in cotangent_copies:
                copy.start()
    square[...] = jnp.zeros_like(square)
    mixed[...] = jnp.zeros_like(mixed)

    def columns_of(chunk):
        return pl.ds(pl.multiple_of(chip_block(place_ref, chunk) * LANES, LANES), LANES)

    def multiply(slab):
        for copy in pieces[slab]:
            copy.wait()
        start = slab * 512
        latent[slab] = dot_rows(attended_ref[...], weight[start : start + 512, :])

    multiply(0)
    for copy in cotangent_copies:
        copy.wait()
    for slab in range(8):
        if slab < 7:
            multiply(slab + 1)
        columns = [columns_of(slab * 4 + part) for part in range(4)]
        scaled = [norm_ref[:, c] for c in columns]
        for start in range(0, square.shape[0], 64):
            rows = slice(start, start + 64)
            here = [latent[slab, rows, p * LANES : (p + 1) * LANES] for p in range(4)]
            arriving = [cotangent[rows, c].astype(f32) * g for c, g in zip(columns, scaled)]
            square[rows, :] += total_of([x * x for x in here])
            mixed[rows, :] += total_of([x * y for x, y in zip(here, arriving)])

    count = cotangent.shape[1]
    inverse = lax.rsqrt(jnp.sum(square[...], axis=1, keepdims=True) / count + epsilon)
    back = inverse * inverse * inverse * (jnp.sum(mixed[...], axis=1, keepdims=True) / count)
    square[...] = jnp.broadcast_to(inverse, square.shape)
    mixed[...] = jnp.broadcast_to(back, mixed.shape)

    def finish(slab, staged, out_ref):
        chunks = [slab * 4 + part for part in range(4)]
        columns = [columns_of(chunk) for chunk in chunks]
        norm = [norm_ref[:, c] for c in columns]
        gain = [jnp.zeros((8, LANES), f32)] * 4
        first = slab % 4 * 512
        for start in range(0, square.shape[0], 64):
            rows = slice(start, start + 64)
            scale, back = square[rows, :], mixed[rows, :]
            for part in range(4):
                here = latent[slab, rows, part * LANES : (part + 1) * LANES]
                scaled = cotangent[rows, columns[part]].astype(f32) * scale
                terms = scaled * here
                terms = [terms[k : k + 8, :] for k in range(0, 64, 8)]
                gain[part] += functools.reduce(jnp.add, terms)
                staged[rows, first + part * LANES : first + (part + 1) * LANES] = (
                    scaled * norm[part] - here * back
                ).astype(bf16)
        for part in range(4):
            spot = pl.ds(pl.multiple_of(chip_block(place_ref, chunks[part]) * 8, 8), 8)
            total = jnp.sum(gain[part], axis=0, keepdims=True)
            gain_ref[spot, :] = jnp.broadcast_to(total, (8, LANES))
        place = pl.ds(first, 512)
        copy = pltpu.make_async_copy(
            staged.at[:, place], out_ref.at[:, place], sems.at[40 + slab]
        )
        copy.start()
        return copy

    copies = [finish(slab, mine, mine_ref) for slab in range(4)]
    copies += [finish(slab, other, other_ref) for slab in range(4, 8)]
    for copy in copies:
        copy.wait()


def latent_call(place, attended, norm_gain, cotangent, weights):
    patches, count = cotangent.shape
    return pl.pallas_call(
        latent_kernel,
        out_shape=[
            jax.ShapeDtypeStruct((patches, count // 2), bf16),
            jax.ShapeDtypeStruct((patches, count // 2), bf16),
            jax.ShapeDtypeStruct((count // LANES * 8, LANES), f32),
        ],
        in_specs=[pl.BlockSpec(memory_space=pltpu.SMEM)]
        + [pl.BlockSpec(memory_space=pltpu.VMEM)] * 2
        + [pl.BlockSpec(memory_space=pl.ANY)] * 2,
        out_specs=[pl.BlockSpec(memory_space=pl.ANY)] * 2
        + [pl.BlockSpec(memory_space=pltpu.VMEM)],
        scratch_shapes=[
            pltpu.VMEM(weights.shape, bf16),
            pltpu.VMEM((patches, count), bf16),
            pltpu.VMEM((8, patches, count // 8), f32),
            pltpu.VMEM((patches, LANES), f32),
            pltpu.VMEM((patches, LANES), f32),
            pltpu.VMEM((patches, count // 2), bf16),
            pltpu.VMEM((patches, count // 2), bf16),
            pltpu.SemaphoreType.DMA((48,)),
        ],
        compiler_params=pltpu.CompilerParams(vmem_limit_bytes=VMEM_GRANT),
        cost_estimate=pl.CostEstimate(
            flops=2 * patches * count * 1024, bytes_accessed=18 * MIB, transcendentals=patches
        ),
        name="latent",
    )(place, attended, norm_gain, cotangent, weights)


def d_attended_kernel(
    place_ref, mine_ref, other_ref, weights_ref, out_ref, d_latent, weight, total, sems
):
    half = mine_ref.shape[1]
    pieces = fetch_weights(place_ref, weights_ref, weight, sems)
    copies = [
        pltpu.make_async_copy(
            (mine_ref, other_ref)[part // 2].at[:, pl.ds(part % 2 * half // 2, half // 2)],
            d_latent.at[part],
            sems.at[32 + part],
        )
        for part in range(4)
    ]
    for part in range(4):
        copies[part].start()
        for copy in pieces[2 * part] + pieces[2 * part + 1]:
            copy.start()
    for part in range(4):
        for copy in [copies[part]] + pieces[2 * part] + pieces[2 * part + 1]:
            copy.wait()
        terms = dot(d_latent[part], weight[part * 1024 : part * 1024 + 1024, :])
        if part == 0:
            total[...] = terms
        elif part < 3:
            total[...] += terms
        else:
            out_ref[...] = (total[...] + terms).astype(bf16)


def d_attended_call(place, mine, other, weights):
    patches, width = mine.shape[0], weights.shape[1]
    return pl.pallas_call(
        d_attended_kernel,
        out_shape=jax.ShapeDtypeStruct((patches, width), bf16),
        in_specs=[pl.BlockSpec(memory_space=pltpu.SMEM)]
        + [pl.BlockSpec(memory_space=pl.ANY)] * 3,
        out_specs=pl.BlockSpec(memory_space=pltpu.VMEM),
        scratch_shapes=[
            pltpu.VMEM((4, patches, mine.shape[1] // 2), bf16),
            pltpu.VMEM(weights.shape, bf16),
            pltpu.VMEM((patches, width), f32),
            pltpu.SemaphoreType.DMA((36,)),
        ],
        compiler_params=pltpu.CompilerParams(vmem_limit_bytes=VMEM_GRANT),
        cost_estimate=pl.CostEstimate(
            flops=4 * patches * mine.shape[1] * width, bytes_accessed=14 * MIB, transcendentals=0
        ),
        name="d_attended",
    )(place, mine, other, weights)


def d_proj_kernel(
    mine_ref, peer_ref, attended_ref, peer_attended_ref, gain_ref, after_ref, *refs
):
    outs, (d_latent, turned, staged, sems) = refs[:4], refs[4:]
    patches, width = attended_ref.shape
    arriving, leaving = [], []
    for k in (1, 2, 3, 0):
        columns = pl.ds((RING - k) % RING * 512, 512)
        for side, source in enumerate((mine_ref, peer_ref)):
            arriving.append(
                pltpu.make_async_copy(
                    source.at[:, columns],
                    d_latent.at[k, pl.ds(side * patches, patches)],
                    sems.at[2 * k + side],
                )
            )
            arriving[-1].start()
    turned[:, :patches] = attended_ref[...].T
    turned[:, patches:] = peer_attended_ref[...].T
    for step, k in enumerate((1, 2, 3, 0)):
        arriving[2 * step].wait()
        arriving[2 * step + 1].wait()
        staged[k, :width, :] = dot(turned[...], d_latent[k]).astype(bf16)
        staged[k, width:, :] = gain_ref[...]
        leaving.append(pltpu.make_async_copy(staged.at[k], outs[k], sems.at[8 + k]))
        leaving[-1].start()
    for copy in leaving:
        copy.wait()


def d_proj_call(mine, peer, attended, peer_attended, gain, after):
    patches, width = attended.shape
    vmem, anywhere = pl.BlockSpec(memory_space=pltpu.VMEM), pl.BlockSpec(memory_space=pl.ANY)
    return pl.pallas_call(
        d_proj_kernel,
        out_shape=[jax.ShapeDtypeStruct((width + 16, 512), bf16)] * 4,
        in_specs=[anywhere, anywhere, vmem, vmem, vmem, anywhere],
        out_specs=[anywhere] * 4,
        scratch_shapes=[
            pltpu.VMEM((4, 2 * patches, 512), bf16),
            pltpu.VMEM((width, 2 * patches), bf16),
            pltpu.VMEM((4, width + 16, 512), bf16),
            pltpu.SemaphoreType.DMA((12,)),
        ],
        compiler_params=pltpu.CompilerParams(vmem_limit_bytes=VMEM_GRANT),
        cost_estimate=pl.CostEstimate(
            flops=4 * patches * mine.shape[1] * width, bytes_accessed=12 * MIB, transcendentals=0
        ),
        name="d_proj",
    )(mine, peer, attended, peer_attended, gain, after)


def rim_kernel(
    key_in, value_in, below_ref, above_ref, key_out, value_out, key_rim, value_rim, sems
):
    own = key_in.shape[0]
    places = ((pl.ds(0, HIGH), pl.ds(0, HIGH)), (pl.ds(own - LOW, LOW), pl.ds(HIGH, LOW)))

    def copies(outward):
        found = []
        for which, (source, out, rim) in enumerate(
            ((key_in, key_out, key_rim), (value_in, value_out, value_rim))
        ):
            for side, (far, near) in enumerate(places):
                sem = sems.at[4 * outward + 2 * which + side]
                if outward:
                    found.append(pltpu.make_async_copy(rim.at[near], out.at[far], sem))
                else:
                    found.append(pltpu.make_async_copy(source.at[far], rim.at[near], sem))
        return found

    inward, outward = copies(0), copies(1)
    for copy in inward:
        copy.start()
    for which, rim in enumerate((key_rim, value_rim)):
        inward[2 * which].wait()
        below = below_ref[which * HIGH : (which + 1) * HIGH, :].astype(f32)
        rim[:HIGH, :] = (rim[:HIGH, :].astype(f32) + below).astype(bf16)
        outward[2 * which].start()
        inward[2 * which + 1].wait()
        above = above_ref[which * LOW : (which + 1) * LOW, :].astype(f32)
        rim[HIGH:, :] = (rim[HIGH:, :].astype(f32) + above).astype(bf16)
        outward[2 * which + 1].start()
    for copy in outward:
        copy.wait()


def rim_call(d_key, d_value, from_below, from_above):
    width = from_below.shape[1]
    anywhere = pl.BlockSpec(memory_space=pl.ANY)
    vmem = pl.BlockSpec(memory_space=pltpu.VMEM)
    return pl.pallas_call(
        rim_kernel,
        out_shape=[jax.ShapeDtypeStruct(d_key.shape, bf16)] * 2,
        in_specs=[anywhere, anywhere, vmem, vmem],
        out_specs=[anywhere, anywhere],
        scratch_shapes=[pltpu.VMEM((HIGH + LOW, width), bf16)] * 2
        + [pltpu.SemaphoreType.DMA((8,))],
        input_output_aliases={0: 0, 1: 1},
        compiler_params=pltpu.CompilerParams(vmem_limit_bytes=VMEM_GRANT),
        name="rims",
    )(d_key, d_value, from_below, from_above)


def along(which, distance):
    pairs = []
    for z in range(RING):
        for x in range(RING):
            for core in range(2):
                on_z = (which == "first") == (core == 0)
                to_z = (z + distance) % RING if on_z else z
                to_x = x if on_z else (x + distance) % RING
                pairs.append(((z * RING + x) * 2 + core, (to_z * RING + to_x) * 2 + core))
    return pairs


def to_peer(value):
    return lax.ppermute(value, "seq", [(i, i ^ 1) for i in range(lax.axis_size("seq"))])


def ring(values, which):
    return [values[0]] + [
        lax.ppermute(values[k], "seq", along(which, k)) for k in range(1, RING)
    ]


def total_of(parts):
    parts = [part.astype(f32) for part in parts]
    return (parts[0] + parts[2]) + (parts[1] + parts[3])


def halves(value):
    upper = value.astype(bf16)
    lower = (value - upper.astype(f32)).astype(bf16)
    return jnp.concatenate([upper, lower])


def joined(value):
    rows = value.shape[0] // 2
    return value[:rows] + value[rows:]


def first_sum_kernel(*refs):
    parts, outs = refs[:4], refs[4:]
    width = parts[0].shape[0] - 16
    gain = joined(total_of([ref[width:, :] for ref in parts]))
    gain = halves(
        jnp.concatenate([gain[:, k * LANES : (k + 1) * LANES] for k in range(RING)])
    )
    for k in range(RING):
        start = (RING - k) % RING * LANES
        columns = slice(start, start + LANES)
        outs[k][:width, :] = total_of([ref[:width, columns] for ref in parts]).astype(bf16)
        outs[k][width:, :] = gain


def first_sum(parts):
    width = parts[0].shape[0] - 16
    vmem = pl.BlockSpec(memory_space=pltpu.VMEM)
    return pl.pallas_call(
        first_sum_kernel,
        out_shape=[jax.ShapeDtypeStruct((width + 64, LANES), bf16)] * RING,
        in_specs=[vmem] * 4,
        out_specs=[vmem] * 4,
        compiler_params=pltpu.CompilerParams(vmem_limit_bytes=VMEM_GRANT),
        name="first_sum",
    )(*parts)


def second_sum_kernel(place_ref, *refs):
    parts, outs, total = refs[:4], refs[4:8], refs[8]
    width = total.shape[0]
    quarter = width // RING
    total[...] = total_of([ref[:width, :] for ref in parts])
    gain = halves(joined(total_of([ref[width:, :] for ref in parts])))
    for k in range(RING):
        start = pl.multiple_of((place_ref[3] + k) % RING * quarter, quarter)
        outs[k][:quarter, :] = total[pl.ds(start, quarter), :].astype(bf16)
        outs[k][quarter:, :] = gain


def second_sum(place, parts):
    width = parts[0].shape[0] - 64
    vmem = pl.BlockSpec(memory_space=pltpu.VMEM)
    return pl.pallas_call(
        second_sum_kernel,
        out_shape=[jax.ShapeDtypeStruct((width // RING + 64, LANES), bf16)] * RING,
        in_specs=[pl.BlockSpec(memory_space=pltpu.SMEM)]
        + [vmem] * 4,
        out_specs=[vmem] * RING,
        scratch_shapes=[pltpu.VMEM((width, LANES), f32)],
        name="second_sum",
    )(place, *parts)


def stream_sum_kernel(*refs):
    parts, part_ref, gain_ref = refs[:4], refs[4], refs[5]
    quarter = part_ref.shape[0]
    total = total_of([ref[...] for ref in parts])
    part_ref[...] = total[:quarter, :].astype(bf16)
    gain_ref[...] = joined(total[quarter:, :])


def stream_sum(parts):
    quarter = parts[0].shape[0] - 64
    vmem = pl.BlockSpec(memory_space=pltpu.VMEM)
    return pl.pallas_call(
        stream_sum_kernel,
        out_shape=[
            jax.ShapeDtypeStruct((quarter, LANES), bf16),
            jax.ShapeDtypeStruct((32, LANES), f32),
        ],
        in_specs=[vmem] * 4,
        out_specs=[vmem] * 2,
        name="stream_sum",
    )(*parts)


def finish_kernel(place_ref, *refs):
    parts, out_ref = refs[:4], refs[4]
    quarter = parts[0].shape[0]
    for k in range(RING):
        start = pl.multiple_of((place_ref[3] - k + RING) % RING * quarter, quarter)
        out_ref[:, pl.ds(start, quarter)] = parts[k][...].astype(f32).T


def finish_call(place, parts):
    quarter = parts[0].shape[0]
    vmem = pl.BlockSpec(memory_space=pltpu.VMEM)
    return pl.pallas_call(
        finish_kernel,
        out_shape=jax.ShapeDtypeStruct((LANES, RING * quarter), f32),
        in_specs=[pl.BlockSpec(memory_space=pltpu.SMEM)] + [vmem] * 4,
        out_specs=vmem,
        name="d_proj_rows",
    )(place, *parts)


def stream_ring(values):
    count = lax.axis_size("dp")
    return [values[0]] + [
        lax.ppermute(values[k], "dp", [(i, (i + k) % count) for i in range(count)])
        for k in range(1, RING)
    ]


def on_device(
    byte_keys, byte_values, doc_ids, queries, patch_end, cotangent, proj_weight, norm_gain
):
    own, width = byte_keys.shape[1:]
    patches = queries.shape[1]
    seq_count = lax.axis_size("seq")
    seq_rank = lax.axis_index("seq")
    upward = [(i, i + 1) for i in range(seq_count - 1)]
    downward = [(i + 1, i) for i in range(seq_count - 1)]
    keys, values, docs = byte_keys[0], byte_values[0], doc_ids[0]
    place = jnp.stack([seq_rank // (2 * RING), seq_rank // 2 % RING, seq_rank % 2, lax.axis_index("dp")])

    low_docs = lax.ppermute(docs[own - LOW :], "seq", upward)
    high_docs = lax.ppermute(docs[:HIGH], "seq", downward)
    low = jnp.concatenate([keys[own - LOW :], values[own - LOW :]])
    high = jnp.concatenate([keys[:HIGH], values[:HIGH]])
    low, high = lax.ppermute(low, "seq", upward), lax.ppermute(high, "seq", downward)
    weights = lax.all_gather(proj_weight, "seq", axis=0, tiled=True)

    ext_docs = jnp.concatenate([low_docs, docs, high_docs])
    ends = patch_end[0] - (seq_rank * own - LOW)
    position = jnp.arange(ext_docs.shape[0], dtype=jnp.int32)
    last_doc = jnp.sum(
        jnp.where(position[None, :] == ends[:, None] - 1, ext_docs[None, :], 0), axis=1
    )
    earlier = (ext_docs[None, :] < last_doc[:, None]) & (position[None, :] < ends[:, None])
    doc_start = jnp.sum(earlier.astype(jnp.int32), axis=1)
    first = jnp.maximum(jnp.maximum(ends - WIN, doc_start), jnp.where(seq_rank == 0, LOW, 0))
    groups = patches // PG
    marks = jnp.stack([first, ends]).reshape(2, groups, PG).transpose(1, 0, 2)
    marks = jnp.pad(jnp.tile(marks, (1, 1, PAIR)), ((0, 0), (0, 6), (0, 0)))
    marks = marks.reshape(groups * 8, PAIR * PG)
    offsets = (ends[::PG] - WIN) // 16 * 16
    short = (ends[PG - 1 :: PG] <= offsets + SHORT).astype(jnp.int32)

    common = (offsets, short, marks, low, high, keys, values, queries[0])
    attended, level = forward_call(common)
    peer_attended = to_peer(attended)

    mine, other, gain = latent_call(place, attended, norm_gain[None], cotangent[0], weights)
    peer_mine = to_peer(other)
    gain = gain.reshape(RING, 8, 8, LANES)[:, :, 0].transpose(1, 0, 2).reshape(8, 512)
    gain = gain + to_peer(gain)
    d_attended = d_attended_call(place, mine, other, weights)
    to_send = d_proj_call(mine, peer_mine, attended, peer_attended, halves(gain), d_attended)
    from_ring = ring(to_send, "first")

    inputs = common + (attended, level, d_attended)
    d_query, d_keys, d_values, d_low, d_high = backward_call(inputs, to_send[0])
    from_ring, d_query = lax.optimization_barrier((from_ring, d_query))
    from_ring = ring(first_sum(from_ring), "second")
    from_ring, d_low, d_high = lax.optimization_barrier((from_ring, d_low, d_high))
    from_above = lax.ppermute(d_low, "seq", downward)
    from_below = lax.ppermute(d_high, "seq", upward)
    to_send = second_sum(place, from_ring)
    part, gain = stream_sum(stream_ring(to_send))
    d_proj = finish_call(place, stream_ring([part] * RING))
    d_gain = gain.reshape(-1)

    d_keys, d_values = rim_call(d_keys, d_values, from_below, from_above)
    return (d_query[None], d_keys[None], d_values[None], d_proj, d_gain)


def solution(mesh):
    in_specs = (
        P("dp", "seq", None),
        P("dp", "seq", None),
        P("dp", "seq"),
        P("dp", "seq", None),
        P("dp", "seq"),
        P("dp", "seq", None),
        P("seq", None),
        P(),
    )
    out_specs = (
        P("dp", "seq", None),
        P("dp", "seq", None),
        P("dp", "seq", None),
        P("seq", None),
        P(),
    )
    return jax.shard_map(
        on_device, mesh=mesh, in_specs=in_specs, out_specs=out_specs, check_vma=False
    )
```

```python
import functools
import math

import jax
import jax.numpy as jnp
from jax import lax
from jax.experimental import pallas as pl
from jax.experimental.pallas import tpu as pltpu
from jax.sharding import PartitionSpec as P

HEADS = 8
HD = 128
WIN = 128
LOW = 384
HIGH = 256
PG = 64
SLAB = 592
SHORT = 448
PAD = 400
PAIR = 2
RING = 4
LANES = 128

masked_score = -1e30
epsilon = 1e-05
score_scale = 1.0 / math.sqrt(HD)
bf16, f32 = jnp.bfloat16, jnp.float32
MIB = 1024 * 1024
VMEM_GRANT = 60 * MIB


def dot(a, b):
    return jnp.dot(a, b, preferred_element_type=f32)


def dot_rows(a, b):
    return lax.dot_general(a, b, (((1,), (1,)), ((), ())), preferred_element_type=f32)


def dot_columns(a, b):
    return lax.dot_general(a, b, (((0,), (0,)), ((), ())), preferred_element_type=f32)


def of_pair(pair):
    return slice(pair * PAIR * HD, (pair + 1) * PAIR * HD)


def spread(block):
    column = lax.broadcasted_iota(jnp.int32, block.shape, 1)
    zero = jnp.zeros_like(block)
    return jnp.concatenate(
        [jnp.where(column // HD == head, block, zero) for head in range(PAIR)]
    )


def gathered_heads(block):
    rows = block.shape[0] // PAIR
    return jnp.concatenate(
        [block[h * rows : (h + 1) * rows, h * HD : (h + 1) * HD] for h in range(PAIR)], axis=1
    )


def fetch_bytes(low_ref, high_ref, keys_ref, values_ref, key_ext, value_ext, sems):
    own = keys_ref.shape[0]
    copies = []
    for which, (own_ref, ext) in enumerate(((keys_ref, key_ext), (values_ref, value_ext))):
        parts = [
            (low_ref.at[pl.ds(which * LOW, LOW)], pl.ds(0, LOW)),
            (high_ref.at[pl.ds(which * HIGH, HIGH)], pl.ds(LOW + own, HIGH)),
        ]
        parts += [
            (own_ref.at[pl.ds(start, 256)], pl.ds(LOW + start, 256))
            for start in range(0, own, 256)
        ]
        for source, rows in parts:
            copies.append(
                pltpu.make_async_copy(source, ext.at[rows], sems.at[len(copies)])
            )
    return copies


def load_bytes(low_ref, high_ref, keys_ref, values_ref, key_ext, value_ext, sems, totals):
    copies = fetch_bytes(low_ref, high_ref, keys_ref, values_ref, key_ext, value_ext, sems)
    for copy in copies:
        copy.start()
    rows = key_ext.shape[0] - PAD
    for ext in (key_ext, value_ext):
        ext[rows:, :] = jnp.zeros((PAD, ext.shape[1]), bf16)
    for total in totals:
        total[...] = jnp.zeros_like(total)
    for copy in copies:
        copy.wait()


def visible_bias(offset, length, span):
    position = offset + lax.broadcasted_iota(jnp.int32, (length, PAIR * PG), 0)
    visible = (position >= span[0:1, :]) & (position < span[1:2, :])
    return jnp.where(visible, 0.0, masked_score)


def each_group(offset_ref, short_ref, groups, one_group):
    step = pl.program_id(0)

    def body(group, carry):
        offset = pl.multiple_of(offset_ref[step * groups + group], 16)
        short = short_ref[step * groups + group]

        @pl.when(short == 1)
        def _():
            one_group(group, offset, SHORT)

        @pl.when(short == 0)
        def _():
            one_group(group, offset, SLAB)

        return carry

    lax.fori_loop(0, groups, body, 0)


def forward_kernel(
    offset_ref, short_ref, span_ref, low_ref, high_ref, keys_ref, values_ref, query_ref,
    attended_ref, level_ref, key_ext, value_ext, sems,
):
    @pl.when(pl.program_id(0) == 0)
    def _():
        load_bytes(low_ref, high_ref, keys_ref, values_ref, key_ext, value_ext, sems, ())

    def one_group(group, offset, length):
        rows = pl.ds(pl.multiple_of(group * PG, PG), PG)
        marks = pl.ds(pl.multiple_of(group * 8, 8), 8)
        slab = pl.ds(offset, length)
        bias = visible_bias(offset, length, span_ref[marks, :])
        pairs = [of_pair(pair) for pair in range(HEADS // PAIR)]
        scores = [dot_rows(key_ext[slab, c], spread(query_ref[rows, c])) for c in pairs]
        scores = [x * score_scale + bias for x in scores]
        top = [jnp.max(x, axis=0, keepdims=True) for x in scores]
        expo = [jnp.exp(x - y) for x, y in zip(scores, top)]
        total = [jnp.sum(x, axis=0, keepdims=True) for x in expo]
        probs = [(x * (1.0 / y)).astype(bf16) for x, y in zip(expo, total)]
        attended = [dot_columns(x, value_ext[slab, c]) for x, c in zip(probs, pairs)]
        for x, c in zip(attended, pairs):
            attended_ref[rows, c] = gathered_heads(x).astype(bf16)
        level = [x + jnp.log(y) for x, y in zip(top, total)]
        level.append(jnp.zeros((8 - len(pairs), PAIR * PG), f32))
        level_ref[marks, :] = jnp.concatenate(level)

    each_group(offset_ref, short_ref, query_ref.shape[0] // PG, one_group)


def backward_kernel(
    offset_ref, short_ref, span_ref, low_ref, high_ref, keys_ref, values_ref, query_ref,
    attended_ref, level_ref, d_attended_ref, after_ref,
    d_query_ref, d_key_ref, d_value_ref, d_low_ref, d_high_ref,
    key_ext, value_ext, sems, d_key, d_value, key_out, value_out, out_sems,
):
    own = keys_ref.shape[0]

    @pl.when(pl.program_id(0) == 0)
    def _():
        load_bytes(
            low_ref, high_ref, keys_ref, values_ref, key_ext, value_ext, sems, (d_key, d_value)
        )

    def one_group(group, offset, length):
        rows = pl.ds(pl.multiple_of(group * PG, PG), PG)
        marks = pl.ds(pl.multiple_of(group * 8, 8), 8)
        slab = pl.ds(offset, length)
        bias = visible_bias(offset, length, span_ref[marks, :])
        levels = level_ref[marks, :]
        for first in range(0, HEADS // PAIR, 2):
            pairs = [of_pair(pair) for pair in range(first, first + 2)]
            query = [spread(query_ref[rows, c]) for c in pairs]
            d_out = [spread(d_attended_ref[rows, c]) for c in pairs]
            scores = [dot_rows(key_ext[slab, c], x) for x, c in zip(query, pairs)]
            d_probs = [dot_rows(value_ext[slab, c], x) for x, c in zip(d_out, pairs)]
            row_dot = []
            for c in pairs:
                both = d_attended_ref[rows, c].astype(f32) * attended_ref[rows, c].astype(f32)
                both = jnp.concatenate([both[:, h * HD : (h + 1) * HD] for h in range(PAIR)])
                row_dot.append(jnp.sum(both.T, axis=0, keepdims=True))
            probs = [
                jnp.exp(x * score_scale + bias - levels[first + i : first + i + 1, :])
                for i, x in enumerate(scores)
            ]
            d_scores = [
                (x * (y - z) * score_scale).astype(bf16)
                for x, y, z in zip(probs, d_probs, row_dot)
            ]
            probs = [x.astype(bf16) for x in probs]
            for c, x in zip(pairs, d_scores):
                d_query = dot_columns(x, key_ext[slab, c])
                d_query_ref[rows, c] = gathered_heads(d_query).astype(bf16)
            for c, x, y in zip(pairs, d_scores, query):
                d_key[slab, c] += dot(x, y)
            for c, x, y in zip(pairs, probs, d_out):
                d_value[slab, c] += dot(x, y)

    each_group(offset_ref, short_ref, query_ref.shape[0] // PG, one_group)

    @pl.when(pl.program_id(0) == pl.num_programs(0) - 1)
    def _():
        copies = []
        sources = ((d_key, key_out, d_key_ref), (d_value, value_out, d_value_ref))
        for which, (total, staged, out_ref) in enumerate(sources):
            parts = [(0, LOW, d_low_ref, which * LOW), (LOW + own, HIGH, d_high_ref, which * HIGH)]
            parts += [(LOW + start, 256, out_ref, start) for start in range(0, own, 256)]
            for start, count, out, place in parts:
                rows = slice(start, start + count)
                staged[rows, :] = total[rows, :].astype(bf16)
                copy = pltpu.make_async_copy(
                    staged.at[pl.ds(start, count)],
                    out.at[pl.ds(place, count)],
                    out_sems.at[len(copies)],
                )
                copy.start()
                copies.append(copy)
        for copy in copies:
            copy.wait()


def forward_call(inputs):
    own, width = inputs[5].shape
    patches = inputs[7].shape[0]
    steps = 4
    ext_rows = LOW + own + HIGH + PAD
    marks = patches // PG * 8
    block = pl.BlockSpec((patches // steps, width), lambda step, *scalars: (step, 0))
    mark_block = pl.BlockSpec((marks // steps, PAIR * PG), lambda step, *scalars: (step, 0))
    return pl.pallas_call(
        forward_kernel,
        out_shape=[
            jax.ShapeDtypeStruct((patches, width), bf16),
            jax.ShapeDtypeStruct((marks, PAIR * PG), f32),
        ],
        grid_spec=pltpu.PrefetchScalarGridSpec(
            num_scalar_prefetch=2,
            grid=(steps,),
            in_specs=[mark_block] + [pl.BlockSpec(memory_space=pl.ANY)] * 4 + [block],
            out_specs=[block, mark_block],
            scratch_shapes=[pltpu.VMEM((ext_rows, width), bf16)] * 2
            + [pltpu.SemaphoreType.DMA((2 * (2 + own // 256),))],
        ),
        compiler_params=pltpu.CompilerParams(vmem_limit_bytes=VMEM_GRANT),
        cost_estimate=pl.CostEstimate(
            flops=4 * HEADS * patches * SLAB * HD,
            bytes_accessed=20 * MIB,
            transcendentals=HEADS * patches * SLAB,
        ),
        name="attention_forward",
    )(*inputs)


def backward_call(inputs, after):
    own, width = inputs[5].shape
    patches = inputs[7].shape[0]
    steps = 4
    ext_rows = LOW + own + HIGH + PAD
    marks = patches // PG * 8
    block = pl.BlockSpec((patches // steps, width), lambda step, *scalars: (step, 0))
    mark_block = pl.BlockSpec((marks // steps, PAIR * PG), lambda step, *scalars: (step, 0))
    anywhere = pl.BlockSpec(memory_space=pl.ANY)
    rows = (patches, own, own, 2 * LOW, 2 * HIGH)
    return pl.pallas_call(
        backward_kernel,
        out_shape=[jax.ShapeDtypeStruct((count, width), bf16) for count in rows],
        grid_spec=pltpu.PrefetchScalarGridSpec(
            num_scalar_prefetch=2,
            grid=(steps,),
            in_specs=[mark_block]
            + [anywhere] * 4
            + [block, block, mark_block, block]
            + [anywhere],
            out_specs=[block] + [anywhere] * 4,
            scratch_shapes=[pltpu.VMEM((ext_rows, width), bf16)] * 2
            + [pltpu.SemaphoreType.DMA((2 * (2 + own // 256),))]
            + [pltpu.VMEM((ext_rows, width), f32)] * 2
            + [pltpu.VMEM((ext_rows - PAD, width), bf16)] * 2
            + [pltpu.SemaphoreType.DMA((2 * (2 + own // 256),))],
        ),
        compiler_params=pltpu.CompilerParams(vmem_limit_bytes=VMEM_GRANT),
        cost_estimate=pl.CostEstimate(
            flops=14 * HEADS * patches * SLAB * HD,
            bytes_accessed=40 * MIB,
            transcendentals=HEADS * patches * SLAB,
        ),
        name="attention_backward",
    )(*inputs, after)


def chip_block(place_ref, chunk):
    side, first, second = chunk // 16, chunk // 4 % 4, chunk % 4
    core = (place_ref[2] + side) % 2
    z = (place_ref[0] - jnp.where(core == 0, first, second) + RING) % RING
    x = (place_ref[1] - jnp.where(core == 0, second, first) + RING) % RING
    return (z * RING + x) * 2 + core


def fetch_weights(place_ref, weights_ref, weight, sems):
    copies = []
    for chunk in range(32):
        start = pl.multiple_of(chip_block(place_ref, chunk) * LANES, LANES)
        copies.append(
            pltpu.make_async_copy(
                weights_ref.at[pl.ds(start, LANES)],
                weight.at[pl.ds(chunk * LANES, LANES)],
                sems.at[chunk],
            )
        )
    return [copies[start : start + 4] for start in range(0, 32, 4)]


def latent_kernel(
    place_ref, attended_ref, norm_ref, cotangent_ref, weights_ref,
    mine_ref, other_ref, gain_ref,
    weight, cotangent, latent, square, mixed, mine, other, sems,
):
    pieces = fetch_weights(place_ref, weights_ref, weight, sems)
    rows_each = cotangent.shape[0] // 8
    cotangent_copies = [
        pltpu.make_async_copy(
            cotangent_ref.at[pl.ds(part * rows_each, rows_each)],
            cotangent.at[pl.ds(part * rows_each, rows_each)],
            sems.at[32 + part],
        )
        for part in range(8)
    ]
    for slab, copies in enumerate(pieces):
        for copy in copies:
            copy.start()
        if slab == 0:
            for copy in cotangent_copies:
                copy.start()
    square[...] = jnp.zeros_like(square)
    mixed[...] = jnp.zeros_like(mixed)

    def columns_of(chunk):
        return pl.ds(pl.multiple_of(chip_block(place_ref, chunk) * LANES, LANES), LANES)

    def multiply(slab):
        for copy in pieces[slab]:
            copy.wait()
        start = slab * 512
        latent[slab] = dot_rows(attended_ref[...], weight[start : start + 512, :])

    multiply(0)
    for copy in cotangent_copies:
        copy.wait()
    for slab in range(8):
        if slab < 7:
            multiply(slab + 1)
        columns = [columns_of(slab * 4 + part) for part in range(4)]
        scaled = [norm_ref[:, c] for c in columns]
        for start in range(0, square.shape[0], 64):
            rows = slice(start, start + 64)
            here = [latent[slab, rows, p * LANES : (p + 1) * LANES] for p in range(4)]
            arriving = [cotangent[rows, c].astype(f32) * g for c, g in zip(columns, scaled)]
            square[rows, :] += total_of([x * x for x in here])
            mixed[rows, :] += total_of([x * y for x, y in zip(here, arriving)])

    count = cotangent.shape[1]
    inverse = lax.rsqrt(jnp.sum(square[...], axis=1, keepdims=True) / count + epsilon)
    back = inverse * inverse * inverse * (jnp.sum(mixed[...], axis=1, keepdims=True) / count)
    square[...] = jnp.broadcast_to(inverse, square.shape)
    mixed[...] = jnp.broadcast_to(back, mixed.shape)

    def finish(slab, staged, out_ref):
        chunks = [slab * 4 + part for part in range(4)]
        columns = [columns_of(chunk) for chunk in chunks]
        norm = [norm_ref[:, c] for c in columns]
        gain = [jnp.zeros((8, LANES), f32)] * 4
        first = slab % 4 * 512
        for start in range(0, square.shape[0], 64):
            rows = slice(start, start + 64)
            scale, back = square[rows, :], mixed[rows, :]
            for part in range(4):
                here = latent[slab, rows, part * LANES : (part + 1) * LANES]
                scaled = cotangent[rows, columns[part]].astype(f32) * scale
                terms = scaled * here
                terms = [terms[k : k + 8, :] for k in range(0, 64, 8)]
                gain[part] += functools.reduce(jnp.add, terms)
                staged[rows, first + part * LANES : first + (part + 1) * LANES] = (
                    scaled * norm[part] - here * back
                ).astype(bf16)
        for part in range(4):
            spot = pl.ds(pl.multiple_of(chip_block(place_ref, chunks[part]) * 8, 8), 8)
            total = jnp.sum(gain[part], axis=0, keepdims=True)
            gain_ref[spot, :] = jnp.broadcast_to(total, (8, LANES))
        place = pl.ds(first, 512)
        copy = pltpu.make_async_copy(
            staged.at[:, place], out_ref.at[:, place], sems.at[40 + slab]
        )
        copy.start()
        return copy

    copies = [finish(slab, mine, mine_ref) for slab in range(4)]
    copies += [finish(slab, other, other_ref) for slab in range(4, 8)]
    for copy in copies:
        copy.wait()


def latent_call(place, attended, norm_gain, cotangent, weights):
    patches, count = cotangent.shape
    return pl.pallas_call(
        latent_kernel,
        out_shape=[
            jax.ShapeDtypeStruct((patches, count // 2), bf16),
            jax.ShapeDtypeStruct((patches, count // 2), bf16),
            jax.ShapeDtypeStruct((count // LANES * 8, LANES), f32),
        ],
        in_specs=[pl.BlockSpec(memory_space=pltpu.SMEM)]
        + [pl.BlockSpec(memory_space=pltpu.VMEM)] * 2
        + [pl.BlockSpec(memory_space=pl.ANY)] * 2,
        out_specs=[pl.BlockSpec(memory_space=pl.ANY)] * 2
        + [pl.BlockSpec(memory_space=pltpu.VMEM)],
        scratch_shapes=[
            pltpu.VMEM(weights.shape, bf16),
            pltpu.VMEM((patches, count), bf16),
            pltpu.VMEM((8, patches, count // 8), f32),
            pltpu.VMEM((patches, LANES), f32),
            pltpu.VMEM((patches, LANES), f32),
            pltpu.VMEM((patches, count // 2), bf16),
            pltpu.VMEM((patches, count // 2), bf16),
            pltpu.SemaphoreType.DMA((48,)),
        ],
        compiler_params=pltpu.CompilerParams(vmem_limit_bytes=VMEM_GRANT),
        cost_estimate=pl.CostEstimate(
            flops=2 * patches * count * 1024, bytes_accessed=18 * MIB, transcendentals=patches
        ),
        name="latent",
    )(place, attended, norm_gain, cotangent, weights)


def d_attended_kernel(
    place_ref, mine_ref, other_ref, weights_ref, out_ref, d_latent, weight, total, sems
):
    half = mine_ref.shape[1]
    pieces = fetch_weights(place_ref, weights_ref, weight, sems)
    copies = [
        pltpu.make_async_copy(
            (mine_ref, other_ref)[part // 2].at[:, pl.ds(part % 2 * half // 2, half // 2)],
            d_latent.at[part],
            sems.at[32 + part],
        )
        for part in range(4)
    ]
    for part in range(4):
        copies[part].start()
        for copy in pieces[2 * part] + pieces[2 * part + 1]:
            copy.start()
    for part in range(4):
        for copy in [copies[part]] + pieces[2 * part] + pieces[2 * part + 1]:
            copy.wait()
        terms = dot(d_latent[part], weight[part * 1024 : part * 1024 + 1024, :])
        if part == 0:
            total[...] = terms
        elif part < 3:
            total[...] += terms
        else:
            out_ref[...] = (total[...] + terms).astype(bf16)


def d_attended_call(place, mine, other, weights):
    patches, width = mine.shape[0], weights.shape[1]
    return pl.pallas_call(
        d_attended_kernel,
        out_shape=jax.ShapeDtypeStruct((patches, width), bf16),
        in_specs=[pl.BlockSpec(memory_space=pltpu.SMEM)]
        + [pl.BlockSpec(memory_space=pl.ANY)] * 3,
        out_specs=pl.BlockSpec(memory_space=pltpu.VMEM),
        scratch_shapes=[
            pltpu.VMEM((4, patches, mine.shape[1] // 2), bf16),
            pltpu.VMEM(weights.shape, bf16),
            pltpu.VMEM((patches, width), f32),
            pltpu.SemaphoreType.DMA((36,)),
        ],
        compiler_params=pltpu.CompilerParams(vmem_limit_bytes=VMEM_GRANT),
        cost_estimate=pl.CostEstimate(
            flops=4 * patches * mine.shape[1] * width, bytes_accessed=14 * MIB, transcendentals=0
        ),
        name="d_attended",
    )(place, mine, other, weights)


def d_proj_kernel(
    mine_ref, peer_ref, attended_ref, peer_attended_ref, gain_ref, after_ref, *refs
):
    outs, (d_latent, rows, turned, staged, sems) = refs[:4], refs[4:]
    patches, width = attended_ref.shape
    arriving, leaving, sides = [], [], []
    for side, source in enumerate((attended_ref, peer_attended_ref)):
        sides.append(pltpu.make_async_copy(source, rows.at[side], sems.at[12 + side]))
        sides[-1].start()
    for k in (1, 2, 3, 0):
        columns = pl.ds((RING - k) % RING * 512, 512)
        for side, source in enumerate((mine_ref, peer_ref)):
            arriving.append(
                pltpu.make_async_copy(
                    source.at[:, columns],
                    d_latent.at[k, pl.ds(side * patches, patches)],
                    sems.at[2 * k + side],
                )
            )
            arriving[-1].start()
    for side in range(2):
        sides[side].wait()
        turned[:, side * patches : (side + 1) * patches] = rows[side].T
    for step, k in enumerate((1, 2, 3, 0)):
        arriving[2 * step].wait()
        arriving[2 * step + 1].wait()
        staged[k, :width, :] = dot(turned[...], d_latent[k]).astype(bf16)
        staged[k, width:, :] = gain_ref[...]
        leaving.append(pltpu.make_async_copy(staged.at[k], outs[k], sems.at[8 + k]))
        leaving[-1].start()
    for copy in leaving:
        copy.wait()


def d_proj_call(mine, peer, attended, peer_attended, gain, after):
    patches, width = attended.shape
    vmem, anywhere = pl.BlockSpec(memory_space=pltpu.VMEM), pl.BlockSpec(memory_space=pl.ANY)
    return pl.pallas_call(
        d_proj_kernel,
        out_shape=[jax.ShapeDtypeStruct((width + 16, 512), bf16)] * 4,
        in_specs=[anywhere] * 4 + [vmem, anywhere],
        out_specs=[anywhere] * 4,
        scratch_shapes=[
            pltpu.VMEM((4, 2 * patches, 512), bf16),
            pltpu.VMEM((2, patches, width), bf16),
            pltpu.VMEM((width, 2 * patches), bf16),
            pltpu.VMEM((4, width + 16, 512), bf16),
            pltpu.SemaphoreType.DMA((14,)),
        ],
        compiler_params=pltpu.CompilerParams(vmem_limit_bytes=VMEM_GRANT),
        cost_estimate=pl.CostEstimate(
            flops=4 * patches * mine.shape[1] * width, bytes_accessed=12 * MIB, transcendentals=0
        ),
        name="d_proj",
    )(mine, peer, attended, peer_attended, gain, after)


def rim_kernel(
    key_in, value_in, below_ref, above_ref, key_out, value_out, key_rim, value_rim, sems
):
    own = key_in.shape[0]
    places = ((pl.ds(0, HIGH), pl.ds(0, HIGH)), (pl.ds(own - LOW, LOW), pl.ds(HIGH, LOW)))

    def copies(outward):
        found = []
        for which, (source, out, rim) in enumerate(
            ((key_in, key_out, key_rim), (value_in, value_out, value_rim))
        ):
            for side, (far, near) in enumerate(places):
                sem = sems.at[4 * outward + 2 * which + side]
                if outward:
                    found.append(pltpu.make_async_copy(rim.at[near], out.at[far], sem))
                else:
                    found.append(pltpu.make_async_copy(source.at[far], rim.at[near], sem))
        return found

    inward, outward = copies(0), copies(1)
    for copy in inward:
        copy.start()
    for which, rim in enumerate((key_rim, value_rim)):
        inward[2 * which].wait()
        below = below_ref[which * HIGH : (which + 1) * HIGH, :].astype(f32)
        rim[:HIGH, :] = (rim[:HIGH, :].astype(f32) + below).astype(bf16)
        outward[2 * which].start()
        inward[2 * which + 1].wait()
        above = above_ref[which * LOW : (which + 1) * LOW, :].astype(f32)
        rim[HIGH:, :] = (rim[HIGH:, :].astype(f32) + above).astype(bf16)
        outward[2 * which + 1].start()
    for copy in outward:
        copy.wait()


def rim_call(d_key, d_value, from_below, from_above):
    width = from_below.shape[1]
    anywhere = pl.BlockSpec(memory_space=pl.ANY)
    vmem = pl.BlockSpec(memory_space=pltpu.VMEM)
    return pl.pallas_call(
        rim_kernel,
        out_shape=[jax.ShapeDtypeStruct(d_key.shape, bf16)] * 2,
        in_specs=[anywhere, anywhere, vmem, vmem],
        out_specs=[anywhere, anywhere],
        scratch_shapes=[pltpu.VMEM((HIGH + LOW, width), bf16)] * 2
        + [pltpu.SemaphoreType.DMA((8,))],
        input_output_aliases={0: 0, 1: 1},
        compiler_params=pltpu.CompilerParams(vmem_limit_bytes=VMEM_GRANT),
        name="rims",
    )(d_key, d_value, from_below, from_above)


def along(which, distance):
    pairs = []
    for z in range(RING):
        for x in range(RING):
            for core in range(2):
                on_z = (which == "first") == (core == 0)
                to_z = (z + distance) % RING if on_z else z
                to_x = x if on_z else (x + distance) % RING
                pairs.append(((z * RING + x) * 2 + core, (to_z * RING + to_x) * 2 + core))
    return pairs


def to_peer(value):
    return lax.ppermute(value, "seq", [(i, i ^ 1) for i in range(lax.axis_size("seq"))])


def ring(values, which):
    return [values[0]] + [
        lax.ppermute(values[k], "seq", along(which, k)) for k in range(1, RING)
    ]


def total_of(parts):
    parts = [part.astype(f32) for part in parts]
    return (parts[0] + parts[2]) + (parts[1] + parts[3])


def halves(value):
    upper = value.astype(bf16)
    lower = (value - upper.astype(f32)).astype(bf16)
    return jnp.concatenate([upper, lower])


def joined(value):
    rows = value.shape[0] // 2
    return value[:rows] + value[rows:]


def first_sum_kernel(*refs):
    parts, outs = refs[:4], refs[4:]
    width = parts[0].shape[0] - 16
    gain = joined(total_of([ref[width:, :] for ref in parts]))
    gain = halves(
        jnp.concatenate([gain[:, k * LANES : (k + 1) * LANES] for k in range(RING)])
    )
    for k in range(RING):
        start = (RING - k) % RING * LANES
        columns = slice(start, start + LANES)
        outs[k][:width, :] = total_of([ref[:width, columns] for ref in parts]).astype(bf16)
        outs[k][width:, :] = gain


def first_sum(parts):
    width = parts[0].shape[0] - 16
    vmem = pl.BlockSpec(memory_space=pltpu.VMEM)
    return pl.pallas_call(
        first_sum_kernel,
        out_shape=[jax.ShapeDtypeStruct((width + 64, LANES), bf16)] * RING,
        in_specs=[vmem] * 4,
        out_specs=[vmem] * 4,
        compiler_params=pltpu.CompilerParams(vmem_limit_bytes=VMEM_GRANT),
        name="first_sum",
    )(*parts)


def second_sum_kernel(place_ref, *refs):
    parts, outs, total = refs[:4], refs[4:8], refs[8]
    width = total.shape[0]
    quarter = width // RING
    total[...] = total_of([ref[:width, :] for ref in parts])
    gain = halves(joined(total_of([ref[width:, :] for ref in parts])))
    for k in range(RING):
        start = pl.multiple_of((place_ref[3] + k) % RING * quarter, quarter)
        outs[k][:quarter, :] = total[pl.ds(start, quarter), :].astype(bf16)
        outs[k][quarter:, :] = gain


def second_sum(place, parts):
    width = parts[0].shape[0] - 64
    vmem = pl.BlockSpec(memory_space=pltpu.VMEM)
    return pl.pallas_call(
        second_sum_kernel,
        out_shape=[jax.ShapeDtypeStruct((width // RING + 64, LANES), bf16)] * RING,
        in_specs=[pl.BlockSpec(memory_space=pltpu.SMEM)]
        + [vmem] * 4,
        out_specs=[vmem] * RING,
        scratch_shapes=[pltpu.VMEM((width, LANES), f32)],
        name="second_sum",
    )(place, *parts)


def stream_sum_kernel(*refs):
    parts, part_ref, gain_ref = refs[:4], refs[4], refs[5]
    quarter = part_ref.shape[0]
    total = total_of([ref[...] for ref in parts])
    part_ref[...] = total[:quarter, :].astype(bf16)
    gain_ref[...] = joined(total[quarter:, :])


def stream_sum(parts):
    quarter = parts[0].shape[0] - 64
    vmem = pl.BlockSpec(memory_space=pltpu.VMEM)
    return pl.pallas_call(
        stream_sum_kernel,
        out_shape=[
            jax.ShapeDtypeStruct((quarter, LANES), bf16),
            jax.ShapeDtypeStruct((32, LANES), f32),
        ],
        in_specs=[vmem] * 4,
        out_specs=[vmem] * 2,
        name="stream_sum",
    )(*parts)


def finish_kernel(place_ref, *refs):
    parts, out_ref = refs[:4], refs[5]
    quarter = parts[0].shape[0]
    for k in range(RING):
        start = pl.multiple_of((place_ref[3] - k + RING) % RING * quarter, quarter)
        out_ref[:, pl.ds(start, quarter)] = parts[k][...].astype(f32).T


def finish_call(place, parts, after):
    quarter = parts[0].shape[0]
    vmem = pl.BlockSpec(memory_space=pltpu.VMEM)
    return pl.pallas_call(
        finish_kernel,
        out_shape=jax.ShapeDtypeStruct((LANES, RING * quarter), f32),
        in_specs=[pl.BlockSpec(memory_space=pltpu.SMEM)]
        + [vmem] * 4
        + [pl.BlockSpec(memory_space=pl.ANY)],
        out_specs=vmem,
        name="d_proj_rows",
    )(place, *parts, after)


def stream_ring(values):
    count = lax.axis_size("dp")
    return [values[0]] + [
        lax.ppermute(values[k], "dp", [(i, (i + k) % count) for i in range(count)])
        for k in range(1, RING)
    ]


def on_device(
    byte_keys, byte_values, doc_ids, queries, patch_end, cotangent, proj_weight, norm_gain
):
    own, width = byte_keys.shape[1:]
    patches = queries.shape[1]
    seq_count = lax.axis_size("seq")
    seq_rank = lax.axis_index("seq")
    upward = [(i, i + 1) for i in range(seq_count - 1)]
    downward = [(i + 1, i) for i in range(seq_count - 1)]
    keys, values, docs = byte_keys[0], byte_values[0], doc_ids[0]
    place = jnp.stack([seq_rank // (2 * RING), seq_rank // 2 % RING, seq_rank % 2, lax.axis_index("dp")])

    low_docs = lax.ppermute(docs[own - LOW :], "seq", upward)
    high_docs = lax.ppermute(docs[:HIGH], "seq", downward)
    low = jnp.concatenate([keys[own - LOW :], values[own - LOW :]])
    high = jnp.concatenate([keys[:HIGH], values[:HIGH]])
    low, high = lax.ppermute(low, "seq", upward), lax.ppermute(high, "seq", downward)
    weights = lax.all_gather(proj_weight, "seq", axis=0, tiled=True)

    ext_docs = jnp.concatenate([low_docs, docs, high_docs])
    ends = patch_end[0] - (seq_rank * own - LOW)
    position = jnp.arange(ext_docs.shape[0], dtype=jnp.int32)
    last_doc = jnp.sum(
        jnp.where(position[None, :] == ends[:, None] - 1, ext_docs[None, :], 0), axis=1
    )
    earlier = (ext_docs[None, :] < last_doc[:, None]) & (position[None, :] < ends[:, None])
    doc_start = jnp.sum(earlier.astype(jnp.int32), axis=1)
    first = jnp.maximum(jnp.maximum(ends - WIN, doc_start), jnp.where(seq_rank == 0, LOW, 0))
    groups = patches // PG
    marks = jnp.stack([first, ends]).reshape(2, groups, PG).transpose(1, 0, 2)
    marks = jnp.pad(jnp.tile(marks, (1, 1, PAIR)), ((0, 0), (0, 6), (0, 0)))
    marks = marks.reshape(groups * 8, PAIR * PG)
    offsets = (ends[::PG] - WIN) // 16 * 16
    short = (ends[PG - 1 :: PG] <= offsets + SHORT).astype(jnp.int32)

    common = (offsets, short, marks, low, high, keys, values, queries[0])
    attended, level = forward_call(common)
    peer_attended = to_peer(attended)

    mine, other, gain = latent_call(place, attended, norm_gain[None], cotangent[0], weights)
    peer_mine = to_peer(other)
    gain = gain.reshape(RING, 8, 8, LANES)[:, :, 0].transpose(1, 0, 2).reshape(8, 512)
    gain = gain + to_peer(gain)
    d_attended = d_attended_call(place, mine, other, weights)
    to_send = d_proj_call(mine, peer_mine, attended, peer_attended, halves(gain), d_attended)
    from_ring = ring(to_send, "first")

    inputs = common + (attended, level, d_attended)
    d_query, d_keys, d_values, d_low, d_high = backward_call(inputs, to_send[0])
    from_ring, d_query = lax.optimization_barrier((from_ring, d_query))
    from_ring = ring(first_sum(from_ring), "second")
    from_ring[1], d_low, d_high = lax.optimization_barrier((from_ring[1], d_low, d_high))
    from_above = lax.ppermute(d_low, "seq", downward)
    from_below = lax.ppermute(d_high, "seq", upward)
    to_send = second_sum(place, from_ring)
    part, gain = stream_sum(stream_ring(to_send))
    d_keys, d_values = rim_call(d_keys, d_values, from_below, from_above)
    d_proj = finish_call(place, stream_ring([part] * RING), d_keys)
    d_gain = gain.reshape(-1)
    return (d_query[None], d_keys[None], d_values[None], d_proj, d_gain)


def solution(mesh):
    in_specs = (
        P("dp", "seq", None),
        P("dp", "seq", None),
        P("dp", "seq"),
        P("dp", "seq", None),
        P("dp", "seq"),
        P("dp", "seq", None),
        P("seq", None),
        P(),
    )
    out_specs = (
        P("dp", "seq", None),
        P("dp", "seq", None),
        P("dp", "seq", None),
        P("seq", None),
        P(),
    )
    return jax.shard_map(
        on_device, mesh=mesh, in_specs=in_specs, out_specs=out_specs, check_vma=False
    )
```

```python
import functools
import math

import jax
import jax.numpy as jnp
from jax import lax
from jax.experimental import pallas as pl
from jax.experimental.pallas import tpu as pltpu
from jax.sharding import PartitionSpec as P

HEADS = 8
HD = 128
WIN = 128
LOW = 384
HIGH = 256
PG = 64
SLAB = 592
SHORT = 448
PAD = 400
PAIR = 2
RING = 4
LANES = 128

masked_score = -1e30
epsilon = 1e-05
score_scale = 1.0 / math.sqrt(HD)
bf16, f32 = jnp.bfloat16, jnp.float32
MIB = 1024 * 1024
VMEM_GRANT = 60 * MIB


def dot(a, b):
    return jnp.dot(a, b, preferred_element_type=f32)


def dot_rows(a, b):
    return lax.dot_general(a, b, (((1,), (1,)), ((), ())), preferred_element_type=f32)


def dot_columns(a, b):
    return lax.dot_general(a, b, (((0,), (0,)), ((), ())), preferred_element_type=f32)


def of_pair(pair):
    return slice(pair * PAIR * HD, (pair + 1) * PAIR * HD)


def spread(block):
    column = lax.broadcasted_iota(jnp.int32, block.shape, 1)
    zero = jnp.zeros_like(block)
    return jnp.concatenate(
        [jnp.where(column // HD == head, block, zero) for head in range(PAIR)]
    )


def gathered_heads(block):
    rows = block.shape[0] // PAIR
    return jnp.concatenate(
        [block[h * rows : (h + 1) * rows, h * HD : (h + 1) * HD] for h in range(PAIR)], axis=1
    )


def fetch_bytes(low_ref, high_ref, keys_ref, values_ref, key_ext, value_ext, sems):
    own = keys_ref.shape[0]
    copies = []
    for which, (own_ref, ext) in enumerate(((keys_ref, key_ext), (values_ref, value_ext))):
        parts = [
            (low_ref.at[pl.ds(which * LOW, LOW)], pl.ds(0, LOW)),
            (high_ref.at[pl.ds(which * HIGH, HIGH)], pl.ds(LOW + own, HIGH)),
        ]
        parts += [
            (own_ref.at[pl.ds(start, 256)], pl.ds(LOW + start, 256))
            for start in range(0, own, 256)
        ]
        for source, rows in parts:
            copies.append(
                pltpu.make_async_copy(source, ext.at[rows], sems.at[len(copies)])
            )
    return copies


def load_bytes(low_ref, high_ref, keys_ref, values_ref, key_ext, value_ext, sems, totals):
    copies = fetch_bytes(low_ref, high_ref, keys_ref, values_ref, key_ext, value_ext, sems)
    for copy in copies:
        copy.start()
    rows = key_ext.shape[0] - PAD
    for ext in (key_ext, value_ext):
        ext[rows:, :] = jnp.zeros((PAD, ext.shape[1]), bf16)
    for total in totals:
        total[...] = jnp.zeros_like(total)
    for copy in copies:
        copy.wait()


def visible_bias(offset, length, span):
    position = offset + lax.broadcasted_iota(jnp.int32, (length, PAIR * PG), 0)
    visible = (position >= span[0:1, :]) & (position < span[1:2, :])
    return jnp.where(visible, 0.0, masked_score)


def each_group(offset_ref, short_ref, groups, one_group):
    step = pl.program_id(0)

    def body(group, carry):
        offset = pl.multiple_of(offset_ref[step * groups + group], 16)
        short = short_ref[step * groups + group]

        @pl.when(short == 1)
        def _():
            one_group(group, offset, SHORT)

        @pl.when(short == 0)
        def _():
            one_group(group, offset, SLAB)

        return carry

    lax.fori_loop(0, groups, body, 0)


def forward_kernel(
    offset_ref, short_ref, span_ref, low_ref, high_ref, keys_ref, values_ref, query_ref,
    attended_ref, level_ref, key_ext, value_ext, sems,
):
    @pl.when(pl.program_id(0) == 0)
    def _():
        load_bytes(low_ref, high_ref, keys_ref, values_ref, key_ext, value_ext, sems, ())

    def one_group(group, offset, length):
        rows = pl.ds(pl.multiple_of(group * PG, PG), PG)
        marks = pl.ds(pl.multiple_of(group * 8, 8), 8)
        slab = pl.ds(offset, length)
        bias = visible_bias(offset, length, span_ref[marks, :])
        pairs = [of_pair(pair) for pair in range(HEADS // PAIR)]
        scores = [dot_rows(key_ext[slab, c], spread(query_ref[rows, c])) for c in pairs]
        scores = [x * score_scale + bias for x in scores]
        top = [jnp.max(x, axis=0, keepdims=True) for x in scores]
        expo = [jnp.exp(x - y) for x, y in zip(scores, top)]
        total = [jnp.sum(x, axis=0, keepdims=True) for x in expo]
        probs = [(x * (1.0 / y)).astype(bf16) for x, y in zip(expo, total)]
        attended = [dot_columns(x, value_ext[slab, c]) for x, c in zip(probs, pairs)]
        for x, c in zip(attended, pairs):
            attended_ref[rows, c] = gathered_heads(x).astype(bf16)
        level = [x + jnp.log(y) for x, y in zip(top, total)]
        level.append(jnp.zeros((8 - len(pairs), PAIR * PG), f32))
        level_ref[marks, :] = jnp.concatenate(level)

    each_group(offset_ref, short_ref, query_ref.shape[0] // PG, one_group)


def backward_kernel(
    offset_ref, short_ref, span_ref, low_ref, high_ref, keys_ref, values_ref, query_ref,
    attended_ref, level_ref, d_attended_ref, after_ref,
    d_query_ref, d_key_ref, d_value_ref, d_low_ref, d_high_ref,
    key_ext, value_ext, sems, d_key, d_value, key_out, value_out, out_sems,
):
    own = keys_ref.shape[0]

    @pl.when(pl.program_id(0) == 0)
    def _():
        load_bytes(
            low_ref, high_ref, keys_ref, values_ref, key_ext, value_ext, sems, (d_key, d_value)
        )

    def one_group(group, offset, length):
        rows = pl.ds(pl.multiple_of(group * PG, PG), PG)
        marks = pl.ds(pl.multiple_of(group * 8, 8), 8)
        slab = pl.ds(offset, length)
        bias = visible_bias(offset, length, span_ref[marks, :])
        levels = level_ref[marks, :]
        for first in range(0, HEADS // PAIR, 2):
            pairs = [of_pair(pair) for pair in range(first, first + 2)]
            query = [spread(query_ref[rows, c]) for c in pairs]
            d_out = [spread(d_attended_ref[rows, c]) for c in pairs]
            scores = [dot_rows(key_ext[slab, c], x) for x, c in zip(query, pairs)]
            d_probs = [dot_rows(value_ext[slab, c], x) for x, c in zip(d_out, pairs)]
            row_dot = []
            for c in pairs:
                both = d_attended_ref[rows, c].astype(f32) * attended_ref[rows, c].astype(f32)
                both = jnp.concatenate([both[:, h * HD : (h + 1) * HD] for h in range(PAIR)])
                row_dot.append(jnp.sum(both.T, axis=0, keepdims=True))
            probs = [
                jnp.exp(x * score_scale + bias - levels[first + i : first + i + 1, :])
                for i, x in enumerate(scores)
            ]
            d_scores = [
                (x * (y - z) * score_scale).astype(bf16)
                for x, y, z in zip(probs, d_probs, row_dot)
            ]
            probs = [x.astype(bf16) for x in probs]
            for c, x in zip(pairs, d_scores):
                d_query = dot_columns(x, key_ext[slab, c])
                d_query_ref[rows, c] = gathered_heads(d_query).astype(bf16)
            for c, x, y in zip(pairs, d_scores, query):
                d_key[slab, c] += dot(x, y)
            for c, x, y in zip(pairs, probs, d_out):
                d_value[slab, c] += dot(x, y)

    each_group(offset_ref, short_ref, query_ref.shape[0] // PG, one_group)

    @pl.when(pl.program_id(0) == pl.num_programs(0) - 1)
    def _():
        copies = []
        sources = ((d_key, key_out, d_key_ref), (d_value, value_out, d_value_ref))
        for which, (total, staged, out_ref) in enumerate(sources):
            parts = [(0, LOW, d_low_ref, which * LOW), (LOW + own, HIGH, d_high_ref, which * HIGH)]
            parts += [(LOW + start, 256, out_ref, start) for start in range(0, own, 256)]
            for start, count, out, place in parts:
                rows = slice(start, start + count)
                staged[rows, :] = total[rows, :].astype(bf16)
                copy = pltpu.make_async_copy(
                    staged.at[pl.ds(start, count)],
                    out.at[pl.ds(place, count)],
                    out_sems.at[len(copies)],
                )
                copy.start()
                copies.append(copy)
        for copy in copies:
            copy.wait()


def forward_call(inputs):
    own, width = inputs[5].shape
    patches = inputs[7].shape[0]
    steps = 4
    ext_rows = LOW + own + HIGH + PAD
    marks = patches // PG * 8
    block = pl.BlockSpec((patches // steps, width), lambda step, *scalars: (step, 0))
    mark_block = pl.BlockSpec((marks // steps, PAIR * PG), lambda step, *scalars: (step, 0))
    return pl.pallas_call(
        forward_kernel,
        out_shape=[
            jax.ShapeDtypeStruct((patches, width), bf16),
            jax.ShapeDtypeStruct((marks, PAIR * PG), f32),
        ],
        grid_spec=pltpu.PrefetchScalarGridSpec(
            num_scalar_prefetch=2,
            grid=(steps,),
            in_specs=[mark_block] + [pl.BlockSpec(memory_space=pl.ANY)] * 4 + [block],
            out_specs=[block, mark_block],
            scratch_shapes=[pltpu.VMEM((ext_rows, width), bf16)] * 2
            + [pltpu.SemaphoreType.DMA((2 * (2 + own // 256),))],
        ),
        compiler_params=pltpu.CompilerParams(vmem_limit_bytes=VMEM_GRANT),
        cost_estimate=pl.CostEstimate(
            flops=4 * HEADS * patches * SLAB * HD,
            bytes_accessed=20 * MIB,
            transcendentals=HEADS * patches * SLAB,
        ),
        name="attention_forward",
    )(*inputs)


def backward_call(inputs, after):
    own, width = inputs[5].shape
    patches = inputs[7].shape[0]
    steps = 4
    ext_rows = LOW + own + HIGH + PAD
    marks = patches // PG * 8
    block = pl.BlockSpec((patches // steps, width), lambda step, *scalars: (step, 0))
    mark_block = pl.BlockSpec((marks // steps, PAIR * PG), lambda step, *scalars: (step, 0))
    anywhere = pl.BlockSpec(memory_space=pl.ANY)
    rows = (patches, own, own, 2 * LOW, 2 * HIGH)
    return pl.pallas_call(
        backward_kernel,
        out_shape=[jax.ShapeDtypeStruct((count, width), bf16) for count in rows],
        grid_spec=pltpu.PrefetchScalarGridSpec(
            num_scalar_prefetch=2,
            grid=(steps,),
            in_specs=[mark_block]
            + [anywhere] * 4
            + [block, block, mark_block, block]
            + [anywhere],
            out_specs=[block] + [anywhere] * 4,
            scratch_shapes=[pltpu.VMEM((ext_rows, width), bf16)] * 2
            + [pltpu.SemaphoreType.DMA((2 * (2 + own // 256),))]
            + [pltpu.VMEM((ext_rows, width), f32)] * 2
            + [pltpu.VMEM((ext_rows - PAD, width), bf16)] * 2
            + [pltpu.SemaphoreType.DMA((2 * (2 + own // 256),))],
        ),
        compiler_params=pltpu.CompilerParams(vmem_limit_bytes=VMEM_GRANT),
        cost_estimate=pl.CostEstimate(
            flops=14 * HEADS * patches * SLAB * HD,
            bytes_accessed=40 * MIB,
            transcendentals=HEADS * patches * SLAB,
        ),
        name="attention_backward",
    )(*inputs, after)


def chip_block(place_ref, chunk):
    side, first, second = chunk // 16, chunk // 4 % 4, chunk % 4
    core = (place_ref[2] + side) % 2
    z = (place_ref[0] - jnp.where(core == 0, first, second) + RING) % RING
    x = (place_ref[1] - jnp.where(core == 0, second, first) + RING) % RING
    return (z * RING + x) * 2 + core


def fetch_weights(place_ref, weights_ref, weight, sems):
    copies = []
    for chunk in range(32):
        start = pl.multiple_of(chip_block(place_ref, chunk) * LANES, LANES)
        copies.append(
            pltpu.make_async_copy(
                weights_ref.at[pl.ds(start, LANES)],
                weight.at[pl.ds(chunk * LANES, LANES)],
                sems.at[chunk],
            )
        )
    return [copies[start : start + 4] for start in range(0, 32, 4)]


def latent_kernel(
    place_ref, attended_ref, norm_ref, cotangent_ref, weights_ref,
    mine_ref, other_ref, gain_ref,
    weight, cotangent, latent, square, mixed, mine, other, sems,
):
    pieces = fetch_weights(place_ref, weights_ref, weight, sems)
    rows_each = cotangent.shape[0] // 8
    cotangent_copies = [
        pltpu.make_async_copy(
            cotangent_ref.at[pl.ds(part * rows_each, rows_each)],
            cotangent.at[pl.ds(part * rows_each, rows_each)],
            sems.at[32 + part],
        )
        for part in range(8)
    ]
    for slab, copies in enumerate(pieces):
        for copy in copies:
            copy.start()
        if slab == 0:
            for copy in cotangent_copies:
                copy.start()
    square[...] = jnp.zeros_like(square)
    mixed[...] = jnp.zeros_like(mixed)

    def columns_of(chunk):
        return pl.ds(pl.multiple_of(chip_block(place_ref, chunk) * LANES, LANES), LANES)

    def multiply(slab):
        for copy in pieces[slab]:
            copy.wait()
        start = slab * 512
        latent[slab] = dot_rows(attended_ref[...], weight[start : start + 512, :])

    multiply(0)
    for copy in cotangent_copies:
        copy.wait()
    for slab in range(8):
        if slab < 7:
            multiply(slab + 1)
        columns = [columns_of(slab * 4 + part) for part in range(4)]
        scaled = [norm_ref[:, c] for c in columns]
        for start in range(0, square.shape[0], 64):
            rows = slice(start, start + 64)
            here = [latent[slab, rows, p * LANES : (p + 1) * LANES] for p in range(4)]
            arriving = [cotangent[rows, c].astype(f32) * g for c, g in zip(columns, scaled)]
            square[rows, :] += total_of([x * x for x in here])
            mixed[rows, :] += total_of([x * y for x, y in zip(here, arriving)])

    count = cotangent.shape[1]
    inverse = lax.rsqrt(jnp.sum(square[...], axis=1, keepdims=True) / count + epsilon)
    back = inverse * inverse * inverse * (jnp.sum(mixed[...], axis=1, keepdims=True) / count)
    square[...] = jnp.broadcast_to(inverse, square.shape)
    mixed[...] = jnp.broadcast_to(back, mixed.shape)

    def finish(slab, staged, out_ref):
        chunks = [slab * 4 + part for part in range(4)]
        columns = [columns_of(chunk) for chunk in chunks]
        norm = [norm_ref[:, c] for c in columns]
        gain = [jnp.zeros((8, LANES), f32)] * 4
        first = slab % 4 * 512
        for start in range(0, square.shape[0], 64):
            rows = slice(start, start + 64)
            scale, back = square[rows, :], mixed[rows, :]
            for part in range(4):
                here = latent[slab, rows, part * LANES : (part + 1) * LANES]
                scaled = cotangent[rows, columns[part]].astype(f32) * scale
                terms = scaled * here
                terms = [terms[k : k + 8, :] for k in range(0, 64, 8)]
                gain[part] += functools.reduce(jnp.add, terms)
                staged[rows, first + part * LANES : first + (part + 1) * LANES] = (
                    scaled * norm[part] - here * back
                ).astype(bf16)
        for part in range(4):
            spot = pl.ds(pl.multiple_of(chip_block(place_ref, chunks[part]) * 8, 8), 8)
            total = jnp.sum(gain[part], axis=0, keepdims=True)
            gain_ref[spot, :] = jnp.broadcast_to(total, (8, LANES))
        place = pl.ds(first, 512)
        copy = pltpu.make_async_copy(
            staged.at[:, place], out_ref.at[:, place], sems.at[40 + slab]
        )
        copy.start()
        return copy

    copies = [finish(slab, mine, mine_ref) for slab in range(4)]
    copies += [finish(slab, other, other_ref) for slab in range(4, 8)]
    for copy in copies:
        copy.wait()


def latent_call(place, attended, norm_gain, cotangent, weights):
    patches, count = cotangent.shape
    return pl.pallas_call(
        latent_kernel,
        out_shape=[
            jax.ShapeDtypeStruct((patches, count // 2), bf16),
            jax.ShapeDtypeStruct((patches, count // 2), bf16),
            jax.ShapeDtypeStruct((count // LANES * 8, LANES), f32),
        ],
        in_specs=[pl.BlockSpec(memory_space=pltpu.SMEM)]
        + [pl.BlockSpec(memory_space=pltpu.VMEM)] * 2
        + [pl.BlockSpec(memory_space=pl.ANY)] * 2,
        out_specs=[pl.BlockSpec(memory_space=pl.ANY)] * 2
        + [pl.BlockSpec(memory_space=pltpu.VMEM)],
        scratch_shapes=[
            pltpu.VMEM(weights.shape, bf16),
            pltpu.VMEM((patches, count), bf16),
            pltpu.VMEM((8, patches, count // 8), f32),
            pltpu.VMEM((patches, LANES), f32),
            pltpu.VMEM((patches, LANES), f32),
            pltpu.VMEM((patches, count // 2), bf16),
            pltpu.VMEM((patches, count // 2), bf16),
            pltpu.SemaphoreType.DMA((48,)),
        ],
        compiler_params=pltpu.CompilerParams(vmem_limit_bytes=VMEM_GRANT),
        cost_estimate=pl.CostEstimate(
            flops=2 * patches * count * 1024, bytes_accessed=18 * MIB, transcendentals=patches
        ),
        name="latent",
    )(place, attended, norm_gain, cotangent, weights)


def d_attended_kernel(
    place_ref, mine_ref, other_ref, weights_ref, out_ref, d_latent, weight, total, sems
):
    half = mine_ref.shape[1]
    pieces = fetch_weights(place_ref, weights_ref, weight, sems)
    copies = [
        pltpu.make_async_copy(
            (mine_ref, other_ref)[part // 2].at[:, pl.ds(part % 2 * half // 2, half // 2)],
            d_latent.at[part],
            sems.at[32 + part],
        )
        for part in range(4)
    ]
    for part in range(4):
        copies[part].start()
        for copy in pieces[2 * part] + pieces[2 * part + 1]:
            copy.start()
    for part in range(4):
        for copy in [copies[part]] + pieces[2 * part] + pieces[2 * part + 1]:
            copy.wait()
        terms = dot(d_latent[part], weight[part * 1024 : part * 1024 + 1024, :])
        if part == 0:
            total[...] = terms
        elif part < 3:
            total[...] += terms
        else:
            out_ref[...] = (total[...] + terms).astype(bf16)


def d_attended_call(place, mine, other, weights):
    patches, width = mine.shape[0], weights.shape[1]
    return pl.pallas_call(
        d_attended_kernel,
        out_shape=jax.ShapeDtypeStruct((patches, width), bf16),
        in_specs=[pl.BlockSpec(memory_space=pltpu.SMEM)]
        + [pl.BlockSpec(memory_space=pl.ANY)] * 3,
        out_specs=pl.BlockSpec(memory_space=pltpu.VMEM),
        scratch_shapes=[
            pltpu.VMEM((4, patches, mine.shape[1] // 2), bf16),
            pltpu.VMEM(weights.shape, bf16),
            pltpu.VMEM((patches, width), f32),
            pltpu.SemaphoreType.DMA((36,)),
        ],
        compiler_params=pltpu.CompilerParams(vmem_limit_bytes=VMEM_GRANT),
        cost_estimate=pl.CostEstimate(
            flops=4 * patches * mine.shape[1] * width, bytes_accessed=14 * MIB, transcendentals=0
        ),
        name="d_attended",
    )(place, mine, other, weights)


def d_proj_kernel(
    mine_ref, peer_ref, attended_ref, peer_attended_ref, gain_ref, after_ref, *refs
):
    outs, (d_latent, rows, turned, staged, sems) = refs[:4], refs[4:]
    patches, width = attended_ref.shape
    arriving, leaving, sides = [], [], []
    for side, source in enumerate((attended_ref, peer_attended_ref)):
        sides.append(pltpu.make_async_copy(source, rows.at[side], sems.at[12 + side]))
        sides[-1].start()
    for k in (1, 2, 3, 0):
        columns = pl.ds((RING - k) % RING * 512, 512)
        for side, source in enumerate((mine_ref, peer_ref)):
            arriving.append(
                pltpu.make_async_copy(
                    source.at[:, columns],
                    d_latent.at[k, pl.ds(side * patches, patches)],
                    sems.at[2 * k + side],
                )
            )
            arriving[-1].start()
    for side in range(2):
        sides[side].wait()
        turned[:, side * patches : (side + 1) * patches] = rows[side].T
    for step, k in enumerate((1, 2, 3, 0)):
        arriving[2 * step].wait()
        arriving[2 * step + 1].wait()
        staged[k, :width, :] = dot(turned[...], d_latent[k]).astype(bf16)
        staged[k, width:, :] = gain_ref[...]
        leaving.append(pltpu.make_async_copy(staged.at[k], outs[k], sems.at[8 + k]))
        leaving[-1].start()
    for copy in leaving:
        copy.wait()


def d_proj_call(mine, peer, attended, peer_attended, gain, after):
    patches, width = attended.shape
    vmem, anywhere = pl.BlockSpec(memory_space=pltpu.VMEM), pl.BlockSpec(memory_space=pl.ANY)
    return pl.pallas_call(
        d_proj_kernel,
        out_shape=[jax.ShapeDtypeStruct((width + 16, 512), bf16)] * 4,
        in_specs=[anywhere] * 4 + [vmem, anywhere],
        out_specs=[anywhere] * 4,
        scratch_shapes=[
            pltpu.VMEM((4, 2 * patches, 512), bf16),
            pltpu.VMEM((2, patches, width), bf16),
            pltpu.VMEM((width, 2 * patches), bf16),
            pltpu.VMEM((4, width + 16, 512), bf16),
            pltpu.SemaphoreType.DMA((14,)),
        ],
        compiler_params=pltpu.CompilerParams(vmem_limit_bytes=VMEM_GRANT),
        cost_estimate=pl.CostEstimate(
            flops=4 * patches * mine.shape[1] * width, bytes_accessed=12 * MIB, transcendentals=0
        ),
        name="d_proj",
    )(mine, peer, attended, peer_attended, gain, after)


def rim_kernel(
    key_in, value_in, below_ref, above_ref, key_out, value_out, key_rim, value_rim, sems
):
    own = key_in.shape[0]
    places = ((pl.ds(0, HIGH), pl.ds(0, HIGH)), (pl.ds(own - LOW, LOW), pl.ds(HIGH, LOW)))

    def copies(outward):
        found = []
        for which, (source, out, rim) in enumerate(
            ((key_in, key_out, key_rim), (value_in, value_out, value_rim))
        ):
            for side, (far, near) in enumerate(places):
                sem = sems.at[4 * outward + 2 * which + side]
                if outward:
                    found.append(pltpu.make_async_copy(rim.at[near], out.at[far], sem))
                else:
                    found.append(pltpu.make_async_copy(source.at[far], rim.at[near], sem))
        return found

    inward, outward = copies(0), copies(1)
    for copy in inward:
        copy.start()
    for which, rim in enumerate((key_rim, value_rim)):
        inward[2 * which].wait()
        below = below_ref[which * HIGH : (which + 1) * HIGH, :].astype(f32)
        rim[:HIGH, :] = (rim[:HIGH, :].astype(f32) + below).astype(bf16)
        outward[2 * which].start()
        inward[2 * which + 1].wait()
        above = above_ref[which * LOW : (which + 1) * LOW, :].astype(f32)
        rim[HIGH:, :] = (rim[HIGH:, :].astype(f32) + above).astype(bf16)
        outward[2 * which + 1].start()
    for copy in outward:
        copy.wait()


def rim_call(d_key, d_value, from_below, from_above):
    width = from_below.shape[1]
    anywhere = pl.BlockSpec(memory_space=pl.ANY)
    vmem = pl.BlockSpec(memory_space=pltpu.VMEM)
    return pl.pallas_call(
        rim_kernel,
        out_shape=[jax.ShapeDtypeStruct(d_key.shape, bf16)] * 2,
        in_specs=[anywhere, anywhere, vmem, vmem],
        out_specs=[anywhere, anywhere],
        scratch_shapes=[pltpu.VMEM((HIGH + LOW, width), bf16)] * 2
        + [pltpu.SemaphoreType.DMA((8,))],
        input_output_aliases={0: 0, 1: 1},
        compiler_params=pltpu.CompilerParams(vmem_limit_bytes=VMEM_GRANT),
        name="rims",
    )(d_key, d_value, from_below, from_above)


def along(which, distance):
    pairs = []
    for z in range(RING):
        for x in range(RING):
            for core in range(2):
                on_z = (which == "first") == (core == 0)
                to_z = (z + distance) % RING if on_z else z
                to_x = x if on_z else (x + distance) % RING
                pairs.append(((z * RING + x) * 2 + core, (to_z * RING + to_x) * 2 + core))
    return pairs


def to_peer(value):
    return lax.ppermute(value, "seq", [(i, i ^ 1) for i in range(lax.axis_size("seq"))])


def ring(values, which):
    return [values[0]] + [
        lax.ppermute(values[k], "seq", along(which, k)) for k in range(1, RING)
    ]


def total_of(parts):
    parts = [part.astype(f32) for part in parts]
    return (parts[0] + parts[2]) + (parts[1] + parts[3])


def halves(value):
    upper = value.astype(bf16)
    lower = (value - upper.astype(f32)).astype(bf16)
    return jnp.concatenate([upper, lower])


def joined(value):
    rows = value.shape[0] // 2
    return value[:rows] + value[rows:]


def first_sum_kernel(place_ref, *refs):
    parts, outs = refs[:4], refs[4:]
    width = parts[0].shape[0] - 16
    quarter = width // RING
    gain = halves(joined(total_of([ref[width:, :] for ref in parts])))
    for k in (1, 2, 3, 0):
        rows = pl.ds(pl.multiple_of((place_ref[3] + k) % RING * quarter, quarter), quarter)
        outs[k][:quarter, :] = total_of([ref[rows, :] for ref in parts]).astype(bf16)
        outs[k][quarter:, :] = gain


def first_sum(place, parts):
    width = parts[0].shape[0] - 16
    vmem = pl.BlockSpec(memory_space=pltpu.VMEM)
    return pl.pallas_call(
        first_sum_kernel,
        out_shape=[jax.ShapeDtypeStruct((width // RING + 16, 512), bf16)] * RING,
        in_specs=[pl.BlockSpec(memory_space=pltpu.SMEM)] + [vmem] * 4,
        out_specs=[vmem] * RING,
        compiler_params=pltpu.CompilerParams(vmem_limit_bytes=VMEM_GRANT),
        name="first_sum",
    )(place, *parts)


def second_sum_kernel(*refs):
    parts, outs = refs[:4], refs[4:]
    quarter = parts[0].shape[0] - 16
    gain = joined(total_of([ref[quarter:, :] for ref in parts]))
    gain = halves(
        jnp.concatenate([gain[:, k * LANES : (k + 1) * LANES] for k in range(RING)])
    )
    for k in range(RING):
        start = (RING - k) % RING * LANES
        columns = slice(start, start + LANES)
        outs[k][:quarter, :] = total_of([ref[:quarter, columns] for ref in parts]).astype(bf16)
        outs[k][quarter:, :] = gain


def second_sum(parts):
    quarter = parts[0].shape[0] - 16
    vmem = pl.BlockSpec(memory_space=pltpu.VMEM)
    return pl.pallas_call(
        second_sum_kernel,
        out_shape=[jax.ShapeDtypeStruct((quarter + 64, LANES), bf16)] * RING,
        in_specs=[vmem] * 4,
        out_specs=[vmem] * RING,
        compiler_params=pltpu.CompilerParams(vmem_limit_bytes=VMEM_GRANT),
        name="second_sum",
    )(*parts)


def last_sum_kernel(*refs):
    parts, part_ref, gain_ref = refs[:4], refs[4], refs[5]
    quarter = part_ref.shape[0]
    total = total_of([ref[...] for ref in parts])
    part_ref[...] = total[:quarter, :].astype(bf16)
    gain_ref[...] = joined(total[quarter:, :])


def last_sum(parts):
    quarter = parts[0].shape[0] - 64
    vmem = pl.BlockSpec(memory_space=pltpu.VMEM)
    return pl.pallas_call(
        last_sum_kernel,
        out_shape=[
            jax.ShapeDtypeStruct((quarter, LANES), bf16),
            jax.ShapeDtypeStruct((32, LANES), f32),
        ],
        in_specs=[vmem] * 4,
        out_specs=[vmem] * 2,
        name="last_sum",
    )(*parts)


def finish_kernel(place_ref, *refs):
    parts, out_ref = refs[:4], refs[5]
    quarter = parts[0].shape[0]
    for k in range(RING):
        start = pl.multiple_of((place_ref[3] - k + RING) % RING * quarter, quarter)
        out_ref[:, pl.ds(start, quarter)] = parts[k][...].astype(f32).T


def finish_call(place, parts, after):
    quarter = parts[0].shape[0]
    vmem = pl.BlockSpec(memory_space=pltpu.VMEM)
    return pl.pallas_call(
        finish_kernel,
        out_shape=jax.ShapeDtypeStruct((LANES, RING * quarter), f32),
        in_specs=[pl.BlockSpec(memory_space=pltpu.SMEM)]
        + [vmem] * 4
        + [pl.BlockSpec(memory_space=pl.ANY)],
        out_specs=vmem,
        name="d_proj_rows",
    )(place, *parts, after)


def stream_ring(values):
    count = lax.axis_size("dp")
    return [values[0]] + [
        lax.ppermute(values[k], "dp", [(i, (i + k) % count) for i in range(count)])
        for k in range(1, RING)
    ]


def on_device(
    byte_keys, byte_values, doc_ids, queries, patch_end, cotangent, proj_weight, norm_gain
):
    own, width = byte_keys.shape[1:]
    patches = queries.shape[1]
    seq_count = lax.axis_size("seq")
    seq_rank = lax.axis_index("seq")
    upward = [(i, i + 1) for i in range(seq_count - 1)]
    downward = [(i + 1, i) for i in range(seq_count - 1)]
    keys, values, docs = byte_keys[0], byte_values[0], doc_ids[0]
    place = jnp.stack([seq_rank // (2 * RING), seq_rank // 2 % RING, seq_rank % 2, lax.axis_index("dp")])

    low_docs = lax.ppermute(docs[own - LOW :], "seq", upward)
    high_docs = lax.ppermute(docs[:HIGH], "seq", downward)
    low = jnp.concatenate([keys[own - LOW :], values[own - LOW :]])
    high = jnp.concatenate([keys[:HIGH], values[:HIGH]])
    low, high = lax.ppermute(low, "seq", upward), lax.ppermute(high, "seq", downward)
    weights = lax.all_gather(proj_weight, "seq", axis=0, tiled=True)

    ext_docs = jnp.concatenate([low_docs, docs, high_docs])
    ends = patch_end[0] - (seq_rank * own - LOW)
    position = jnp.arange(ext_docs.shape[0], dtype=jnp.int32)
    last_doc = jnp.sum(
        jnp.where(position[None, :] == ends[:, None] - 1, ext_docs[None, :], 0), axis=1
    )
    earlier = (ext_docs[None, :] < last_doc[:, None]) & (position[None, :] < ends[:, None])
    doc_start = jnp.sum(earlier.astype(jnp.int32), axis=1)
    first = jnp.maximum(jnp.maximum(ends - WIN, doc_start), jnp.where(seq_rank == 0, LOW, 0))
    groups = patches // PG
    marks = jnp.stack([first, ends]).reshape(2, groups, PG).transpose(1, 0, 2)
    marks = jnp.pad(jnp.tile(marks, (1, 1, PAIR)), ((0, 0), (0, 6), (0, 0)))
    marks = marks.reshape(groups * 8, PAIR * PG)
    offsets = (ends[::PG] - WIN) // 16 * 16
    short = (ends[PG - 1 :: PG] <= offsets + SHORT).astype(jnp.int32)

    common = (offsets, short, marks, low, high, keys, values, queries[0])
    attended, level = forward_call(common)
    peer_attended = to_peer(attended)

    mine, other, gain = latent_call(place, attended, norm_gain[None], cotangent[0], weights)
    peer_mine = to_peer(other)
    gain = gain.reshape(RING, 8, 8, LANES)[:, :, 0].transpose(1, 0, 2).reshape(8, 512)
    gain = gain + to_peer(gain)
    d_attended = d_attended_call(place, mine, other, weights)
    to_send = d_proj_call(mine, peer_mine, attended, peer_attended, halves(gain), d_attended)
    from_ring = ring(to_send, "first")

    inputs = common + (attended, level, d_attended)
    d_query, d_keys, d_values, d_low, d_high = backward_call(inputs, to_send[0])
    from_ring, d_query = lax.optimization_barrier((from_ring, d_query))
    to_send, d_low, d_high = lax.optimization_barrier((first_sum(place, from_ring), d_low, d_high))
    from_streams = stream_ring(to_send)
    from_above = lax.ppermute(d_low, "seq", downward)
    from_below = lax.ppermute(d_high, "seq", upward)
    part, gain = last_sum(ring(second_sum(from_streams), "second"))
    d_keys, d_values = rim_call(d_keys, d_values, from_below, from_above)
    d_proj = finish_call(place, stream_ring([part] * RING), d_keys)
    d_gain = gain.reshape(-1)
    return (d_query[None], d_keys[None], d_values[None], d_proj, d_gain)


def solution(mesh):
    in_specs = (
        P("dp", "seq", None),
        P("dp", "seq", None),
        P("dp", "seq"),
        P("dp", "seq", None),
        P("dp", "seq"),
        P("dp", "seq", None),
        P("seq", None),
        P(),
    )
    out_specs = (
        P("dp", "seq", None),
        P("dp", "seq", None),
        P("dp", "seq", None),
        P("seq", None),
        P(),
    )
    return jax.shard_map(
        on_device, mesh=mesh, in_specs=in_specs, out_specs=out_specs, check_vma=False
    )
```

```python
import functools
import math

import jax
import jax.numpy as jnp
from jax import lax
from jax.experimental import pallas as pl
from jax.experimental.pallas import tpu as pltpu
from jax.sharding import PartitionSpec as P

HEADS = 8
HD = 128
WIN = 128
LOW = 384
HIGH = 256
PG = 64
SLAB = 592
SHORT = 448
PAD = 400
PAIR = 2
RING = 4
LANES = 128

masked_score = -1e30
epsilon = 1e-05
score_scale = 1.0 / math.sqrt(HD)
bf16, f32 = jnp.bfloat16, jnp.float32
MIB = 1024 * 1024
VMEM_GRANT = 60 * MIB


def dot(a, b):
    return jnp.dot(a, b, preferred_element_type=f32)


def dot_rows(a, b):
    return lax.dot_general(a, b, (((1,), (1,)), ((), ())), preferred_element_type=f32)


def dot_columns(a, b):
    return lax.dot_general(a, b, (((0,), (0,)), ((), ())), preferred_element_type=f32)


def of_pair(pair):
    return slice(pair * PAIR * HD, (pair + 1) * PAIR * HD)


def spread(block):
    column = lax.broadcasted_iota(jnp.int32, block.shape, 1)
    zero = jnp.zeros_like(block)
    return jnp.concatenate(
        [jnp.where(column // HD == head, block, zero) for head in range(PAIR)]
    )


def gathered_heads(block):
    rows = block.shape[0] // PAIR
    return jnp.concatenate(
        [block[h * rows : (h + 1) * rows, h * HD : (h + 1) * HD] for h in range(PAIR)], axis=1
    )


def fetch_bytes(low_ref, high_ref, keys_ref, values_ref, key_ext, value_ext, sems):
    own = keys_ref.shape[0]
    copies = []
    for which, (own_ref, ext) in enumerate(((keys_ref, key_ext), (values_ref, value_ext))):
        parts = [
            (low_ref.at[pl.ds(which * LOW, LOW)], pl.ds(0, LOW)),
            (high_ref.at[pl.ds(which * HIGH, HIGH)], pl.ds(LOW + own, HIGH)),
        ]
        parts += [
            (own_ref.at[pl.ds(start, 256)], pl.ds(LOW + start, 256))
            for start in range(0, own, 256)
        ]
        for source, rows in parts:
            copies.append(
                pltpu.make_async_copy(source, ext.at[rows], sems.at[len(copies)])
            )
    return copies


def load_bytes(low_ref, high_ref, keys_ref, values_ref, key_ext, value_ext, sems, totals):
    copies = fetch_bytes(low_ref, high_ref, keys_ref, values_ref, key_ext, value_ext, sems)
    for copy in copies:
        copy.start()
    rows = key_ext.shape[0] - PAD
    for ext in (key_ext, value_ext):
        ext[rows:, :] = jnp.zeros((PAD, ext.shape[1]), bf16)
    for total in totals:
        total[...] = jnp.zeros_like(total)
    for copy in copies:
        copy.wait()


def visible_bias(offset, length, span):
    position = offset + lax.broadcasted_iota(jnp.int32, (length, PAIR * PG), 0)
    visible = (position >= span[0:1, :]) & (position < span[1:2, :])
    return jnp.where(visible, 0.0, masked_score)


def each_group(offset_ref, short_ref, groups, one_group):
    step = pl.program_id(0)

    def body(group, carry):
        offset = pl.multiple_of(offset_ref[step * groups + group], 16)
        short = short_ref[step * groups + group]

        @pl.when(short == 1)
        def _():
            one_group(group, offset, SHORT)

        @pl.when(short == 0)
        def _():
            one_group(group, offset, SLAB)

        return carry

    lax.fori_loop(0, groups, body, 0)


def forward_kernel(
    offset_ref, short_ref, span_ref, low_ref, high_ref, keys_ref, values_ref, query_ref,
    attended_ref, level_ref, key_ext, value_ext, sems,
):
    @pl.when(pl.program_id(0) == 0)
    def _():
        load_bytes(low_ref, high_ref, keys_ref, values_ref, key_ext, value_ext, sems, ())

    def one_group(group, offset, length):
        rows = pl.ds(pl.multiple_of(group * PG, PG), PG)
        marks = pl.ds(pl.multiple_of(group * 8, 8), 8)
        slab = pl.ds(offset, length)
        bias = visible_bias(offset, length, span_ref[marks, :])
        pairs = [of_pair(pair) for pair in range(HEADS // PAIR)]
        scores = [dot_rows(key_ext[slab, c], spread(query_ref[rows, c])) for c in pairs]
        scores = [x * score_scale + bias for x in scores]
        top = [jnp.max(x, axis=0, keepdims=True) for x in scores]
        expo = [jnp.exp(x - y) for x, y in zip(scores, top)]
        total = [jnp.sum(x, axis=0, keepdims=True) for x in expo]
        probs = [(x * (1.0 / y)).astype(bf16) for x, y in zip(expo, total)]
        attended = [dot_columns(x, value_ext[slab, c]) for x, c in zip(probs, pairs)]
        for x, c in zip(attended, pairs):
            attended_ref[rows, c] = gathered_heads(x).astype(bf16)
        level = [x + jnp.log(y) for x, y in zip(top, total)]
        level.append(jnp.zeros((8 - len(pairs), PAIR * PG), f32))
        level_ref[marks, :] = jnp.concatenate(level)

    each_group(offset_ref, short_ref, query_ref.shape[0] // PG, one_group)


def backward_kernel(
    offset_ref, short_ref, span_ref, low_ref, high_ref, keys_ref, values_ref, query_ref,
    attended_ref, level_ref, d_attended_ref, after_ref,
    d_query_ref, d_key_ref, d_value_ref, d_low_ref, d_high_ref,
    key_ext, value_ext, sems, d_key, d_value, key_out, value_out, out_sems,
):
    own = keys_ref.shape[0]

    @pl.when(pl.program_id(0) == 0)
    def _():
        load_bytes(
            low_ref, high_ref, keys_ref, values_ref, key_ext, value_ext, sems, (d_key, d_value)
        )

    def one_group(group, offset, length):
        rows = pl.ds(pl.multiple_of(group * PG, PG), PG)
        marks = pl.ds(pl.multiple_of(group * 8, 8), 8)
        slab = pl.ds(offset, length)
        bias = visible_bias(offset, length, span_ref[marks, :])
        levels = level_ref[marks, :]
        for first in range(0, HEADS // PAIR, 2):
            pairs = [of_pair(pair) for pair in range(first, first + 2)]
            query = [spread(query_ref[rows, c]) for c in pairs]
            d_out = [spread(d_attended_ref[rows, c]) for c in pairs]
            scores = [dot_rows(key_ext[slab, c], x) for x, c in zip(query, pairs)]
            d_probs = [dot_rows(value_ext[slab, c], x) for x, c in zip(d_out, pairs)]
            row_dot = []
            for c in pairs:
                both = d_attended_ref[rows, c].astype(f32) * attended_ref[rows, c].astype(f32)
                both = jnp.concatenate([both[:, h * HD : (h + 1) * HD] for h in range(PAIR)])
                row_dot.append(jnp.sum(both.T, axis=0, keepdims=True))
            probs = [
                jnp.exp(x * score_scale + bias - levels[first + i : first + i + 1, :])
                for i, x in enumerate(scores)
            ]
            d_scores = [
                (x * (y - z) * score_scale).astype(bf16)
                for x, y, z in zip(probs, d_probs, row_dot)
            ]
            probs = [x.astype(bf16) for x in probs]
            for c, x in zip(pairs, d_scores):
                d_query = dot_columns(x, key_ext[slab, c])
                d_query_ref[rows, c] = gathered_heads(d_query).astype(bf16)
            for c, x, y in zip(pairs, d_scores, query):
                d_key[slab, c] += dot(x, y)
            for c, x, y in zip(pairs, probs, d_out):
                d_value[slab, c] += dot(x, y)

    each_group(offset_ref, short_ref, query_ref.shape[0] // PG, one_group)

    @pl.when(pl.program_id(0) == pl.num_programs(0) - 1)
    def _():
        copies = []
        sources = ((d_key, key_out, d_key_ref), (d_value, value_out, d_value_ref))
        for which, (total, staged, out_ref) in enumerate(sources):
            parts = [(0, LOW, d_low_ref, which * LOW), (LOW + own, HIGH, d_high_ref, which * HIGH)]
            parts += [(LOW + start, 256, out_ref, start) for start in range(0, own, 256)]
            for start, count, out, place in parts:
                rows = slice(start, start + count)
                staged[rows, :] = total[rows, :].astype(bf16)
                copy = pltpu.make_async_copy(
                    staged.at[pl.ds(start, count)],
                    out.at[pl.ds(place, count)],
                    out_sems.at[len(copies)],
                )
                copy.start()
                copies.append(copy)
        for copy in copies:
            copy.wait()


def forward_call(inputs):
    own, width = inputs[5].shape
    patches = inputs[7].shape[0]
    steps = 4
    ext_rows = LOW + own + HIGH + PAD
    marks = patches // PG * 8
    block = pl.BlockSpec((patches // steps, width), lambda step, *scalars: (step, 0))
    mark_block = pl.BlockSpec((marks // steps, PAIR * PG), lambda step, *scalars: (step, 0))
    return pl.pallas_call(
        forward_kernel,
        out_shape=[
            jax.ShapeDtypeStruct((patches, width), bf16),
            jax.ShapeDtypeStruct((marks, PAIR * PG), f32),
        ],
        grid_spec=pltpu.PrefetchScalarGridSpec(
            num_scalar_prefetch=2,
            grid=(steps,),
            in_specs=[mark_block] + [pl.BlockSpec(memory_space=pl.ANY)] * 4 + [block],
            out_specs=[block, mark_block],
            scratch_shapes=[pltpu.VMEM((ext_rows, width), bf16)] * 2
            + [pltpu.SemaphoreType.DMA((2 * (2 + own // 256),))],
        ),
        compiler_params=pltpu.CompilerParams(vmem_limit_bytes=VMEM_GRANT),
        cost_estimate=pl.CostEstimate(
            flops=4 * HEADS * patches * SLAB * HD,
            bytes_accessed=20 * MIB,
            transcendentals=HEADS * patches * SLAB,
        ),
        name="attention_forward",
    )(*inputs)


def backward_call(inputs, after):
    own, width = inputs[5].shape
    patches = inputs[7].shape[0]
    steps = 4
    ext_rows = LOW + own + HIGH + PAD
    marks = patches // PG * 8
    block = pl.BlockSpec((patches // steps, width), lambda step, *scalars: (step, 0))
    mark_block = pl.BlockSpec((marks // steps, PAIR * PG), lambda step, *scalars: (step, 0))
    anywhere = pl.BlockSpec(memory_space=pl.ANY)
    rows = (patches, own, own, 2 * LOW, 2 * HIGH)
    return pl.pallas_call(
        backward_kernel,
        out_shape=[jax.ShapeDtypeStruct((count, width), bf16) for count in rows],
        grid_spec=pltpu.PrefetchScalarGridSpec(
            num_scalar_prefetch=2,
            grid=(steps,),
            in_specs=[mark_block]
            + [anywhere] * 4
            + [block, block, mark_block, block]
            + [anywhere],
            out_specs=[block] + [anywhere] * 4,
            scratch_shapes=[pltpu.VMEM((ext_rows, width), bf16)] * 2
            + [pltpu.SemaphoreType.DMA((2 * (2 + own // 256),))]
            + [pltpu.VMEM((ext_rows, width), f32)] * 2
            + [pltpu.VMEM((ext_rows - PAD, width), bf16)] * 2
            + [pltpu.SemaphoreType.DMA((2 * (2 + own // 256),))],
        ),
        compiler_params=pltpu.CompilerParams(vmem_limit_bytes=VMEM_GRANT),
        cost_estimate=pl.CostEstimate(
            flops=14 * HEADS * patches * SLAB * HD,
            bytes_accessed=40 * MIB,
            transcendentals=HEADS * patches * SLAB,
        ),
        name="attention_backward",
    )(*inputs, after)


def chip_block(place_ref, chunk):
    side, first, second = chunk // 16, chunk // 4 % 4, chunk % 4
    core = (place_ref[2] + side) % 2
    z = (place_ref[0] - jnp.where(core == 0, first, second) + RING) % RING
    x = (place_ref[1] - jnp.where(core == 0, second, first) + RING) % RING
    return (z * RING + x) * 2 + core


def fetch_weights(place_ref, weights_ref, weight, sems):
    copies = []
    for chunk in range(32):
        start = pl.multiple_of(chip_block(place_ref, chunk) * LANES, LANES)
        copies.append(
            pltpu.make_async_copy(
                weights_ref.at[pl.ds(start, LANES)],
                weight.at[pl.ds(chunk * LANES, LANES)],
                sems.at[chunk],
            )
        )
    return [copies[start : start + 4] for start in range(0, 32, 4)]


def latent_kernel(
    place_ref, attended_ref, norm_ref, cotangent_ref, weights_ref,
    mine_ref, other_ref, gain_ref, d_attended_ref,
    weight, cotangent, latent, square, mixed, mine, other, total, sems,
):
    pieces = fetch_weights(place_ref, weights_ref, weight, sems)
    rows_each = cotangent.shape[0] // 8
    cotangent_copies = [
        pltpu.make_async_copy(
            cotangent_ref.at[pl.ds(part * rows_each, rows_each)],
            cotangent.at[pl.ds(part * rows_each, rows_each)],
            sems.at[32 + part],
        )
        for part in range(8)
    ]
    for slab, copies in enumerate(pieces):
        for copy in copies:
            copy.start()
        if slab == 0:
            for copy in cotangent_copies:
                copy.start()
    square[...] = jnp.zeros_like(square)
    mixed[...] = jnp.zeros_like(mixed)

    def columns_of(chunk):
        return pl.ds(pl.multiple_of(chip_block(place_ref, chunk) * LANES, LANES), LANES)

    def multiply(slab):
        for copy in pieces[slab]:
            copy.wait()
        start = slab * 512
        latent[slab] = dot_rows(attended_ref[...], weight[start : start + 512, :])

    multiply(0)
    for copy in cotangent_copies:
        copy.wait()
    for slab in range(8):
        if slab < 7:
            multiply(slab + 1)
        columns = [columns_of(slab * 4 + part) for part in range(4)]
        scaled = [norm_ref[:, c] for c in columns]
        for start in range(0, square.shape[0], 64):
            rows = slice(start, start + 64)
            here = [latent[slab, rows, p * LANES : (p + 1) * LANES] for p in range(4)]
            arriving = [cotangent[rows, c].astype(f32) * g for c, g in zip(columns, scaled)]
            square[rows, :] += total_of([x * x for x in here])
            mixed[rows, :] += total_of([x * y for x, y in zip(here, arriving)])

    count = cotangent.shape[1]
    inverse = lax.rsqrt(jnp.sum(square[...], axis=1, keepdims=True) / count + epsilon)
    back = inverse * inverse * inverse * (jnp.sum(mixed[...], axis=1, keepdims=True) / count)
    square[...] = jnp.broadcast_to(inverse, square.shape)
    mixed[...] = jnp.broadcast_to(back, mixed.shape)

    def finish(slab, staged, out_ref):
        chunks = [slab * 4 + part for part in range(4)]
        columns = [columns_of(chunk) for chunk in chunks]
        norm = [norm_ref[:, c] for c in columns]
        gain = [jnp.zeros((8, LANES), f32)] * 4
        first = slab % 4 * 512
        for start in range(0, square.shape[0], 64):
            rows = slice(start, start + 64)
            scale, back = square[rows, :], mixed[rows, :]
            for part in range(4):
                here = latent[slab, rows, part * LANES : (part + 1) * LANES]
                scaled = cotangent[rows, columns[part]].astype(f32) * scale
                terms = scaled * here
                terms = [terms[k : k + 8, :] for k in range(0, 64, 8)]
                gain[part] += functools.reduce(jnp.add, terms)
                staged[rows, first + part * LANES : first + (part + 1) * LANES] = (
                    scaled * norm[part] - here * back
                ).astype(bf16)
        for part in range(4):
            spot = pl.ds(pl.multiple_of(chip_block(place_ref, chunks[part]) * 8, 8), 8)
            total = jnp.sum(gain[part], axis=0, keepdims=True)
            gain_ref[spot, :] = jnp.broadcast_to(total, (8, LANES))
        place = pl.ds(first, 512)
        copy = pltpu.make_async_copy(
            staged.at[:, place], out_ref.at[:, place], sems.at[40 + slab]
        )
        copy.start()
        return copy

    copies = []
    for part in range(4):
        staged, out_ref = (mine, mine_ref) if part < 2 else (other, other_ref)
        copies += [finish(slab, staged, out_ref) for slab in (2 * part, 2 * part + 1)]
        columns = slice(part % 2 * 1024, part % 2 * 1024 + 1024)
        terms = dot(staged[:, columns], weight[part * 1024 : part * 1024 + 1024, :])
        if part == 0:
            total[...] = terms
        elif part < 3:
            total[...] += terms
        else:
            d_attended_ref[...] = (total[...] + terms).astype(bf16)
    for copy in copies:
        copy.wait()


def latent_call(place, attended, norm_gain, cotangent, weights):
    patches, count = cotangent.shape
    return pl.pallas_call(
        latent_kernel,
        out_shape=[
            jax.ShapeDtypeStruct((patches, count // 2), bf16),
            jax.ShapeDtypeStruct((patches, count // 2), bf16),
            jax.ShapeDtypeStruct((count // LANES * 8, LANES), f32),
            jax.ShapeDtypeStruct(attended.shape, bf16),
        ],
        in_specs=[pl.BlockSpec(memory_space=pltpu.SMEM)]
        + [pl.BlockSpec(memory_space=pltpu.VMEM)] * 2
        + [pl.BlockSpec(memory_space=pl.ANY)] * 2,
        out_specs=[pl.BlockSpec(memory_space=pl.ANY)] * 2
        + [pl.BlockSpec(memory_space=pltpu.VMEM)] * 2,
        scratch_shapes=[
            pltpu.VMEM(weights.shape, bf16),
            pltpu.VMEM((patches, count), bf16),
            pltpu.VMEM((8, patches, count // 8), f32),
            pltpu.VMEM((patches, LANES), f32),
            pltpu.VMEM((patches, LANES), f32),
            pltpu.VMEM((patches, count // 2), bf16),
            pltpu.VMEM((patches, count // 2), bf16),
            pltpu.VMEM(attended.shape, f32),
            pltpu.SemaphoreType.DMA((48,)),
        ],
        compiler_params=pltpu.CompilerParams(vmem_limit_bytes=VMEM_GRANT),
        cost_estimate=pl.CostEstimate(
            flops=4 * patches * count * 1024, bytes_accessed=18 * MIB, transcendentals=patches
        ),
        name="latent",
    )(place, attended, norm_gain, cotangent, weights)


def d_proj_kernel(
    mine_ref, peer_ref, attended_ref, peer_attended_ref, gain_ref, *refs
):
    outs, (d_latent, rows, turned, staged, sems) = refs[:4], refs[4:]
    patches, width = attended_ref.shape
    arriving, leaving, sides = [], [], []
    for side, source in enumerate((attended_ref, peer_attended_ref)):
        sides.append(pltpu.make_async_copy(source, rows.at[side], sems.at[12 + side]))
        sides[-1].start()
    for k in (1, 2, 3, 0):
        columns = pl.ds((RING - k) % RING * 512, 512)
        for side, source in enumerate((mine_ref, peer_ref)):
            arriving.append(
                pltpu.make_async_copy(
                    source.at[:, columns],
                    d_latent.at[k, pl.ds(side * patches, patches)],
                    sems.at[2 * k + side],
                )
            )
            arriving[-1].start()
    for side in range(2):
        sides[side].wait()
        turned[:, side * patches : (side + 1) * patches] = rows[side].T
    for step, k in enumerate((1, 2, 3, 0)):
        arriving[2 * step].wait()
        arriving[2 * step + 1].wait()
        staged[k, :width, :] = dot(turned[...], d_latent[k]).astype(bf16)
        staged[k, width:, :] = gain_ref[...]
        leaving.append(pltpu.make_async_copy(staged.at[k], outs[k], sems.at[8 + k]))
        leaving[-1].start()
    for copy in leaving:
        copy.wait()


def d_proj_call(mine, peer, attended, peer_attended, gain):
    patches, width = attended.shape
    vmem, anywhere = pl.BlockSpec(memory_space=pltpu.VMEM), pl.BlockSpec(memory_space=pl.ANY)
    return pl.pallas_call(
        d_proj_kernel,
        out_shape=[jax.ShapeDtypeStruct((width + 16, 512), bf16)] * 4,
        in_specs=[anywhere] * 4 + [vmem],
        out_specs=[anywhere] * 4,
        scratch_shapes=[
            pltpu.VMEM((4, 2 * patches, 512), bf16),
            pltpu.VMEM((2, patches, width), bf16),
            pltpu.VMEM((width, 2 * patches), bf16),
            pltpu.VMEM((4, width + 16, 512), bf16),
            pltpu.SemaphoreType.DMA((14,)),
        ],
        compiler_params=pltpu.CompilerParams(vmem_limit_bytes=VMEM_GRANT),
        cost_estimate=pl.CostEstimate(
            flops=4 * patches * mine.shape[1] * width, bytes_accessed=12 * MIB, transcendentals=0
        ),
        name="d_proj",
    )(mine, peer, attended, peer_attended, gain)


def rim_kernel(
    key_in, value_in, below_ref, above_ref, key_out, value_out, rims, arriving, sems
):
    own = key_in.shape[0]
    places = ((pl.ds(0, HIGH), pl.ds(0, HIGH)), (pl.ds(own - LOW, LOW), pl.ds(HIGH, LOW)))
    steps = []
    for which, (source, out) in enumerate(((key_in, key_out), (value_in, value_out))):
        for side, (far, near) in enumerate(places):
            count = (HIGH, LOW)[side]
            from_ref = (below_ref, above_ref)[side].at[pl.ds(which * count, count)]
            rim, other = rims.at[which, near], arriving.at[which, near]
            sem = 3 * (2 * which + side)
            inward = [
                pltpu.make_async_copy(source.at[far], rim, sems.at[sem]),
                pltpu.make_async_copy(from_ref, other, sems.at[sem + 1]),
            ]
            outward = pltpu.make_async_copy(rim, out.at[far], sems.at[sem + 2])
            for copy in inward:
                copy.start()
            steps.append((rim, other, inward, outward))
    for rim, other, inward, outward in steps:
        for copy in inward:
            copy.wait()
        rim[...] = (rim[...].astype(f32) + other[...].astype(f32)).astype(bf16)
        outward.start()
    for *_, outward in steps:
        outward.wait()


def rim_call(d_key, d_value, from_below, from_above):
    width = from_below.shape[1]
    anywhere = pl.BlockSpec(memory_space=pl.ANY)
    return pl.pallas_call(
        rim_kernel,
        out_shape=[jax.ShapeDtypeStruct(d_key.shape, bf16)] * 2,
        in_specs=[anywhere] * 4,
        out_specs=[anywhere] * 2,
        scratch_shapes=[pltpu.VMEM((2, HIGH + LOW, width), bf16)] * 2
        + [pltpu.SemaphoreType.DMA((12,))],
        input_output_aliases={0: 0, 1: 1},
        compiler_params=pltpu.CompilerParams(vmem_limit_bytes=VMEM_GRANT),
        name="rims",
    )(d_key, d_value, from_below, from_above)


def along(which, distance):
    pairs = []
    for z in range(RING):
        for x in range(RING):
            for core in range(2):
                on_z = (which == "first") == (core == 0)
                to_z = (z + distance) % RING if on_z else z
                to_x = x if on_z else (x + distance) % RING
                pairs.append(((z * RING + x) * 2 + core, (to_z * RING + to_x) * 2 + core))
    return pairs


def to_peer(value):
    return lax.ppermute(value, "seq", [(i, i ^ 1) for i in range(lax.axis_size("seq"))])


def ring(values, which):
    return [values[0]] + [
        lax.ppermute(values[k], "seq", along(which, k)) for k in range(1, RING)
    ]


def total_of(parts):
    parts = [part.astype(f32) for part in parts]
    return (parts[0] + parts[2]) + (parts[1] + parts[3])


def halves(value):
    upper = value.astype(bf16)
    lower = (value - upper.astype(f32)).astype(bf16)
    return jnp.concatenate([upper, lower])


def joined(value):
    rows = value.shape[0] // 2
    return value[:rows] + value[rows:]


def first_sum_kernel(place_ref, *refs):
    parts, outs = refs[:4], refs[4:]
    width = parts[0].shape[0] - 16
    quarter = width // RING
    gain = halves(joined(total_of([ref[width:, :] for ref in parts])))
    for k in (1, 2, 3, 0):
        rows = pl.ds(pl.multiple_of((place_ref[3] + k) % RING * quarter, quarter), quarter)
        outs[k][:quarter, :] = total_of([ref[rows, :] for ref in parts]).astype(bf16)
        outs[k][quarter:, :] = gain


def first_sum(place, parts):
    width = parts[0].shape[0] - 16
    vmem = pl.BlockSpec(memory_space=pltpu.VMEM)
    return pl.pallas_call(
        first_sum_kernel,
        out_shape=[jax.ShapeDtypeStruct((width // RING + 16, 512), bf16)] * RING,
        in_specs=[pl.BlockSpec(memory_space=pltpu.SMEM)] + [vmem] * 4,
        out_specs=[vmem] * RING,
        compiler_params=pltpu.CompilerParams(vmem_limit_bytes=VMEM_GRANT),
        name="first_sum",
    )(place, *parts)


def second_sum_kernel(*refs):
    parts, outs = refs[:4], refs[4:]
    quarter = parts[0].shape[0] - 16
    gain = joined(total_of([ref[quarter:, :] for ref in parts]))
    gain = halves(
        jnp.concatenate([gain[:, k * LANES : (k + 1) * LANES] for k in range(RING)])
    )
    for k in range(RING):
        start = (RING - k) % RING * LANES
        columns = slice(start, start + LANES)
        outs[k][:quarter, :] = total_of([ref[:quarter, columns] for ref in parts]).astype(bf16)
        outs[k][quarter:, :] = gain


def second_sum(parts):
    quarter = parts[0].shape[0] - 16
    vmem = pl.BlockSpec(memory_space=pltpu.VMEM)
    return pl.pallas_call(
        second_sum_kernel,
        out_shape=[jax.ShapeDtypeStruct((quarter + 64, LANES), bf16)] * RING,
        in_specs=[vmem] * 4,
        out_specs=[vmem] * RING,
        compiler_params=pltpu.CompilerParams(vmem_limit_bytes=VMEM_GRANT),
        name="second_sum",
    )(*parts)


def last_sum_kernel(*refs):
    parts, part_ref, gain_ref = refs[:4], refs[5], refs[6]
    quarter = part_ref.shape[0]
    total = total_of([ref[...] for ref in parts])
    part_ref[...] = total[:quarter, :].astype(bf16)
    gain_ref[...] = joined(total[quarter:, :])


def last_sum(parts, after):
    quarter = parts[0].shape[0] - 64
    vmem = pl.BlockSpec(memory_space=pltpu.VMEM)
    return pl.pallas_call(
        last_sum_kernel,
        out_shape=[
            jax.ShapeDtypeStruct((quarter, LANES), bf16),
            jax.ShapeDtypeStruct((32, LANES), f32),
        ],
        in_specs=[vmem] * 4 + [pl.BlockSpec(memory_space=pl.ANY)],
        out_specs=[vmem] * 2,
        name="last_sum",
    )(*parts, after)


def finish_kernel(place_ref, *refs):
    parts, out_ref = refs[:4], refs[4]
    quarter = parts[0].shape[0]
    for k in range(RING):
        start = pl.multiple_of((place_ref[3] - k + RING) % RING * quarter, quarter)
        out_ref[:, pl.ds(start, quarter)] = parts[k][...].astype(f32).T


def finish_call(place, parts):
    quarter = parts[0].shape[0]
    vmem = pl.BlockSpec(memory_space=pltpu.VMEM)
    return pl.pallas_call(
        finish_kernel,
        out_shape=jax.ShapeDtypeStruct((LANES, RING * quarter), f32),
        in_specs=[pl.BlockSpec(memory_space=pltpu.SMEM)]
        + [vmem] * 4,
        out_specs=vmem,
        name="d_proj_rows",
    )(place, *parts)


def stream_ring(values):
    count = lax.axis_size("dp")
    return [values[0]] + [
        lax.ppermute(values[k], "dp", [(i, (i + k) % count) for i in range(count)])
        for k in range(1, RING)
    ]


def on_device(
    byte_keys, byte_values, doc_ids, queries, patch_end, cotangent, proj_weight, norm_gain
):
    own, width = byte_keys.shape[1:]
    patches = queries.shape[1]
    seq_count = lax.axis_size("seq")
    seq_rank = lax.axis_index("seq")
    upward = [(i, i + 1) for i in range(seq_count - 1)]
    downward = [(i + 1, i) for i in range(seq_count - 1)]
    keys, values, docs = byte_keys[0], byte_values[0], doc_ids[0]
    place = jnp.stack([seq_rank // (2 * RING), seq_rank // 2 % RING, seq_rank % 2, lax.axis_index("dp")])

    low_docs = lax.ppermute(docs[own - LOW :], "seq", upward)
    high_docs = lax.ppermute(docs[:HIGH], "seq", downward)
    low = jnp.concatenate([keys[own - LOW :], values[own - LOW :]])
    high = jnp.concatenate([keys[:HIGH], values[:HIGH]])
    low, high = lax.ppermute(low, "seq", upward), lax.ppermute(high, "seq", downward)
    weights = lax.all_gather(proj_weight, "seq", axis=0, tiled=True)

    ext_docs = jnp.concatenate([low_docs, docs, high_docs])
    ends = patch_end[0] - (seq_rank * own - LOW)
    position = jnp.arange(ext_docs.shape[0], dtype=jnp.int32)
    last_doc = jnp.sum(
        jnp.where(position[None, :] == ends[:, None] - 1, ext_docs[None, :], 0), axis=1
    )
    earlier = (ext_docs[None, :] < last_doc[:, None]) & (position[None, :] < ends[:, None])
    doc_start = jnp.sum(earlier.astype(jnp.int32), axis=1)
    first = jnp.maximum(jnp.maximum(ends - WIN, doc_start), jnp.where(seq_rank == 0, LOW, 0))
    groups = patches // PG
    marks = jnp.stack([first, ends]).reshape(2, groups, PG).transpose(1, 0, 2)
    marks = jnp.pad(jnp.tile(marks, (1, 1, PAIR)), ((0, 0), (0, 6), (0, 0)))
    marks = marks.reshape(groups * 8, PAIR * PG)
    offsets = (ends[::PG] - WIN) // 16 * 16
    short = (ends[PG - 1 :: PG] <= offsets + SHORT).astype(jnp.int32)

    common = (offsets, short, marks, low, high, keys, values, queries[0])
    attended, level = forward_call(common)
    peer_attended = to_peer(attended)

    mine, other, gain, d_attended = latent_call(place, attended, norm_gain[None], cotangent[0], weights)
    peer_mine = to_peer(other)
    gain = gain.reshape(RING, 8, 8, LANES)[:, :, 0].transpose(1, 0, 2).reshape(8, 512)
    gain = gain + to_peer(gain)
    to_send = d_proj_call(mine, peer_mine, attended, peer_attended, halves(gain))
    from_ring = ring(to_send, "first")

    inputs = common + (attended, level, d_attended)
    d_query, d_keys, d_values, d_low, d_high = backward_call(inputs, to_send[0])
    from_ring, d_query = lax.optimization_barrier((from_ring, d_query))
    to_send, d_low, d_high = lax.optimization_barrier((first_sum(place, from_ring), d_low, d_high))
    from_streams = stream_ring(to_send)
    from_above = lax.ppermute(d_low, "seq", downward)
    from_below = lax.ppermute(d_high, "seq", upward)
    from_ring = ring(second_sum(from_streams), "second")
    d_keys, d_values = rim_call(d_keys, d_values, from_below, from_above)
    part, gain = last_sum(from_ring, d_keys)
    d_proj = finish_call(place, stream_ring([part] * RING))
    d_gain = gain.reshape(-1)
    return (d_query[None], d_keys[None], d_values[None], d_proj, d_gain)


def solution(mesh):
    in_specs = (
        P("dp", "seq", None),
        P("dp", "seq", None),
        P("dp", "seq"),
        P("dp", "seq", None),
        P("dp", "seq"),
        P("dp", "seq", None),
        P("seq", None),
        P(),
    )
    out_specs = (
        P("dp", "seq", None),
        P("dp", "seq", None),
        P("dp", "seq", None),
        P("seq", None),
        P(),
    )
    return jax.shard_map(
        on_device, mesh=mesh, in_specs=in_specs, out_specs=out_specs, check_vma=False
    )
```

```python
import functools
import math

import jax
import jax.numpy as jnp
from jax import lax
from jax.experimental import pallas as pl
from jax.experimental.pallas import tpu as pltpu
from jax.sharding import PartitionSpec as P

HEADS = 8
HD = 128
WIN = 128
LOW = 384
HIGH = 256
PG = 64
SLAB = 592
SHORT = 448
PAD = 400
PAIR = 2
RING = 4
LANES = 128

masked_score = -1e30
epsilon = 1e-05
score_scale = 1.0 / math.sqrt(HD)
bf16, f32 = jnp.bfloat16, jnp.float32
MIB = 1024 * 1024
VMEM_GRANT = 60 * MIB


def dot(a, b):
    return jnp.dot(a, b, preferred_element_type=f32)


def dot_rows(a, b):
    return lax.dot_general(a, b, (((1,), (1,)), ((), ())), preferred_element_type=f32)


def dot_columns(a, b):
    return lax.dot_general(a, b, (((0,), (0,)), ((), ())), preferred_element_type=f32)


def of_pair(pair):
    return slice(pair * PAIR * HD, (pair + 1) * PAIR * HD)


def spread(block):
    column = lax.broadcasted_iota(jnp.int32, block.shape, 1)
    zero = jnp.zeros_like(block)
    return jnp.concatenate(
        [jnp.where(column // HD == head, block, zero) for head in range(PAIR)]
    )


def gathered_heads(block):
    rows = block.shape[0] // PAIR
    return jnp.concatenate(
        [block[h * rows : (h + 1) * rows, h * HD : (h + 1) * HD] for h in range(PAIR)], axis=1
    )


def fetch_bytes(low_ref, high_ref, keys_ref, values_ref, key_ext, value_ext, sems):
    own = keys_ref.shape[0]
    copies = []
    for which, (own_ref, ext) in enumerate(((keys_ref, key_ext), (values_ref, value_ext))):
        parts = [
            (low_ref.at[pl.ds(which * LOW, LOW)], pl.ds(0, LOW)),
            (high_ref.at[pl.ds(which * HIGH, HIGH)], pl.ds(LOW + own, HIGH)),
        ]
        parts += [
            (own_ref.at[pl.ds(start, 256)], pl.ds(LOW + start, 256))
            for start in range(0, own, 256)
        ]
        for source, rows in parts:
            copies.append(
                pltpu.make_async_copy(source, ext.at[rows], sems.at[len(copies)])
            )
    return copies


def load_bytes(low_ref, high_ref, keys_ref, values_ref, key_ext, value_ext, sems, totals):
    copies = fetch_bytes(low_ref, high_ref, keys_ref, values_ref, key_ext, value_ext, sems)
    for copy in copies:
        copy.start()
    rows = key_ext.shape[0] - PAD
    for ext in (key_ext, value_ext):
        ext[rows:, :] = jnp.zeros((PAD, ext.shape[1]), bf16)
    for total in totals:
        total[...] = jnp.zeros_like(total)
    for copy in copies:
        copy.wait()


def visible_bias(offset, length, span):
    position = offset + lax.broadcasted_iota(jnp.int32, (length, PAIR * PG), 0)
    visible = (position >= span[0:1, :]) & (position < span[1:2, :])
    return jnp.where(visible, 0.0, masked_score)


def each_group(offset_ref, short_ref, groups, one_group):
    step = pl.program_id(0)

    def body(group, carry):
        offset = pl.multiple_of(offset_ref[step * groups + group], 16)
        short = short_ref[step * groups + group]

        @pl.when(short == 1)
        def _():
            one_group(group, offset, SHORT)

        @pl.when(short == 0)
        def _():
            one_group(group, offset, SLAB)

        return carry

    lax.fori_loop(0, groups, body, 0)


def forward_kernel(
    offset_ref, short_ref, span_ref, low_ref, high_ref, keys_ref, values_ref, query_ref,
    attended_ref, level_ref, key_ext, value_ext, sems,
):
    @pl.when(pl.program_id(0) == 0)
    def _():
        load_bytes(low_ref, high_ref, keys_ref, values_ref, key_ext, value_ext, sems, ())

    def one_group(group, offset, length):
        rows = pl.ds(pl.multiple_of(group * PG, PG), PG)
        marks = pl.ds(pl.multiple_of(group * 8, 8), 8)
        slab = pl.ds(offset, length)
        bias = visible_bias(offset, length, span_ref[marks, :])
        pairs = [of_pair(pair) for pair in range(HEADS // PAIR)]
        scores = [dot_rows(key_ext[slab, c], spread(query_ref[rows, c])) for c in pairs]
        scores = [x * score_scale + bias for x in scores]
        top = [jnp.max(x, axis=0, keepdims=True) for x in scores]
        expo = [jnp.exp(x - y) for x, y in zip(scores, top)]
        total = [jnp.sum(x, axis=0, keepdims=True) for x in expo]
        probs = [(x * (1.0 / y)).astype(bf16) for x, y in zip(expo, total)]
        attended = [dot_columns(x, value_ext[slab, c]) for x, c in zip(probs, pairs)]
        for x, c in zip(attended, pairs):
            attended_ref[rows, c] = gathered_heads(x).astype(bf16)
        level = [x + jnp.log(y) for x, y in zip(top, total)]
        level.append(jnp.zeros((8 - len(pairs), PAIR * PG), f32))
        level_ref[marks, :] = jnp.concatenate(level)

    each_group(offset_ref, short_ref, query_ref.shape[0] // PG, one_group)


def backward_kernel(
    offset_ref, short_ref, span_ref, low_ref, high_ref, keys_ref, values_ref, query_ref,
    attended_ref, level_ref, d_attended_ref, after_ref,
    d_query_ref, d_key_ref, d_value_ref, d_low_ref, d_high_ref,
    key_ext, value_ext, sems, d_key, d_value, key_out, value_out, out_sems,
):
    own = keys_ref.shape[0]

    @pl.when(pl.program_id(0) == 0)
    def _():
        load_bytes(
            low_ref, high_ref, keys_ref, values_ref, key_ext, value_ext, sems, (d_key, d_value)
        )

    def one_group(group, offset, length):
        rows = pl.ds(pl.multiple_of(group * PG, PG), PG)
        marks = pl.ds(pl.multiple_of(group * 8, 8), 8)
        slab = pl.ds(offset, length)
        bias = visible_bias(offset, length, span_ref[marks, :])
        levels = level_ref[marks, :]
        for first in range(0, HEADS // PAIR, 2):
            pairs = [of_pair(pair) for pair in range(first, first + 2)]
            query = [spread(query_ref[rows, c]) for c in pairs]
            d_out = [spread(d_attended_ref[rows, c]) for c in pairs]
            scores = [dot_rows(key_ext[slab, c], x) for x, c in zip(query, pairs)]
            d_probs = [dot_rows(value_ext[slab, c], x) for x, c in zip(d_out, pairs)]
            row_dot = []
            for c in pairs:
                both = d_attended_ref[rows, c].astype(f32) * attended_ref[rows, c].astype(f32)
                both = jnp.concatenate([both[:, h * HD : (h + 1) * HD] for h in range(PAIR)])
                row_dot.append(jnp.sum(both.T, axis=0, keepdims=True))
            probs = [
                jnp.exp(x * score_scale + bias - levels[first + i : first + i + 1, :])
                for i, x in enumerate(scores)
            ]
            d_scores = [
                (x * (y - z) * score_scale).astype(bf16)
                for x, y, z in zip(probs, d_probs, row_dot)
            ]
            probs = [x.astype(bf16) for x in probs]
            for c, x in zip(pairs, d_scores):
                d_query = dot_columns(x, key_ext[slab, c])
                d_query_ref[rows, c] = gathered_heads(d_query).astype(bf16)
            for c, x, y in zip(pairs, d_scores, query):
                d_key[slab, c] += dot(x, y)
            for c, x, y in zip(pairs, probs, d_out):
                d_value[slab, c] += dot(x, y)

    each_group(offset_ref, short_ref, query_ref.shape[0] // PG, one_group)

    @pl.when(pl.program_id(0) == pl.num_programs(0) - 1)
    def _():
        copies = []
        sources = ((d_key, key_out, d_key_ref), (d_value, value_out, d_value_ref))
        for which, (total, staged, out_ref) in enumerate(sources):
            parts = [(0, LOW, d_low_ref, which * LOW), (LOW + own, HIGH, d_high_ref, which * HIGH)]
            parts += [(LOW + start, 256, out_ref, start) for start in range(0, own, 256)]
            for start, count, out, place in parts:
                rows = slice(start, start + count)
                staged[rows, :] = total[rows, :].astype(bf16)
                copy = pltpu.make_async_copy(
                    staged.at[pl.ds(start, count)],
                    out.at[pl.ds(place, count)],
                    out_sems.at[len(copies)],
                )
                copy.start()
                copies.append(copy)
        for copy in copies:
            copy.wait()


def forward_call(inputs):
    own, width = inputs[5].shape
    patches = inputs[7].shape[0]
    steps = 4
    ext_rows = LOW + own + HIGH + PAD
    marks = patches // PG * 8
    block = pl.BlockSpec((patches // steps, width), lambda step, *scalars: (step, 0))
    mark_block = pl.BlockSpec((marks // steps, PAIR * PG), lambda step, *scalars: (step, 0))
    return pl.pallas_call(
        forward_kernel,
        out_shape=[
            jax.ShapeDtypeStruct((patches, width), bf16),
            jax.ShapeDtypeStruct((marks, PAIR * PG), f32),
        ],
        grid_spec=pltpu.PrefetchScalarGridSpec(
            num_scalar_prefetch=2,
            grid=(steps,),
            in_specs=[mark_block] + [pl.BlockSpec(memory_space=pl.ANY)] * 4 + [block],
            out_specs=[block, mark_block],
            scratch_shapes=[pltpu.VMEM((ext_rows, width), bf16)] * 2
            + [pltpu.SemaphoreType.DMA((2 * (2 + own // 256),))],
        ),
        compiler_params=pltpu.CompilerParams(vmem_limit_bytes=VMEM_GRANT),
        cost_estimate=pl.CostEstimate(
            flops=4 * HEADS * patches * SLAB * HD,
            bytes_accessed=20 * MIB,
            transcendentals=HEADS * patches * SLAB,
        ),
        name="attention_forward",
    )(*inputs)


def backward_call(inputs, after):
    own, width = inputs[5].shape
    patches = inputs[7].shape[0]
    steps = 4
    ext_rows = LOW + own + HIGH + PAD
    marks = patches // PG * 8
    block = pl.BlockSpec((patches // steps, width), lambda step, *scalars: (step, 0))
    mark_block = pl.BlockSpec((marks // steps, PAIR * PG), lambda step, *scalars: (step, 0))
    anywhere = pl.BlockSpec(memory_space=pl.ANY)
    rows = (patches, own, own, 2 * LOW, 2 * HIGH)
    return pl.pallas_call(
        backward_kernel,
        out_shape=[jax.ShapeDtypeStruct((count, width), bf16) for count in rows],
        grid_spec=pltpu.PrefetchScalarGridSpec(
            num_scalar_prefetch=2,
            grid=(steps,),
            in_specs=[mark_block]
            + [anywhere] * 4
            + [block, block, mark_block, block]
            + [anywhere],
            out_specs=[block] + [anywhere] * 4,
            scratch_shapes=[pltpu.VMEM((ext_rows, width), bf16)] * 2
            + [pltpu.SemaphoreType.DMA((2 * (2 + own // 256),))]
            + [pltpu.VMEM((ext_rows, width), f32)] * 2
            + [pltpu.VMEM((ext_rows - PAD, width), bf16)] * 2
            + [pltpu.SemaphoreType.DMA((2 * (2 + own // 256),))],
        ),
        compiler_params=pltpu.CompilerParams(vmem_limit_bytes=VMEM_GRANT),
        cost_estimate=pl.CostEstimate(
            flops=14 * HEADS * patches * SLAB * HD,
            bytes_accessed=40 * MIB,
            transcendentals=HEADS * patches * SLAB,
        ),
        name="attention_backward",
    )(*inputs, after)


def chip_block(place_ref, chunk):
    side, first, second = chunk // 16, chunk // 4 % 4, chunk % 4
    core = (place_ref[2] + side) % 2
    z = (place_ref[0] - jnp.where(core == 0, first, second) + RING) % RING
    x = (place_ref[1] - jnp.where(core == 0, second, first) + RING) % RING
    return (z * RING + x) * 2 + core


def fetch_weights(place_ref, weights_ref, weight, sems):
    copies = []
    for chunk in range(32):
        start = pl.multiple_of(chip_block(place_ref, chunk) * LANES, LANES)
        copies.append(
            pltpu.make_async_copy(
                weights_ref.at[pl.ds(start, LANES)],
                weight.at[pl.ds(chunk * LANES, LANES)],
                sems.at[chunk],
            )
        )
    return [copies[start : start + 4] for start in range(0, 32, 4)]


def latent_kernel(
    place_ref, attended_ref, norm_ref, cotangent_ref, weights_ref,
    mine_ref, other_ref, gain_ref, d_attended_ref,
    weight, cotangent, latent, square, mixed, mine, other, total, sems,
):
    pieces = fetch_weights(place_ref, weights_ref, weight, sems)
    rows_each = cotangent.shape[0] // 8
    cotangent_copies = [
        pltpu.make_async_copy(
            cotangent_ref.at[pl.ds(part * rows_each, rows_each)],
            cotangent.at[pl.ds(part * rows_each, rows_each)],
            sems.at[32 + part],
        )
        for part in range(8)
    ]
    for slab, copies in enumerate(pieces):
        for copy in copies:
            copy.start()
        if slab == 0:
            for copy in cotangent_copies:
                copy.start()
    square[...] = jnp.zeros_like(square)
    mixed[...] = jnp.zeros_like(mixed)

    def columns_of(chunk):
        return pl.ds(pl.multiple_of(chip_block(place_ref, chunk) * LANES, LANES), LANES)

    def multiply(slab):
        for copy in pieces[slab]:
            copy.wait()
        start = slab * 512
        latent[slab] = dot_rows(attended_ref[...], weight[start : start + 512, :])

    multiply(0)
    for copy in cotangent_copies:
        copy.wait()
    for slab in range(8):
        if slab < 7:
            multiply(slab + 1)
        columns = [columns_of(slab * 4 + part) for part in range(4)]
        scaled = [norm_ref[:, c] for c in columns]
        for start in range(0, square.shape[0], 64):
            rows = slice(start, start + 64)
            here = [latent[slab, rows, p * LANES : (p + 1) * LANES] for p in range(4)]
            arriving = [cotangent[rows, c].astype(f32) * g for c, g in zip(columns, scaled)]
            square[rows, :] += total_of([x * x for x in here])
            mixed[rows, :] += total_of([x * y for x, y in zip(here, arriving)])

    count = cotangent.shape[1]
    inverse = lax.rsqrt(jnp.sum(square[...], axis=1, keepdims=True) / count + epsilon)
    back = inverse * inverse * inverse * (jnp.sum(mixed[...], axis=1, keepdims=True) / count)
    square[...] = jnp.broadcast_to(inverse, square.shape)
    mixed[...] = jnp.broadcast_to(back, mixed.shape)

    def finish(slab, staged, out_ref):
        chunks = [slab * 4 + part for part in range(4)]
        columns = [columns_of(chunk) for chunk in chunks]
        norm = [norm_ref[:, c] for c in columns]
        gain = [jnp.zeros((8, LANES), f32)] * 4
        first = slab % 4 * 512
        for start in range(0, square.shape[0], 64):
            rows = slice(start, start + 64)
            scale, back = square[rows, :], mixed[rows, :]
            for part in range(4):
                here = latent[slab, rows, part * LANES : (part + 1) * LANES]
                scaled = cotangent[rows, columns[part]].astype(f32) * scale
                terms = scaled * here
                terms = [terms[k : k + 8, :] for k in range(0, 64, 8)]
                gain[part] += functools.reduce(jnp.add, terms)
                staged[rows, first + part * LANES : first + (part + 1) * LANES] = (
                    scaled * norm[part] - here * back
                ).astype(bf16)
        for part in range(4):
            spot = pl.ds(pl.multiple_of(chip_block(place_ref, chunks[part]) * 8, 8), 8)
            total = jnp.sum(gain[part], axis=0, keepdims=True)
            gain_ref[spot, :] = jnp.broadcast_to(total, (8, LANES))
        place = pl.ds(first, 512)
        copy = pltpu.make_async_copy(
            staged.at[:, place], out_ref.at[:, place], sems.at[40 + slab]
        )
        copy.start()
        return copy

    copies = []
    for part in range(4):
        staged, out_ref = (mine, mine_ref) if part < 2 else (other, other_ref)
        copies += [finish(slab, staged, out_ref) for slab in (2 * part, 2 * part + 1)]
        columns = slice(part % 2 * 1024, part % 2 * 1024 + 1024)
        terms = dot(staged[:, columns], weight[part * 1024 : part * 1024 + 1024, :])
        if part == 0:
            total[...] = terms
        elif part < 3:
            total[...] += terms
        else:
            d_attended_ref[...] = (total[...] + terms).astype(bf16)
    for copy in copies:
        copy.wait()


def latent_call(place, attended, norm_gain, cotangent, weights):
    patches, count = cotangent.shape
    return pl.pallas_call(
        latent_kernel,
        out_shape=[
            jax.ShapeDtypeStruct((patches, count // 2), bf16),
            jax.ShapeDtypeStruct((patches, count // 2), bf16),
            jax.ShapeDtypeStruct((count // LANES * 8, LANES), f32),
            jax.ShapeDtypeStruct(attended.shape, bf16),
        ],
        in_specs=[pl.BlockSpec(memory_space=pltpu.SMEM)]
        + [pl.BlockSpec(memory_space=pltpu.VMEM)] * 2
        + [pl.BlockSpec(memory_space=pl.ANY)] * 2,
        out_specs=[pl.BlockSpec(memory_space=pl.ANY)] * 2
        + [pl.BlockSpec(memory_space=pltpu.VMEM)] * 2,
        scratch_shapes=[
            pltpu.VMEM(weights.shape, bf16),
            pltpu.VMEM((patches, count), bf16),
            pltpu.VMEM((8, patches, count // 8), f32),
            pltpu.VMEM((patches, LANES), f32),
            pltpu.VMEM((patches, LANES), f32),
            pltpu.VMEM((patches, count // 2), bf16),
            pltpu.VMEM((patches, count // 2), bf16),
            pltpu.VMEM(attended.shape, f32),
            pltpu.SemaphoreType.DMA((48,)),
        ],
        compiler_params=pltpu.CompilerParams(vmem_limit_bytes=VMEM_GRANT),
        cost_estimate=pl.CostEstimate(
            flops=4 * patches * count * 1024, bytes_accessed=18 * MIB, transcendentals=patches
        ),
        name="latent",
    )(place, attended, norm_gain, cotangent, weights)


def d_proj_kernel(
    mine_ref, peer_ref, attended_ref, peer_attended_ref, gain_ref, *refs
):
    outs, (d_latent, rows, turned, staged, sems) = refs[:4], refs[4:]
    patches, width = attended_ref.shape
    arriving, leaving, sides = [], [], []
    for side, source in enumerate((attended_ref, peer_attended_ref)):
        sides.append(pltpu.make_async_copy(source, rows.at[side], sems.at[12 + side]))
        sides[-1].start()
    for k in (1, 2, 3, 0):
        columns = pl.ds((RING - k) % RING * 512, 512)
        for side, source in enumerate((mine_ref, peer_ref)):
            arriving.append(
                pltpu.make_async_copy(
                    source.at[:, columns],
                    d_latent.at[k, pl.ds(side * patches, patches)],
                    sems.at[2 * k + side],
                )
            )
            arriving[-1].start()
    for side in range(2):
        sides[side].wait()
        turned[:, side * patches : (side + 1) * patches] = rows[side].T
    for step, k in enumerate((1, 2, 3, 0)):
        arriving[2 * step].wait()
        arriving[2 * step + 1].wait()
        staged[k, :width, :] = dot(turned[...], d_latent[k]).astype(bf16)
        staged[k, width:, :] = gain_ref[...]
        leaving.append(pltpu.make_async_copy(staged.at[k], outs[k], sems.at[8 + k]))
        leaving[-1].start()
    for copy in leaving:
        copy.wait()


def d_proj_call(mine, peer, attended, peer_attended, gain):
    patches, width = attended.shape
    vmem, anywhere = pl.BlockSpec(memory_space=pltpu.VMEM), pl.BlockSpec(memory_space=pl.ANY)
    return pl.pallas_call(
        d_proj_kernel,
        out_shape=[jax.ShapeDtypeStruct((width + 16, 512), bf16)] * 4,
        in_specs=[anywhere] * 4 + [vmem],
        out_specs=[anywhere] * 4,
        scratch_shapes=[
            pltpu.VMEM((4, 2 * patches, 512), bf16),
            pltpu.VMEM((2, patches, width), bf16),
            pltpu.VMEM((width, 2 * patches), bf16),
            pltpu.VMEM((4, width + 16, 512), bf16),
            pltpu.SemaphoreType.DMA((14,)),
        ],
        compiler_params=pltpu.CompilerParams(vmem_limit_bytes=VMEM_GRANT),
        cost_estimate=pl.CostEstimate(
            flops=4 * patches * mine.shape[1] * width, bytes_accessed=12 * MIB, transcendentals=0
        ),
        name="d_proj",
    )(mine, peer, attended, peer_attended, gain)


def rim_kernel(
    key_in, value_in, below_ref, above_ref, key_out, value_out, rims, arriving, sems
):
    own = key_in.shape[0]
    places = ((pl.ds(0, HIGH), pl.ds(0, HIGH)), (pl.ds(own - LOW, LOW), pl.ds(HIGH, LOW)))
    steps = []
    for which, (source, out) in enumerate(((key_in, key_out), (value_in, value_out))):
        for side, (far, near) in enumerate(places):
            count = (HIGH, LOW)[side]
            from_ref = (below_ref, above_ref)[side].at[pl.ds(which * count, count)]
            rim, other = rims.at[which, near], arriving.at[which, near]
            sem = 3 * (2 * which + side)
            inward = [
                pltpu.make_async_copy(source.at[far], rim, sems.at[sem]),
                pltpu.make_async_copy(from_ref, other, sems.at[sem + 1]),
            ]
            outward = pltpu.make_async_copy(rim, out.at[far], sems.at[sem + 2])
            for copy in inward:
                copy.start()
            steps.append((rim, other, inward, outward))
    for rim, other, inward, outward in steps:
        for copy in inward:
            copy.wait()
        rim[...] = (rim[...].astype(f32) + other[...].astype(f32)).astype(bf16)
        outward.start()
    for *_, outward in steps:
        outward.wait()


def rim_call(d_key, d_value, from_below, from_above):
    width = from_below.shape[1]
    anywhere = pl.BlockSpec(memory_space=pl.ANY)
    return pl.pallas_call(
        rim_kernel,
        out_shape=[jax.ShapeDtypeStruct(d_key.shape, bf16)] * 2,
        in_specs=[anywhere] * 4,
        out_specs=[anywhere] * 2,
        scratch_shapes=[pltpu.VMEM((2, HIGH + LOW, width), bf16)] * 2
        + [pltpu.SemaphoreType.DMA((12,))],
        input_output_aliases={0: 0, 1: 1},
        compiler_params=pltpu.CompilerParams(vmem_limit_bytes=VMEM_GRANT),
        name="rims",
    )(d_key, d_value, from_below, from_above)


def along(which, distance):
    pairs = []
    for z in range(RING):
        for x in range(RING):
            for core in range(2):
                on_z = (which == "first") == (core == 0)
                to_z = (z + distance) % RING if on_z else z
                to_x = x if on_z else (x + distance) % RING
                pairs.append(((z * RING + x) * 2 + core, (to_z * RING + to_x) * 2 + core))
    return pairs


def to_peer(value):
    return lax.ppermute(value, "seq", [(i, i ^ 1) for i in range(lax.axis_size("seq"))])


def ring(values, which):
    return [values[0]] + [
        lax.ppermute(values[k], "seq", along(which, k)) for k in range(1, RING)
    ]


def total_of(parts):
    parts = [part.astype(f32) for part in parts]
    return (parts[0] + parts[2]) + (parts[1] + parts[3])


def halves(value):
    upper = value.astype(bf16)
    lower = (value - upper.astype(f32)).astype(bf16)
    return jnp.concatenate([upper, lower])


def joined(value):
    rows = value.shape[0] // 2
    return value[:rows] + value[rows:]


def first_sum_kernel(*refs):
    parts, outs = refs[:4], refs[4:]
    width = parts[0].shape[0] - 16
    gain = joined(total_of([ref[width:, :] for ref in parts]))
    gain = halves(
        jnp.concatenate([gain[:, k * LANES : (k + 1) * LANES] for k in range(RING)])
    )
    for k in range(RING):
        start = (RING - k) % RING * LANES
        columns = slice(start, start + LANES)
        outs[k][:width, :] = total_of([ref[:width, columns] for ref in parts]).astype(bf16)
        outs[k][width:, :] = gain


def first_sum(parts):
    width = parts[0].shape[0] - 16
    vmem = pl.BlockSpec(memory_space=pltpu.VMEM)
    return pl.pallas_call(
        first_sum_kernel,
        out_shape=[jax.ShapeDtypeStruct((width + 64, LANES), bf16)] * RING,
        in_specs=[vmem] * 4,
        out_specs=[vmem] * 4,
        compiler_params=pltpu.CompilerParams(vmem_limit_bytes=VMEM_GRANT),
        name="first_sum",
    )(*parts)


def second_sum_kernel(place_ref, *refs):
    parts, outs, total = refs[:4], refs[4:8], refs[8]
    width = total.shape[0]
    quarter = width // RING
    total[...] = total_of([ref[:width, :] for ref in parts])
    gain = halves(joined(total_of([ref[width:, :] for ref in parts])))
    for k in range(RING):
        start = pl.multiple_of((place_ref[3] + k) % RING * quarter, quarter)
        outs[k][:quarter, :] = total[pl.ds(start, quarter), :].astype(bf16)
        outs[k][quarter:, :] = gain


def second_sum(place, parts):
    width = parts[0].shape[0] - 64
    vmem = pl.BlockSpec(memory_space=pltpu.VMEM)
    return pl.pallas_call(
        second_sum_kernel,
        out_shape=[jax.ShapeDtypeStruct((width // RING + 64, LANES), bf16)] * RING,
        in_specs=[pl.BlockSpec(memory_space=pltpu.SMEM)]
        + [vmem] * 4,
        out_specs=[vmem] * RING,
        scratch_shapes=[pltpu.VMEM((width, LANES), f32)],
        name="second_sum",
    )(place, *parts)


def last_sum_kernel(*refs):
    parts, part_ref, gain_ref = refs[:4], refs[4], refs[5]
    quarter = part_ref.shape[0]
    total = total_of([ref[...] for ref in parts])
    part_ref[...] = total[:quarter, :].astype(bf16)
    gain_ref[...] = joined(total[quarter:, :])


def last_sum(parts):
    quarter = parts[0].shape[0] - 64
    vmem = pl.BlockSpec(memory_space=pltpu.VMEM)
    return pl.pallas_call(
        last_sum_kernel,
        out_shape=[
            jax.ShapeDtypeStruct((quarter, LANES), bf16),
            jax.ShapeDtypeStruct((32, LANES), f32),
        ],
        in_specs=[vmem] * 4,
        out_specs=[vmem] * 2,
        name="last_sum",
    )(*parts)


def finish_kernel(place_ref, *refs):
    parts, out_ref = refs[:4], refs[4]
    quarter = parts[0].shape[0]
    for k in range(RING):
        start = pl.multiple_of((place_ref[3] - k + RING) % RING * quarter, quarter)
        out_ref[:, pl.ds(start, quarter)] = parts[k][...].astype(f32).T


def finish_call(place, parts):
    quarter = parts[0].shape[0]
    vmem = pl.BlockSpec(memory_space=pltpu.VMEM)
    return pl.pallas_call(
        finish_kernel,
        out_shape=jax.ShapeDtypeStruct((LANES, RING * quarter), f32),
        in_specs=[pl.BlockSpec(memory_space=pltpu.SMEM)]
        + [vmem] * 4,
        out_specs=vmem,
        name="d_proj_rows",
    )(place, *parts)


def stream_ring(values):
    count = lax.axis_size("dp")
    return [values[0]] + [
        lax.ppermute(values[k], "dp", [(i, (i + k) % count) for i in range(count)])
        for k in range(1, RING)
    ]


def on_device(
    byte_keys, byte_values, doc_ids, queries, patch_end, cotangent, proj_weight, norm_gain
):
    own, width = byte_keys.shape[1:]
    patches = queries.shape[1]
    seq_count = lax.axis_size("seq")
    seq_rank = lax.axis_index("seq")
    upward = [(i, i + 1) for i in range(seq_count - 1)]
    downward = [(i + 1, i) for i in range(seq_count - 1)]
    keys, values, docs = byte_keys[0], byte_values[0], doc_ids[0]
    place = jnp.stack([seq_rank // (2 * RING), seq_rank // 2 % RING, seq_rank % 2, lax.axis_index("dp")])

    low_docs = lax.ppermute(docs[own - LOW :], "seq", upward)
    high_docs = lax.ppermute(docs[:HIGH], "seq", downward)
    low = jnp.concatenate([keys[own - LOW :], values[own - LOW :]])
    high = jnp.concatenate([keys[:HIGH], values[:HIGH]])
    low, high = lax.ppermute(low, "seq", upward), lax.ppermute(high, "seq", downward)
    weights = lax.all_gather(proj_weight, "seq", axis=0, tiled=True)

    ext_docs = jnp.concatenate([low_docs, docs, high_docs])
    ends = patch_end[0] - (seq_rank * own - LOW)
    position = jnp.arange(ext_docs.shape[0], dtype=jnp.int32)
    last_doc = jnp.sum(
        jnp.where(position[None, :] == ends[:, None] - 1, ext_docs[None, :], 0), axis=1
    )
    earlier = (ext_docs[None, :] < last_doc[:, None]) & (position[None, :] < ends[:, None])
    doc_start = jnp.sum(earlier.astype(jnp.int32), axis=1)
    first = jnp.maximum(jnp.maximum(ends - WIN, doc_start), jnp.where(seq_rank == 0, LOW, 0))
    groups = patches // PG
    marks = jnp.stack([first, ends]).reshape(2, groups, PG).transpose(1, 0, 2)
    marks = jnp.pad(jnp.tile(marks, (1, 1, PAIR)), ((0, 0), (0, 6), (0, 0)))
    marks = marks.reshape(groups * 8, PAIR * PG)
    offsets = (ends[::PG] - WIN) // 16 * 16
    short = (ends[PG - 1 :: PG] <= offsets + SHORT).astype(jnp.int32)

    common = (offsets, short, marks, low, high, keys, values, queries[0])
    attended, level = forward_call(common)
    peer_attended = to_peer(attended)

    mine, other, gain, d_attended = latent_call(place, attended, norm_gain[None], cotangent[0], weights)
    peer_mine = to_peer(other)
    gain = gain.reshape(RING, 8, 8, LANES)[:, :, 0].transpose(1, 0, 2).reshape(8, 512)
    gain = gain + to_peer(gain)
    to_send = d_proj_call(mine, peer_mine, attended, peer_attended, halves(gain))
    from_ring = ring(to_send, "first")

    inputs = common + (attended, level, d_attended)
    d_query, d_keys, d_values, d_low, d_high = backward_call(inputs, to_send[0])
    from_ring, d_query = lax.optimization_barrier((from_ring, d_query))
    from_ring = ring(first_sum(from_ring), "second")
    from_ring, d_low, d_high = lax.optimization_barrier((from_ring, d_low, d_high))
    from_above = lax.ppermute(d_low, "seq", downward)
    from_below = lax.ppermute(d_high, "seq", upward)
    part, gain = last_sum(stream_ring(second_sum(place, from_ring)))
    d_proj = finish_call(place, stream_ring([part] * RING))
    d_keys, d_values = rim_call(d_keys, d_values, from_below, from_above)
    d_gain = gain.reshape(-1)
    return (d_query[None], d_keys[None], d_values[None], d_proj, d_gain)


def solution(mesh):
    in_specs = (
        P("dp", "seq", None),
        P("dp", "seq", None),
        P("dp", "seq"),
        P("dp", "seq", None),
        P("dp", "seq"),
        P("dp", "seq", None),
        P("seq", None),
        P(),
    )
    out_specs = (
        P("dp", "seq", None),
        P("dp", "seq", None),
        P("dp", "seq", None),
        P("seq", None),
        P(),
    )
    return jax.shard_map(
        on_device, mesh=mesh, in_specs=in_specs, out_specs=out_specs, check_vma=False
    )
```
